32 devices in a mesh: leaf: 16 (over z, y, core), oct: 2 (over x).
Axes of the slice: x: 2, y: 2, z: 4, core: 2. Of those that a mesh axis runs over, the one named last changes fastest.
Arguments:
- children: bfloat16 [1024, 4096], P(('leaf', 'oct')), may hold values from -6 to 6
- child_slot: int32 [128, 8], P('leaf', 'oct'), may hold values from 0 to 31, as said below
- two_scale: bfloat16 [32, 32], replicated, may hold values from -1 to 1
- factors: bfloat16 [27, 30720], replicated, may hold values from -0.5390625 to 0.5390625
- disp_kind: int32 [128, 4], P(('leaf', 'oct')), may hold values from 0 to 26
- target_leaf: int32 [128, 4, 1], P(('leaf', 'oct')), may hold values from 0 to 15; in each aligned block of 16 rows (0 to 15, 16 to 31, ..., all dimensions but the last counted through in order) at most 2 rows name the same one
- target_node: int32 [128, 4], P(('leaf', 'oct')), may hold values from 0 to 3
Outputs:
- octant_out: bfloat16 [64, 8, 4096], P('leaf', 'oct')
The draws below stay inside these ranges and needn't reach their ends.
Inputs may be any that keep to these rules, and one draw needn't show every extreme that they name: Over the parents of one subtree and the octants held by one device along oct, child_slot takes every value exactly once. `target_leaf`: of the 16 entries of one device, at most 2 name the same subtree; some device reaches 2.
All inputs are finite; a program needn't handle non-finite values.
Results may differ from the reference program's by a relative error of at most 0.018.
Values may be sent and summed in bfloat16 or wider, within the bound.
No kernel may reach another device: no remote copies, remote signals or barrier semaphores. Data moves between devices by JAX's collectives and lax.ppermute only.
A program may use at most 64 MiB of HBM per device.

```python
import math
import jax
import jax.numpy as jnp
import numpy as np
from jax import lax

K = 16
TERMS = 10
DISPS = 4
KINDS = 27
PAR_DEV = 4
TGT_DEV = 2
PARENTS = 128
BLOCKS = 1024
TARGETS = 64
CAP = 2
N_LEAF = 16
N_OCT = 2


def draw_child_slot(key, part):
    group_size = PAR_DEV * N_OCT
    held_octants = 8 // N_OCT
    block_total = PAR_DEV * 8
    device_keys = jax.random.split(jax.random.fold_in(key, 17), N_LEAF * N_OCT)
    shuffled = jax.vmap(lambda one_key: jax.random.permutation(one_key, block_total))(device_keys)
    shuffled = shuffled.reshape(N_LEAF, N_OCT, group_size, held_octants)
    shuffled = jnp.transpose(shuffled, (0, 2, 1, 3)).reshape(N_LEAF * group_size, 8)
    return shuffled.astype(jnp.int32)


def plant(array, stream_key, smallest, high):
    spot = [jax.random.randint(jax.random.fold_in(stream_key, axis), (), 0, length) for axis, length in enumerate(array.shape)]
    longest = array.shape.index(max(array.shape))
    next_to = spot[:longest] + [(spot[longest] + 1) % array.shape[longest]] + spot[longest + 1:]
    return array.at[tuple(spot)].set(smallest).at[tuple(next_to)].set(high)


def level_of(stream_key, shape, cuts, low, high):
    loudness = 1.0
    for position, blocks in cuts:
        draws = jax.random.uniform(jax.random.fold_in(jax.random.fold_in(stream_key, 6), position), (blocks,), jnp.float32, low / len(cuts), high / len(cuts))
        loudness = loudness * jnp.repeat(jnp.exp(draws), shape[position] // blocks).reshape((-1,) + (1,) * (len(shape) - 1 - position))
    return loudness


def deal_out(own_key, own, number, rows, count, top, bound, slope):
    order = jax.random.permutation(own_key, count)
    packed, usual = portions_of(count, rows * top, bound, slope, True), portions_of(count, rows * top, bound, slope, False)
    places = jnp.arange(count)

    def named(sizes, offset_by):
        used = int((sizes > 0).sum())
        fixed = max(1, used // 4)
        shifted = fixed + (places - fixed + offset_by * (used - fixed)) % max(1, count - fixed)
        return jnp.zeros((count,), jnp.int32).at[order[jnp.where(places < fixed, places, shifted)]].set(jnp.asarray(sizes, jnp.int32))

    sizes = jnp.where(number % 4 == 0, named(packed, number // 4), named(usual, number - number // 4 - 1))
    mixed = jax.random.permutation(jax.random.fold_in(own, 3), count)
    donor, taker = mixed[0:count // 2 * 2:2], mixed[1:count // 2 * 2:2]
    margin = jnp.minimum(sizes[donor] - 1, bound - sizes[taker]) // 2
    margin = jnp.where((donor == order[0]) | (taker == order[0]) | (sizes[taker] == 0), 0, jnp.maximum(margin, 0))
    shifted = jax.random.randint(jax.random.fold_in(own, 4), (count // 2,), 0, 1 << 20) % (margin + 1)
    sizes = sizes.at[donor].add(-shifted).at[taker].add(shifted)
    items = jnp.searchsorted(jnp.cumsum(sizes), jnp.arange(rows * top), side="right").astype(jnp.int32)
    table = items.reshape(top, rows).T
    table = table[jax.random.permutation(jax.random.fold_in(own, 1), rows)]
    offset_by = jax.random.randint(jax.random.fold_in(own, 2), (rows, 1), 0, top)
    return jnp.take_along_axis(table, (jnp.arange(top)[None, :] + offset_by) % top, axis=1)


def portions_of(count, total, bound, slope, full):
    loads = [(1 << 20) // math.isqrt(standing ** slope) + 1 for standing in range(1, count + 1)]
    largest = bound if full else min(bound, max(-(-total // count), total * loads[0] // sum(loads)))
    least = 1 if total - largest >= count - 1 else 0
    given, surplus = [largest] + [least] * (count - 1), total - largest - least * (count - 1)
    while surplus > 0:
        movable = [i for i in range(1, count) if given[i] < largest] or [i for i in range(1, count) if given[i] < bound]
        pool, budget = sum([loads[i] for i in movable]), surplus
        for i in movable:
            addition = min(bound - given[i], max(1, budget * loads[i] // pool), surplus)
            given[i] = given[i] + addition
            surplus = surplus - addition
    return np.array(given)


def bell_draw(rng, extent, spread, limit, cuts=(), kind=jnp.bfloat16):
    values = spread * jax.random.normal(rng, extent, jnp.float32)
    if cuts:
        values = values * level_of(rng, extent, cuts, -0.22, 0.18)
    return jnp.clip(values, -limit, limit).astype(kind)


def setup_inputs(seed: int = 0) -> dict:
    keys = jax.random.split(jax.random.key(seed), 8)
    children = bell_draw(keys[0], (BLOCKS, K * K * K), 1.0, 6.0, ((0, 32),))
    child_slot = draw_child_slot(jax.random.fold_in(keys[7], 71), 0)
    two_scale = bell_draw(keys[2], (2 * K, 2 * K), (2 * K) ** -0.5, 1.0)
    factors = bell_draw(keys[3], (KINDS, 3 * TERMS * 4 * K * K), 0.09, 0.5390625)
    disp_kind = plant(jax.random.randint(keys[4], (PARENTS, DISPS), 0, KINDS), jax.random.fold_in(keys[4], 1), 0, KINDS - 1).astype(jnp.int32)
    target_leaf_keys = jax.random.split(jax.random.fold_in(keys[5], 1), PARENTS * DISPS // (PAR_DEV * DISPS))
    target_leaf_turns = jax.random.permutation(jax.random.fold_in(keys[5], 3), PARENTS * DISPS // (PAR_DEV * DISPS))
    target_leaf = jax.vmap(lambda own, number: deal_out(jax.random.fold_in(keys[5], 2), own, number, PAR_DEV * DISPS, N_LEAF, 1, CAP, 2))(target_leaf_keys, target_leaf_turns).reshape((PARENTS, DISPS, 1))
    target_node = plant(jax.random.randint(keys[6], (PARENTS, DISPS), 0, TGT_DEV * N_OCT), jax.random.fold_in(keys[6], 1), 0, (TGT_DEV * N_OCT) - 1).astype(jnp.int32)
    return {"children": children, "child_slot": child_slot, "two_scale": two_scale, "factors": factors, "disp_kind": disp_kind, "target_leaf": target_leaf, "target_node": target_node}


def filter_blocks(block_batch, filter_halfset):
    half_edge = filter_halfset.shape[2]
    count_batch = block_batch.shape[0]
    split_blocks = block_batch.reshape(count_batch, 2, 2, 2, half_edge, half_edge, half_edge).astype(jnp.float32)
    halfset_width = filter_halfset.astype(jnp.float32)
    first_pass = jnp.einsum('nijlpsr,aip->najlsr', split_blocks, halfset_width).astype(jnp.bfloat16)
    second_sweep = jnp.einsum('najlsr,bjs->nablr', first_pass.astype(jnp.float32), halfset_width).astype(jnp.bfloat16)
    third_sweep = jnp.einsum('qyixz,wxz->qyiw', second_sweep.astype(jnp.float32), halfset_width).astype(jnp.bfloat16)
    return third_sweep


def unfilter_blocks(cube_batch, filter_halfset):
    half_edge = filter_halfset.shape[2]
    count_batch = cube_batch.shape[0]
    halfset_width = filter_halfset.astype(jnp.float32)
    first_pass = jnp.einsum('nabc,aip->nipbc', cube_batch.astype(jnp.float32), halfset_width).astype(jnp.bfloat16)
    second_sweep = jnp.einsum('nipbc,bjs->nipjsc', first_pass.astype(jnp.float32), halfset_width).astype(jnp.bfloat16)
    third_sweep = jnp.einsum('xmezhw,wbf->xmezhbf', second_sweep.astype(jnp.float32), halfset_width).astype(jnp.bfloat16)
    ordered = jnp.transpose(third_sweep, (0, 1, 3, 5, 2, 4, 6))
    return ordered.reshape(count_batch, 8, half_edge * half_edge * half_edge)


def apply_parent(parent_cube, factor_set):
    cube_wide = parent_cube.astype(jnp.float32)
    factor_wide = factor_set.astype(jnp.float32)
    section_z = jnp.einsum('abc,ktdc->ktabd', cube_wide, factor_wide[:, 2]).astype(jnp.bfloat16)
    section_y = jnp.einsum('ktabd,kteb->ktaed', section_z.astype(jnp.float32), factor_wide[:, 1]).astype(jnp.bfloat16)
    summed = jnp.einsum('ktaed,ktfa->kfed', section_y.astype(jnp.float32), factor_wide[:, 0]).astype(jnp.bfloat16)
    return summed.reshape(summed.shape[0], -1)


def reference(children, child_slot, two_scale, factors, disp_kind, target_leaf, target_node):
    edge_len = 2 * K
    group_size = PAR_DEV * N_OCT
    held_octants = 8 // N_OCT
    node_count = TGT_DEV * N_OCT
    filter_halfset = two_scale.reshape(edge_len, 2, K)
    factor_table = factors.reshape(KINDS, 3, TERMS, edge_len, edge_len)
    parent_ids = jnp.arange(PARENTS, dtype=jnp.int32)
    octant_ids = jnp.arange(8, dtype=jnp.int32)
    owner_device = (parent_ids[:, None] // group_size) * N_OCT + octant_ids[None, :] // held_octants
    block_rows = (owner_device * (8 * PAR_DEV) + child_slot).astype(jnp.int32)
    goal_nodes = (target_leaf[:, :, 0] * node_count + target_node).astype(jnp.int32)

    def scan_step(node_totals, scan_item):
        block_row, kind_index, goal_node = scan_item
        picked_blocks = children[block_row]
        parent_cube = filter_blocks(picked_blocks[None], filter_halfset)[0]
        contribution = apply_parent(parent_cube, factor_table[kind_index])
        return node_totals.at[goal_node].add(contribution.astype(jnp.float32)), None

    start_totals = jnp.zeros((TARGETS, edge_len * edge_len * edge_len), jnp.float32)
    node_totals, unused_out = lax.scan(scan_step, start_totals, (block_rows, disp_kind, goal_nodes))
    target_blocks = node_totals.astype(jnp.bfloat16).reshape(TARGETS, edge_len, edge_len, edge_len)
    return lax.map(lambda single_cube: unfilter_blocks(single_cube[None], filter_halfset)[0], target_blocks)
```

```python
import functools

import jax
import jax.numpy as jnp
from jax import lax
from jax.experimental import pallas as pl
from jax.experimental.pallas import tpu as pltpu
from jax.sharding import PartitionSpec as P

BF = jnp.bfloat16
F32 = jnp.float32


def dot(x, y):
    return jnp.dot(x, y, preferred_element_type=F32)


def apply_kernel(
    kind_ref, near_ref, far_ref, ft1_ref, ft2_ref, f0_ref, s1e_ref, s2e_ref, m1_ref, m2_ref,
    fw1_ref, fw2_ref, sa_ref, st_ref, keep_ref, send_ref, cube_ref, sec_ref, *, half,
):
    edge = 2 * half
    low = half // 2
    wide = edge * low
    quarter = wide // 4
    terms = f0_ref.shape[2] // edge

    @pl.when(pl.program_id(0) == 0)
    def _():
        total = None
        for bit in range(2):
            rows = []
            for mid in range(2):
                rows += [near_ref[0, 2 * mid + bit], far_ref[0, 2 * mid + bit]]
            part = dot(jnp.concatenate(rows, axis=0), fw1_ref[bit])
            total = part if total is None else total + part
        total = total.astype(BF)
        lanes = wide // 2
        moved = jnp.concatenate(
            [
                jnp.concatenate(
                    [
                        total[:edge, lanes * i : lanes * (i + 1)],
                        total[edge:, lanes * i : lanes * (i + 1)],
                    ],
                    axis=1,
                )
                for i in range(4)
            ],
            axis=0,
        )
        second = dot(moved, fw2_ref[...]).astype(BF)
        for i in range(4):
            cube_ref[edge * i : edge * (i + 1), :] = dot(
                sa_ref[...], second[edge * i : edge * (i + 1)]
            ).astype(BF)

    cube = cube_ref[...]
    w1e = dot(ft1_ref[0], s1e_ref[...]).astype(BF)
    w2e = dot(ft2_ref[0], s2e_ref[...]).astype(BF)
    g0 = dot(st_ref[...], f0_ref[0]).astype(BF)
    for t in range(terms):
        one = w1e[edge * t : edge * (t + 1)]
        w1 = jnp.concatenate(
            [one * m1_ref[edge * i : edge * (i + 1), :] for i in range(low)], axis=0
        )
        first = dot(cube, w1).astype(BF)
        moved = jnp.concatenate(
            [
                jnp.concatenate(
                    [
                        first[edge * i : edge * (i + 1), quarter * j : quarter * (j + 1)]
                        for i in range(4)
                    ],
                    axis=1,
                )
                for j in range(4)
            ],
            axis=0,
        )
        base = 2 * edge * t
        w2 = jnp.concatenate(
            [
                w2e[base + half * i : base + half * (i + 1)] * m2_ref[half * q : half * (q + 1), :]
                for i in range(4)
                for q in range(low // 2)
            ],
            axis=0,
        )
        second = dot(moved, w2).astype(BF)
        for i in range(4):
            sec_ref[i, edge * t : edge * (t + 1), :] = second[edge * i : edge * (i + 1)]
    for i in range(4):
        out = dot(g0, sec_ref[i]).astype(BF)
        keep_ref[0, :, wide * i : wide * (i + 1)] = out[:half]
        send_ref[0, :, wide * i : wide * (i + 1)] = out[half:]


def apply_parent(parent, kinds, near, far, ft1, ft2, f0, consts, half):
    s1e, s2e, m1, m2, fw1, fw2, sa, st = consts
    disps = kinds.shape[0]
    edge = 2 * half
    wide = edge * half // 2
    terms = f0.shape[2] // edge

    def whole(array):
        return pl.BlockSpec(array.shape, lambda k, kinds: (0,) * array.ndim)

    def of_kind(array):
        return pl.BlockSpec((1,) + array.shape[1:], lambda k, kinds: (kinds[k], 0, 0))

    def of_parent(array):
        return pl.BlockSpec((1,) + array.shape[1:], lambda k, kinds: (parent, 0, 0, 0))

    shape = jax.ShapeDtypeStruct((disps, half, 4 * wide), BF)
    out_spec = pl.BlockSpec((1, half, 4 * wide), lambda k, kinds: (k, 0, 0))
    return pl.pallas_call(
        functools.partial(apply_kernel, half=half),
        grid_spec=pltpu.PrefetchScalarGridSpec(
            num_scalar_prefetch=1,
            grid=(disps,),
            in_specs=[
                of_parent(near),
                of_parent(far),
                of_kind(ft1),
                of_kind(ft2),
                of_kind(f0),
                whole(s1e),
                whole(s2e),
                whole(m1),
                whole(m2),
                whole(fw1),
                whole(fw2),
                whole(sa),
                whole(st),
            ],
            out_specs=[out_spec, out_spec],
            scratch_shapes=[
                pltpu.VMEM((4 * edge, wide), BF),
                pltpu.VMEM((4, terms * edge, wide), BF),
            ],
        ),
        out_shape=[shape, shape],
        compiler_params=pltpu.CompilerParams(vmem_limit_bytes=48 * 1024 * 1024),
    )(kinds, near, far, ft1, ft2, f0, s1e, s2e, m1, m2, fw1, fw2, sa, st)


def sum_kernel(slot_ref, *refs, rows):
    row_refs, (even_ref, odd_ref, total_ref) = refs[:-3], refs[-3:]
    total_ref[...] = jnp.zeros_like(total_ref)
    for i in range(len(row_refs)):
        for j in range(rows):
            slot = slot_ref[i * rows + j]
            total_ref[slot] = total_ref[slot] + row_refs[i][j].astype(F32)
    count = even_ref.shape[0]
    even_ref[...] = total_ref[:count].astype(BF)
    odd_ref[...] = total_ref[count:].astype(BF)


def sum_rows(slots, arrays, slot_count):
    rows = arrays[0].shape[0]
    tail = arrays[0].shape[1:]
    shape = jax.ShapeDtypeStruct((slot_count // 2,) + tail, BF)
    return pl.pallas_call(
        functools.partial(sum_kernel, rows=rows),
        in_specs=[pl.BlockSpec(memory_space=pltpu.SMEM)]
        + [pl.BlockSpec(memory_space=pltpu.VMEM)] * len(arrays),
        out_specs=[pl.BlockSpec(memory_space=pltpu.VMEM)] * 2,
        out_shape=[shape, shape],
        scratch_shapes=[pltpu.VMEM((slot_count,) + tail, F32)],
        compiler_params=pltpu.CompilerParams(vmem_limit_bytes=60 * 1024 * 1024),
    )(slots, *arrays)


def swap(x, axis, mask):
    count = lax.axis_size(axis)
    return lax.ppermute(x, axis, [(i, i ^ mask) for i in range(count)])


def local(children, child_slot, two_scale, factors, disp_kind, target_leaf, target_node):
    oct_count = lax.axis_size("oct")
    leaf_count = lax.axis_size("leaf")
    my_leaf = lax.axis_index("leaf")
    my_oct = lax.axis_index("oct")
    edge = two_scale.shape[0]
    half = edge // 2
    low = half // 2
    wide = edge * low
    held = child_slot.shape[1]
    parents, disps = disp_kind.shape
    paired = oct_count == 2

    blocks = children.reshape(-1, half, half * half)
    if paired:
        theirs = lax.dynamic_slice_in_dim(child_slot, (1 - my_oct) * parents, parents, 0)
        mine = lax.dynamic_slice_in_dim(child_slot, my_oct * parents, parents, 0)
        far = swap(blocks[theirs], "oct", 1)
        near = blocks[mine]
    else:
        arrived = lax.all_to_all(
            blocks[child_slot], "oct", split_axis=0, concat_axis=1, tiled=True
        ).reshape(parents, 2, 4, half, half * half)
        near, far = arrived[:, 0], arrived[:, 1]

    nodes = 2 * oct_count
    goal = target_leaf.reshape(parents, disps) * nodes + target_node
    if paired:
        goals = jnp.stack([goal, swap(goal, "oct", 1)], axis=1)
    else:
        goals = lax.all_gather(goal, "oct").transpose(1, 0, 2)
    leaf_off = jnp.bitwise_xor(goals // nodes, my_leaf)
    slots = ((leaf_off % 2) * (leaf_count // 2) + leaf_off // 2) * nodes + goals % nodes

    kinds = factors.shape[0]
    table = factors.reshape(kinds, 3, -1, edge, edge)
    terms = table.shape[2]
    f0 = table[:, 0].transpose(0, 2, 1, 3).reshape(kinds, edge, terms * edge)
    ft1 = table[:, 1].transpose(0, 1, 3, 2).reshape(kinds, terms * edge, edge)
    ft2 = table[:, 2].transpose(0, 1, 3, 2).reshape(kinds, terms * 4, 1, low, edge)
    ft2 = jnp.broadcast_to(ft2, (kinds, terms * 4, 2, low, edge)).reshape(
        kinds, terms * 2 * edge, edge
    )
    lane = jnp.arange(wide)
    row = jnp.arange(wide)
    s1e = jnp.repeat(two_scale, low, axis=1)
    s2e = jnp.broadcast_to(
        two_scale.reshape(edge, 2, 1, half), (edge, 2, low, half)
    ).reshape(edge, wide)
    m1 = (row[:, None] // edge == lane[None, :] % low).astype(BF)
    dup_rows = jnp.arange(2 * edge)
    m2 = (dup_rows[:, None] // low == (lane[None, :] // half) % low).astype(BF)
    transposed = two_scale.T
    by_bit = jnp.repeat(transposed.reshape(2, half, edge), half, axis=2)
    fw1 = jnp.where(
        (row[:, None] // half == jnp.arange(2 * wide)[None, :] % half)[None],
        jnp.tile(by_bit, (1, half, 1)),
        jnp.zeros((), BF),
    )
    spread = jnp.broadcast_to(
        jnp.tile(transposed, (1, low)).reshape(2, 1, half, wide), (2, low, half, wide)
    ).reshape(wide, wide)
    fw2 = jnp.where(
        (row[:, None] // half) % low == lane[None, :] // edge, spread, jnp.zeros((), BF)
    )
    if paired:
        turned = two_scale.reshape(edge, 2, half)
        turned = jnp.where(my_oct == 0, turned, turned[:, ::-1]).reshape(edge, edge)
    else:
        turned = two_scale
    consts = (s1e, s2e, m1, m2, fw1, fw2, turned, turned.T)

    arrays = []
    for parent in range(parents):
        kept, sent = apply_parent(
            parent, disp_kind[parent], near, far, ft1, ft2, f0, consts, half
        )
        if paired:
            arrays += [kept, swap(sent, "oct", 1)]
        else:
            rows = jnp.stack([kept, sent], axis=1).reshape(disps, 2, half, 2, 2, 2, low * half)
            rows = rows.transpose(1, 3, 5, 0, 2, 4, 6)
            rows = rows.reshape(oct_count, held, disps, half, half * half)
            rows = rows.transpose(0, 2, 1, 3, 4)
            rows = lax.all_to_all(rows, "oct", split_axis=0, concat_axis=0, tiled=True)
            arrays += [rows.reshape(oct_count * disps, held * half, half * half)]

    even, odd = sum_rows(slots.reshape(-1), arrays, leaf_count * nodes)
    total = even.astype(F32) + swap(odd, "leaf", 1).astype(F32)
    total = total.astype(BF).reshape((leaf_count // 2, nodes) + total.shape[1:])
    mask = 2
    while mask < leaf_count:
        pairs = total.reshape((-1, 2) + total.shape[1:])
        total = pairs[:, 0].astype(F32) + swap(pairs[:, 1], "leaf", mask).astype(F32)
        total = total.astype(BF)
        mask *= 2
    total = total.reshape(nodes, -1)
    if paired:
        out = total.reshape(nodes, half, 2, 2, 2, low * half)
        return out.transpose(0, 2, 4, 1, 3, 5).reshape(nodes, held, -1)
    return total.reshape(nodes, held, -1)


def solution(mesh):
    placed = (
        P(("leaf", "oct"), None),
        P("leaf", "oct"),
        P(),
        P(),
        P(("leaf", "oct"), None),
        P(("leaf", "oct"), None, None),
        P(("leaf", "oct"), None),
    )
    return jax.shard_map(
        local, mesh=mesh, in_specs=placed, out_specs=P("leaf", "oct", None), check_vma=False
    )
```

```python
import functools

import jax
import jax.numpy as jnp
from jax import lax
from jax.experimental import pallas as pl
from jax.experimental.pallas import tpu as pltpu
from jax.sharding import PartitionSpec as P

BF = jnp.bfloat16
F32 = jnp.float32


def dot(x, y):
    return jnp.dot(x, y, preferred_element_type=F32)


def one_hot(shape, row_of, lane_of):
    rows = lax.broadcasted_iota(jnp.int32, shape, 0)
    lanes = lax.broadcasted_iota(jnp.int32, shape, 1)
    return (row_of(rows) == lane_of(lanes)).astype(BF)


def exact(x, y):
    return dot(x, y).astype(BF)


def weights_kernel(
    scale_ref, s1e_ref, s2e_ref, m1_ref, m2_ref, fw1_ref, fw2_ref, sa_ref, st_ref, *, half, paired
):
    edge = 2 * half
    low = half // 2
    wide = edge * low
    scale = scale_ref[...]
    turn = lax.axis_index("oct") * half if paired else 0

    def same(x):
        return x

    def turned(x):
        return lax.rem(x + turn, edge)

    def chunked(x):
        return (x % low) * 4 + x // low

    by_chunk = exact(one_hot((edge, edge), chunked, same), scale)
    s1e_ref[...] = exact(by_chunk, one_hot((edge, wide), same, lambda x: x // low))
    s2e_ref[...] = exact(
        by_chunk, one_hot((edge, wide), same, lambda x: x // (wide // 2) * half + x % half)
    )
    m1_ref[...] = one_hot((wide, wide), lambda x: x // edge, lambda x: x % low)
    m2_ref[...] = one_hot((2 * edge, wide), lambda x: x // low, lambda x: x // half % low)
    sa_ref[...] = exact(scale, one_hot((edge, edge), same, turned))
    pick = one_hot((edge, edge), turned, same)
    st_ref[...] = lax.dot_general(
        pick, by_chunk, (((1,), (1,)), ((), ())), preferred_element_type=F32
    ).astype(BF)

    def spread(row_of, lane_of, lane_count):
        rows = lax.dot_general(
            one_hot((wide, edge), row_of, same),
            scale,
            (((1,), (1,)), ((), ())),
            preferred_element_type=F32,
        ).astype(BF)
        return exact(rows, one_hot((edge, lane_count), same, lane_of))

    for bit in range(2):
        fw1_ref[bit] = spread(
            lambda x: x % half + bit * half, lambda x: x // half, 2 * wide
        ) * one_hot((wide, 2 * wide), lambda x: x // half, lambda x: x % half)
    fw2_ref[...] = spread(
        lambda x: x // (wide // 2) * half + x % half, lambda x: x % edge, wide
    ) * one_hot((wide, wide), lambda x: x // half % low, lambda x: x // edge)


def make_weights(two_scale, paired):
    edge = two_scale.shape[0]
    half = edge // 2
    wide = edge * half // 2
    shapes = [
        (edge, wide), (edge, wide), (wide, wide), (2 * edge, wide),
        (2, wide, 2 * wide), (wide, wide), (edge, edge), (edge, edge),
    ]
    return pl.pallas_call(
        functools.partial(weights_kernel, half=half, paired=paired),
        in_specs=[pl.BlockSpec(memory_space=pltpu.VMEM)],
        out_specs=[pl.BlockSpec(memory_space=pltpu.VMEM)] * len(shapes),
        out_shape=[jax.ShapeDtypeStruct(shape, BF) for shape in shapes],
        compiler_params=pltpu.CompilerParams(vmem_limit_bytes=32 * 1024 * 1024),
    )(two_scale)


def pick_kernel(slot_ref, blocks_ref, out_ref, *, parents):
    first = (1 - lax.axis_index("oct")) * parents
    for i in range(parents):
        for j in range(out_ref.shape[1]):
            out_ref[i, j] = blocks_ref[slot_ref[first + i, j]]


def pick_blocks(child_slot, blocks, parents):
    shape = (parents, child_slot.shape[1]) + blocks.shape[1:]
    return pl.pallas_call(
        functools.partial(pick_kernel, parents=parents),
        in_specs=[
            pl.BlockSpec(memory_space=pltpu.SMEM),
            pl.BlockSpec(memory_space=pltpu.VMEM),
        ],
        out_specs=pl.BlockSpec(memory_space=pltpu.VMEM),
        out_shape=jax.ShapeDtypeStruct(shape, BF),
    )(child_slot, blocks)


def by_output(table, edge, terms):
    low = edge // 4
    lanes = 4 * edge
    chunk = lax.broadcasted_iota(jnp.int32, (low, lanes), 1) // edge
    groups = []
    for start in range(0, terms, 4):
        tiles = [
            table[low * min(t, terms - 1) : low * (min(t, terms - 1) + 1)]
            for t in range(start, start + 4)
        ]
        for step in (1, 2):
            upper = (chunk // step) % 2 == 1
            mixed = list(tiles)
            for i in range(4):
                if i & step == 0:
                    mixed[i] = jnp.where(
                        upper, pltpu.roll(tiles[i + step], edge * step, 1), tiles[i]
                    )
                    mixed[i + step] = jnp.where(
                        upper, tiles[i + step], pltpu.roll(tiles[i], lanes - edge * step, 1)
                    )
            tiles = mixed
        groups.append(jnp.concatenate(tiles, axis=0))
    return jnp.concatenate(groups, axis=1)[:, : terms * edge]


def apply_kernel(
    kind_ref, slot_ref, blocks_ref, far_ref, table_ref, s1e_ref, s2e_ref, m1_ref, m2_ref,
    fw1_ref, fw2_ref, sa_ref, st_ref, keep_ref, send_ref, cube_ref, sec_ref,
    *, half, terms, parent,
):
    edge = 2 * half
    low = half // 2
    wide = edge * low
    quarter = wide // 4

    @pl.when(pl.program_id(0) == 0)
    def _():
        if slot_ref is None:
            near = [blocks_ref[0, i] for i in range(4)]
        else:
            first = lax.axis_index("oct") * far_ref.shape[0] + parent
            near = [blocks_ref[slot_ref[first, i]] for i in range(4)]
        total = None
        for bit in range(2):
            rows = []
            for mid in range(2):
                rows += [near[2 * mid + bit], far_ref[parent, 2 * mid + bit]]
            part = dot(jnp.concatenate(rows, axis=0), fw1_ref[bit])
            total = part if total is None else total + part
        total = total.astype(BF)
        lanes = wide // 2
        moved = jnp.concatenate(
            [
                jnp.concatenate(
                    [
                        total[:edge, lanes * i : lanes * (i + 1)],
                        total[edge:, lanes * i : lanes * (i + 1)],
                    ],
                    axis=1,
                )
                for i in range(4)
            ],
            axis=0,
        )
        second = dot(moved, fw2_ref[...]).astype(BF)
        for i in range(4):
            cube_ref[edge * i : edge * (i + 1), :] = dot(
                sa_ref[...], second[edge * i : edge * (i + 1)]
            ).astype(BF)

    cube = cube_ref[...]
    table = table_ref[0].astype(F32)
    rows = terms * low
    f0, f1, f2 = [
        by_output(table[rows * i : rows * (i + 1)], edge, terms) for i in range(3)
    ]
    ft1 = f1.T.astype(BF)
    ft2 = f2.T.reshape(terms * 4, 1, low, edge)
    ft2 = jnp.broadcast_to(ft2, (terms * 4, 2, low, edge)).reshape(terms * 2 * edge, edge)
    w1e = dot(ft1, s1e_ref[...]).astype(BF)
    w2e = dot(ft2.astype(BF), s2e_ref[...]).astype(BF)
    g0 = dot(st_ref[...], f0.astype(BF)).astype(BF)
    for t in range(terms):
        one = w1e[edge * t : edge * (t + 1)]
        w1 = jnp.concatenate(
            [one * m1_ref[edge * i : edge * (i + 1), :] for i in range(low)], axis=0
        )
        first = dot(cube, w1).astype(BF)
        moved = jnp.concatenate(
            [
                jnp.concatenate(
                    [
                        first[edge * i : edge * (i + 1), quarter * j : quarter * (j + 1)]
                        for i in range(4)
                    ],
                    axis=1,
                )
                for j in range(4)
            ],
            axis=0,
        )
        base = 2 * edge * t
        w2 = jnp.concatenate(
            [
                w2e[base + half * i : base + half * (i + 1)] * m2_ref[half * q : half * (q + 1), :]
                for i in range(4)
                for q in range(low // 2)
            ],
            axis=0,
        )
        second = dot(moved, w2).astype(BF)
        for i in range(4):
            sec_ref[i, edge * t : edge * (t + 1), :] = second[edge * i : edge * (i + 1)]
    for i in range(4):
        out = dot(g0, sec_ref[i]).astype(BF)
        keep_ref[0, :, wide * i : wide * (i + 1)] = out[:half]
        send_ref[0, :, wide * i : wide * (i + 1)] = out[half:]


def apply_parent(parent, kinds, child_slot, near, far, table, weights, half):
    edge = 2 * half
    wide = edge * half // 2
    terms = table.shape[1] // (3 * edge // 4)
    disps = kinds.shape[1]

    def whole(array):
        return pl.BlockSpec(array.shape, lambda k, *scalars: (0,) * array.ndim)

    def of_kind(array):
        return pl.BlockSpec((1,) + array.shape[1:], lambda k, kinds, *rest: (kinds[parent, k], 0, 0))

    def of_parent(array):
        return pl.BlockSpec((1,) + array.shape[1:], lambda k, *scalars: (parent, 0, 0, 0))

    shape = jax.ShapeDtypeStruct((disps, half, 4 * wide), BF)
    out_spec = pl.BlockSpec((1, half, 4 * wide), lambda k, *scalars: (k, 0, 0))
    kernel = functools.partial(apply_kernel, half=half, terms=terms, parent=parent)
    if child_slot is None:
        scalars = (kinds,)
        body = lambda kind_ref, *refs: kernel(kind_ref, None, *refs)
        near_spec = of_parent(near)
    else:
        scalars = (kinds, child_slot)
        body = kernel
        near_spec = whole(near)
    return pl.pallas_call(
        body,
        grid_spec=pltpu.PrefetchScalarGridSpec(
            num_scalar_prefetch=len(scalars),
            grid=(disps,),
            in_specs=[near_spec, whole(far), of_kind(table)] + [whole(w) for w in weights],
            out_specs=[out_spec, out_spec],
            scratch_shapes=[
                pltpu.VMEM((4 * edge, wide), BF),
                pltpu.VMEM((4, terms * edge, wide), BF),
            ],
        ),
        out_shape=[shape, shape],
        compiler_params=pltpu.CompilerParams(vmem_limit_bytes=48 * 1024 * 1024),
    )(*scalars, near, far, table, *weights)


def sum_kernel(slot_ref, *refs, rows):
    row_refs, (even_ref, odd_ref, total_ref) = refs[:-3], refs[-3:]
    total_ref[...] = jnp.zeros_like(total_ref)
    for i in range(len(row_refs)):
        for j in range(rows):
            slot = slot_ref[i * rows + j]
            total_ref[slot] = total_ref[slot] + row_refs[i][j].astype(F32)
    count = even_ref.shape[0]
    even_ref[...] = total_ref[:count].astype(BF)
    odd_ref[...] = total_ref[count:].astype(BF)


def sum_rows(slots, arrays, slot_count):
    rows = arrays[0].shape[0]
    tail = arrays[0].shape[1:]
    shape = jax.ShapeDtypeStruct((slot_count // 2,) + tail, BF)
    return pl.pallas_call(
        functools.partial(sum_kernel, rows=rows),
        in_specs=[pl.BlockSpec(memory_space=pltpu.SMEM)]
        + [pl.BlockSpec(memory_space=pltpu.VMEM)] * len(arrays),
        out_specs=[pl.BlockSpec(memory_space=pltpu.VMEM)] * 2,
        out_shape=[shape, shape],
        scratch_shapes=[pltpu.VMEM((slot_count,) + tail, F32)],
        compiler_params=pltpu.CompilerParams(vmem_limit_bytes=60 * 1024 * 1024),
    )(slots, *arrays)


def swap(x, axis, mask):
    count = lax.axis_size(axis)
    return lax.ppermute(x, axis, [(i, i ^ mask) for i in range(count)])


def local(children, child_slot, two_scale, factors, disp_kind, target_leaf, target_node):
    oct_count = lax.axis_size("oct")
    leaf_count = lax.axis_size("leaf")
    my_leaf = lax.axis_index("leaf")
    edge = two_scale.shape[0]
    half = edge // 2
    low = half // 2
    held = child_slot.shape[1]
    parents, disps = disp_kind.shape
    paired = oct_count == 2

    blocks = children.reshape(-1, half, half * half)
    if paired:
        near = blocks
        far = swap(pick_blocks(child_slot, blocks, parents), "oct", 1)
        near_slot = child_slot
    else:
        arrived = lax.all_to_all(
            blocks[child_slot], "oct", split_axis=0, concat_axis=1, tiled=True
        ).reshape(parents, 2, 4, half, half * half)
        near, far = arrived[:, 0], arrived[:, 1]
        near_slot = None

    nodes = 2 * oct_count
    goal = target_leaf.reshape(parents, disps) * nodes + target_node
    if paired:
        goals = jnp.stack([goal, swap(goal, "oct", 1)], axis=1)
    else:
        goals = lax.all_gather(goal, "oct").transpose(1, 0, 2)
    leaf_off = jnp.bitwise_xor(goals // nodes, my_leaf)
    slots = ((leaf_off % 2) * (leaf_count // 2) + leaf_off // 2) * nodes + goals % nodes

    table = factors.reshape(factors.shape[0], -1, 4 * edge)
    weights = make_weights(two_scale, paired)

    arrays = []
    for parent in range(parents):
        kept, sent = apply_parent(
            parent, disp_kind, near_slot, near, far, table, weights, half
        )
        if paired:
            arrays += [kept, swap(sent, "oct", 1)]
        else:
            rows = jnp.stack([kept, sent], axis=1).reshape(disps, 2, half, 2, 2, 2, low * half)
            rows = rows.transpose(1, 3, 5, 0, 2, 4, 6)
            rows = rows.reshape(oct_count, held, disps, half, half * half)
            rows = rows.transpose(0, 2, 1, 3, 4)
            rows = lax.all_to_all(rows, "oct", split_axis=0, concat_axis=0, tiled=True)
            arrays += [rows.reshape(oct_count * disps, held * half, half * half)]

    even, odd = sum_rows(slots.reshape(-1), arrays, leaf_count * nodes)
    total = even.astype(F32) + swap(odd, "leaf", 1).astype(F32)
    total = total.astype(BF).reshape((leaf_count // 2, nodes) + total.shape[1:])
    mask = 2
    while mask < leaf_count:
        pairs = total.reshape((-1, 2) + total.shape[1:])
        total = pairs[:, 0].astype(F32) + swap(pairs[:, 1], "leaf", mask).astype(F32)
        total = total.astype(BF)
        mask *= 2
    total = total.reshape(nodes, -1)
    if paired:
        out = total.reshape(nodes, half, 2, 2, 2, low * half)
        return out.transpose(0, 2, 4, 1, 3, 5).reshape(nodes, held, -1)
    return total.reshape(nodes, held, -1)


def solution(mesh):
    placed = (
        P(("leaf", "oct"), None),
        P("leaf", "oct"),
        P(),
        P(),
        P(("leaf", "oct"), None),
        P(("leaf", "oct"), None, None),
        P(("leaf", "oct"), None),
    )
    return jax.shard_map(
        local, mesh=mesh, in_specs=placed, out_specs=P("leaf", "oct", None), check_vma=False
    )
```

```python
import functools

import jax
import jax.numpy as jnp
from jax import lax
from jax.experimental import pallas as pl
from jax.experimental.pallas import tpu as pltpu
from jax.sharding import PartitionSpec as P

BF = jnp.bfloat16
F32 = jnp.float32


def dot(x, y):
    return jnp.dot(x, y, preferred_element_type=F32)


def one_hot(shape, row_of, lane_of):
    rows = lax.broadcasted_iota(jnp.int32, shape, 0)
    lanes = lax.broadcasted_iota(jnp.int32, shape, 1)
    return (row_of(rows) == lane_of(lanes)).astype(BF)


def exact(x, y):
    return dot(x, y).astype(BF)


def weights_kernel(
    scale_ref, s1e_ref, s2e_ref, m1_ref, m2_ref, fw1_ref, fw2_ref, sa_ref, st_ref, *, half, paired
):
    edge = 2 * half
    low = half // 2
    wide = edge * low
    scale = scale_ref[...]
    turn = lax.axis_index("oct") * half if paired else 0

    def same(x):
        return x

    def turned(x):
        return lax.rem(x + turn, edge)

    def chunked(x):
        return (x % low) * 4 + x // low

    by_chunk = exact(one_hot((edge, edge), chunked, same), scale)
    s1e_ref[...] = exact(by_chunk, one_hot((edge, wide), same, lambda x: x // low))
    s2e_ref[...] = exact(
        by_chunk, one_hot((edge, wide), same, lambda x: x // (wide // 2) * half + x % half)
    )
    m1_ref[...] = one_hot((wide, wide), lambda x: x // edge, lambda x: x % low)
    m2_ref[...] = one_hot((2 * edge, wide), lambda x: x // low, lambda x: x // half % low)
    sa_ref[...] = exact(scale, one_hot((edge, edge), same, turned))
    pick = one_hot((edge, edge), turned, same)
    st_ref[...] = lax.dot_general(
        pick, by_chunk, (((1,), (1,)), ((), ())), preferred_element_type=F32
    ).astype(BF)

    def spread(row_of, lane_of, lane_count):
        rows = lax.dot_general(
            one_hot((wide, edge), row_of, same),
            scale,
            (((1,), (1,)), ((), ())),
            preferred_element_type=F32,
        ).astype(BF)
        return exact(rows, one_hot((edge, lane_count), same, lane_of))

    for bit in range(2):
        fw1_ref[bit] = spread(
            lambda x: x % half + bit * half, lambda x: x // half, 2 * wide
        ) * one_hot((wide, 2 * wide), lambda x: x // half, lambda x: x % half)
    fw2_ref[...] = spread(
        lambda x: x // (wide // 2) * half + x % half, lambda x: x % edge, wide
    ) * one_hot((wide, wide), lambda x: x // half % low, lambda x: x // edge)


def make_weights(two_scale, paired):
    edge = two_scale.shape[0]
    half = edge // 2
    wide = edge * half // 2
    shapes = [
        (edge, wide), (edge, wide), (wide, wide), (2 * edge, wide),
        (2, wide, 2 * wide), (wide, wide), (edge, edge), (edge, edge),
    ]
    return pl.pallas_call(
        functools.partial(weights_kernel, half=half, paired=paired),
        in_specs=[pl.BlockSpec(memory_space=pltpu.VMEM)],
        out_specs=[pl.BlockSpec(memory_space=pltpu.VMEM)] * len(shapes),
        out_shape=[jax.ShapeDtypeStruct(shape, BF) for shape in shapes],
        compiler_params=pltpu.CompilerParams(vmem_limit_bytes=32 * 1024 * 1024),
    )(two_scale)


def pick_kernel(slot_ref, blocks_ref, out_ref, *, parents):
    first = (1 - lax.axis_index("oct")) * parents
    for i in range(parents):
        for j in range(out_ref.shape[1]):
            out_ref[i, j] = blocks_ref[slot_ref[first + i, j]]


def pick_blocks(child_slot, blocks, parents):
    shape = (parents, child_slot.shape[1]) + blocks.shape[1:]
    return pl.pallas_call(
        functools.partial(pick_kernel, parents=parents),
        in_specs=[
            pl.BlockSpec(memory_space=pltpu.SMEM),
            pl.BlockSpec(memory_space=pltpu.VMEM),
        ],
        out_specs=pl.BlockSpec(memory_space=pltpu.VMEM),
        out_shape=jax.ShapeDtypeStruct(shape, BF),
    )(child_slot, blocks)


def by_output(table, edge, terms):
    low = edge // 4
    lanes = 4 * edge
    chunk = lax.broadcasted_iota(jnp.int32, (low, lanes), 1) // edge
    groups = []
    for start in range(0, terms, 4):
        tiles = [
            table[low * min(t, terms - 1) : low * (min(t, terms - 1) + 1)]
            for t in range(start, start + 4)
        ]
        for step in (1, 2):
            upper = (chunk // step) % 2 == 1
            mixed = list(tiles)
            for i in range(4):
                if i & step == 0:
                    mixed[i] = jnp.where(
                        upper, pltpu.roll(tiles[i + step], edge * step, 1), tiles[i]
                    )
                    mixed[i + step] = jnp.where(
                        upper, tiles[i + step], pltpu.roll(tiles[i], lanes - edge * step, 1)
                    )
            tiles = mixed
        groups.append(jnp.concatenate(tiles, axis=0))
    return jnp.concatenate(groups, axis=1)[:, : terms * edge]


def apply_kernel(
    kind_ref, slot_ref, blocks_ref, far_ref, table_ref, s1e_ref, s2e_ref, m1_ref, m2_ref,
    fw1_ref, fw2_ref, sa_ref, st_ref, keep_ref, send_ref, cube_ref, sec_ref,
    *, half, terms, parent,
):
    edge = 2 * half
    low = half // 2
    wide = edge * low
    quarter = wide // 4

    @pl.when(pl.program_id(0) == 0)
    def _():
        if slot_ref is None:
            near = [blocks_ref[0, i] for i in range(4)]
        else:
            first = lax.axis_index("oct") * far_ref.shape[0] + parent
            near = [blocks_ref[slot_ref[first, i]] for i in range(4)]
        total = None
        for bit in range(2):
            rows = []
            for mid in range(2):
                rows += [near[2 * mid + bit], far_ref[parent, 2 * mid + bit]]
            part = dot(jnp.concatenate(rows, axis=0), fw1_ref[bit])
            total = part if total is None else total + part
        total = total.astype(BF)
        lanes = wide // 2
        moved = jnp.concatenate(
            [
                jnp.concatenate(
                    [
                        total[:edge, lanes * i : lanes * (i + 1)],
                        total[edge:, lanes * i : lanes * (i + 1)],
                    ],
                    axis=1,
                )
                for i in range(4)
            ],
            axis=0,
        )
        second = dot(moved, fw2_ref[...]).astype(BF)
        for i in range(4):
            cube_ref[edge * i : edge * (i + 1), :] = dot(
                sa_ref[...], second[edge * i : edge * (i + 1)]
            ).astype(BF)

    cube = cube_ref[...]
    table = table_ref[0].astype(F32)
    rows = terms * low
    f0, f1, f2 = [
        by_output(table[rows * i : rows * (i + 1)], edge, terms) for i in range(3)
    ]
    ft1 = f1.T.astype(BF)
    ft2 = f2.T.reshape(terms * 4, 1, low, edge)
    ft2 = jnp.broadcast_to(ft2, (terms * 4, 2, low, edge)).reshape(terms * 2 * edge, edge)
    w1e = dot(ft1, s1e_ref[...]).astype(BF)
    w2e = dot(ft2.astype(BF), s2e_ref[...]).astype(BF)
    g0 = dot(st_ref[...], f0.astype(BF)).astype(BF)
    for t in range(terms):
        one = w1e[edge * t : edge * (t + 1)]
        w1 = jnp.concatenate(
            [one * m1_ref[edge * i : edge * (i + 1), :] for i in range(low)], axis=0
        )
        first = dot(cube, w1).astype(BF)
        moved = jnp.concatenate(
            [
                jnp.concatenate(
                    [
                        first[edge * i : edge * (i + 1), quarter * j : quarter * (j + 1)]
                        for i in range(4)
                    ],
                    axis=1,
                )
                for j in range(4)
            ],
            axis=0,
        )
        base = 2 * edge * t
        w2 = jnp.concatenate(
            [
                w2e[base + half * i : base + half * (i + 1)] * m2_ref[half * q : half * (q + 1), :]
                for i in range(4)
                for q in range(low // 2)
            ],
            axis=0,
        )
        second = dot(moved, w2).astype(BF)
        for i in range(4):
            sec_ref[i, edge * t : edge * (t + 1), :] = second[edge * i : edge * (i + 1)]
    for i in range(4):
        out = dot(g0, sec_ref[i]).astype(BF)
        keep_ref[0, :, wide * i : wide * (i + 1)] = out[:half]
        send_ref[0, :, wide * i : wide * (i + 1)] = out[half:]


def apply_parent(parent, kinds, child_slot, near, far, table, weights, half):
    edge = 2 * half
    wide = edge * half // 2
    terms = table.shape[1] // (3 * edge // 4)
    disps = kinds.shape[1]

    def whole(array):
        return pl.BlockSpec(array.shape, lambda k, *scalars: (0,) * array.ndim)

    def of_kind(array):
        return pl.BlockSpec((1,) + array.shape[1:], lambda k, kinds, *rest: (kinds[parent, k], 0, 0))

    def of_parent(array):
        return pl.BlockSpec((1,) + array.shape[1:], lambda k, *scalars: (parent, 0, 0, 0))

    shape = jax.ShapeDtypeStruct((disps, half, 4 * wide), BF)
    out_spec = pl.BlockSpec((1, half, 4 * wide), lambda k, *scalars: (k, 0, 0))
    kernel = functools.partial(apply_kernel, half=half, terms=terms, parent=parent)
    if child_slot is None:
        scalars = (kinds,)
        body = lambda kind_ref, *refs: kernel(kind_ref, None, *refs)
        near_spec = of_parent(near)
    else:
        scalars = (kinds, child_slot)
        body = kernel
        near_spec = whole(near)
    return pl.pallas_call(
        body,
        grid_spec=pltpu.PrefetchScalarGridSpec(
            num_scalar_prefetch=len(scalars),
            grid=(disps,),
            in_specs=[near_spec, whole(far), of_kind(table)] + [whole(w) for w in weights],
            out_specs=[out_spec, out_spec],
            scratch_shapes=[
                pltpu.VMEM((4 * edge, wide), BF),
                pltpu.VMEM((4, terms * edge, wide), BF),
            ],
        ),
        out_shape=[shape, shape],
        compiler_params=pltpu.CompilerParams(vmem_limit_bytes=48 * 1024 * 1024),
    )(*scalars, near, far, table, *weights)


def sum_kernel(slot_ref, *refs, rows):
    row_refs, (even_ref, odd_ref, total_ref) = refs[:-3], refs[-3:]
    total_ref[...] = jnp.zeros_like(total_ref)
    for i in range(len(row_refs)):
        for j in range(rows):
            slot = slot_ref[i * rows + j]
            total_ref[slot] = total_ref[slot] + row_refs[i][j].astype(F32)
    count = even_ref.shape[0]
    even_ref[...] = total_ref[:count].astype(BF)
    odd_ref[...] = total_ref[count:].astype(BF)


def sum_rows(slots, arrays, slot_count):
    rows = arrays[0].shape[0]
    tail = arrays[0].shape[1:]
    shape = jax.ShapeDtypeStruct((slot_count // 2,) + tail, BF)
    return pl.pallas_call(
        functools.partial(sum_kernel, rows=rows),
        in_specs=[pl.BlockSpec(memory_space=pltpu.SMEM)]
        + [pl.BlockSpec(memory_space=pltpu.VMEM)] * len(arrays),
        out_specs=[pl.BlockSpec(memory_space=pltpu.VMEM)] * 2,
        out_shape=[shape, shape],
        scratch_shapes=[pltpu.VMEM((slot_count,) + tail, F32)],
        compiler_params=pltpu.CompilerParams(vmem_limit_bytes=60 * 1024 * 1024),
    )(slots, *arrays)


def combine_kernel(*refs, bits, lanes, inputs, last):
    kept, arrived, outs = refs[:inputs], refs[inputs : 2 * inputs], refs[2 * inputs :]
    for i, bit in enumerate(bits):
        source, start = (i, 0) if inputs == len(bits) else (0, lanes * i)
        for r in range(arrived[source].shape[0]):
            total = kept[source][r, :, :, start : start + lanes].astype(F32)
            total = total + arrived[source][r, :, :, start : start + lanes].astype(F32)
            total = total.astype(BF)
            if not last:
                place = (r >> (bit + 1) << bit) | (r & ((1 << bit) - 1))
                outs[2 * i + (r >> bit & 1)][place] = total
            elif outs[0].shape[1] == 4:
                half = lanes // 4
                for c in range(4):
                    to = half * (c // 2)
                    outs[0][:, 2 * i + c % 2, :, to : to + half] = total[
                        :, :, half * c : half * (c + 1)
                    ]
            else:
                outs[0][:, 0, :, lanes * i : lanes * (i + 1)] = total


def combine(kept, arrived, bits, out=None):
    lanes = arrived[0].shape[-1] * len(arrived) // len(bits)
    if out is None:
        shape = (arrived[0].shape[0] // 2,) + arrived[0].shape[1:3] + (lanes,)
        shapes = [shape] * (2 * len(bits))
    else:
        shapes = [out]
    return pl.pallas_call(
        functools.partial(
            combine_kernel, bits=bits, lanes=lanes, inputs=len(kept), last=out is not None
        ),
        in_specs=[pl.BlockSpec(memory_space=pltpu.VMEM)] * (2 * len(kept)),
        out_specs=[pl.BlockSpec(memory_space=pltpu.VMEM)] * len(shapes),
        out_shape=[jax.ShapeDtypeStruct(shape, BF) for shape in shapes],
        compiler_params=pltpu.CompilerParams(vmem_limit_bytes=48 * 1024 * 1024),
    )(*kept, *arrived)


def swap(x, axis, mask):
    count = lax.axis_size(axis)
    return lax.ppermute(x, axis, [(i, i ^ mask) for i in range(count)])


def local(children, child_slot, two_scale, factors, disp_kind, target_leaf, target_node):
    oct_count = lax.axis_size("oct")
    leaf_count = lax.axis_size("leaf")
    my_leaf = lax.axis_index("leaf")
    edge = two_scale.shape[0]
    half = edge // 2
    low = half // 2
    held = child_slot.shape[1]
    parents, disps = disp_kind.shape
    paired = oct_count == 2

    blocks = children.reshape(-1, half, half * half)
    if paired:
        near = blocks
        far = swap(pick_blocks(child_slot, blocks, parents), "oct", 1)
        near_slot = child_slot
    else:
        arrived = lax.all_to_all(
            blocks[child_slot], "oct", split_axis=0, concat_axis=1, tiled=True
        ).reshape(parents, 2, 4, half, half * half)
        near, far = arrived[:, 0], arrived[:, 1]
        near_slot = None

    nodes = 2 * oct_count
    goal = target_leaf.reshape(parents, disps) * nodes + target_node
    if paired:
        goals = jnp.stack([goal, swap(goal, "oct", 1)], axis=1)
    else:
        goals = lax.all_gather(goal, "oct").transpose(1, 0, 2)
    leaf_off = jnp.bitwise_xor(goals // nodes, my_leaf)
    slots = ((leaf_off % 2) * (leaf_count // 2) + leaf_off // 2) * nodes + goals % nodes

    table = factors.reshape(factors.shape[0], -1, 4 * edge)
    weights = make_weights(two_scale, paired)

    arrays = []
    for parent in range(parents):
        kept, sent = apply_parent(
            parent, disp_kind, near_slot, near, far, table, weights, half
        )
        if paired:
            arrays += [kept, swap(sent, "oct", 1)]
        else:
            rows = jnp.stack([kept, sent], axis=1).reshape(disps, 2, half, 2, 2, 2, low * half)
            rows = rows.transpose(1, 3, 5, 0, 2, 4, 6)
            rows = rows.reshape(oct_count, held, disps, half, half * half)
            rows = rows.transpose(0, 2, 1, 3, 4)
            rows = lax.all_to_all(rows, "oct", split_axis=0, concat_axis=0, tiled=True)
            arrays += [rows.reshape(oct_count * disps, held * half, half * half)]

    even, odd = sum_rows(slots.reshape(-1), arrays, leaf_count * nodes)
    shape = (leaf_count // 2, nodes) + even.shape[1:]
    even = even.reshape(shape)
    odd = swap(odd, "leaf", 1).reshape(shape)
    masks = [1 << i for i in range(1, (leaf_count - 1).bit_length())]
    orders = [masks, masks[1::-1] + masks[2:]]
    left = [list(masks), list(masks)]
    kept, arrived = [even], [odd]
    for step in range(len(masks)):
        bits = [left[i].index(orders[i][step]) for i in range(2)]
        parts = combine(kept, arrived, bits)
        kept = [parts[0], parts[2]]
        arrived = [swap(parts[2 * i + 1], "leaf", orders[i][step]) for i in range(2)]
        for i in range(2):
            left[i].remove(orders[i][step])
    tail = (nodes, held, half, half * half) if paired else (nodes, 1) + shape[2:]
    (out,) = combine(kept, arrived, (0, 0), tail)
    return out.reshape(nodes, held, -1)


def solution(mesh):
    placed = (
        P(("leaf", "oct"), None),
        P("leaf", "oct"),
        P(),
        P(),
        P(("leaf", "oct"), None),
        P(("leaf", "oct"), None, None),
        P(("leaf", "oct"), None),
    )
    return jax.shard_map(
        local, mesh=mesh, in_specs=placed, out_specs=P("leaf", "oct", None), check_vma=False
    )
```

```python
import functools

import jax
import jax.numpy as jnp
from jax import lax
from jax.experimental import pallas as pl
from jax.experimental.pallas import tpu as pltpu
from jax.sharding import PartitionSpec as P

BF = jnp.bfloat16
F32 = jnp.float32


def dot(x, y):
    return jnp.dot(x, y, preferred_element_type=F32)


def one_hot(shape, row_of, lane_of):
    rows = lax.broadcasted_iota(jnp.int32, shape, 0)
    lanes = lax.broadcasted_iota(jnp.int32, shape, 1)
    return (row_of(rows) == lane_of(lanes)).astype(BF)


def exact(x, y):
    return dot(x, y).astype(BF)


def weights_kernel(
    scale_ref, s1e_ref, s2e_ref, m1_ref, m2_ref, fw1_ref, fw2_ref, sa_ref, st_ref, *, half, paired
):
    edge = 2 * half
    low = half // 2
    wide = edge * low
    scale = scale_ref[...]
    turn = lax.axis_index("oct") * half if paired else 0

    def same(x):
        return x

    def turned(x):
        return lax.rem(x + turn, edge)

    def chunked(x):
        return (x % low) * 4 + x // low

    by_chunk = exact(one_hot((edge, edge), chunked, same), scale)
    s1e_ref[...] = exact(by_chunk, one_hot((edge, wide), same, lambda x: x // low))
    s2e_ref[...] = exact(by_chunk, one_hot((edge, wide // 2), same, lambda x: x % edge))
    m1_ref[...] = one_hot((low * half, wide), lambda x: x // half, lambda x: x % low)
    m2_ref[...] = one_hot((edge, wide // 2), lambda x: x // low, lambda x: x // edge)
    sa_ref[...] = exact(scale, one_hot((edge, edge), same, turned))
    pick = one_hot((edge, edge), turned, same)
    st_ref[...] = lax.dot_general(
        pick, by_chunk, (((1,), (1,)), ((), ())), preferred_element_type=F32
    ).astype(BF)

    def spread(row_of, lane_of, lane_count):
        rows = lax.dot_general(
            one_hot((wide, edge), row_of, same),
            scale,
            (((1,), (1,)), ((), ())),
            preferred_element_type=F32,
        ).astype(BF)
        return exact(rows, one_hot((edge, lane_count), same, lane_of))

    for bit in range(2):
        fw1_ref[bit] = spread(
            lambda x: x % half + bit * half, lambda x: x // half, 2 * wide
        ) * one_hot((wide, 2 * wide), lambda x: x // half, lambda x: x % half)
    fw2_ref[...] = spread(
        lambda x: x // (wide // 2) * half + x % half, lambda x: x % edge, wide
    ) * one_hot((wide, wide), lambda x: x // half % low, lambda x: x // edge)


def make_weights(two_scale, paired):
    edge = two_scale.shape[0]
    half = edge // 2
    low = half // 2
    wide = edge * low
    shapes = [
        (edge, wide), (edge, wide // 2), (low * half, wide), (edge, wide // 2),
        (2, wide, 2 * wide), (wide, wide), (edge, edge), (edge, edge),
    ]
    return pl.pallas_call(
        functools.partial(weights_kernel, half=half, paired=paired),
        in_specs=[pl.BlockSpec(memory_space=pltpu.VMEM)],
        out_specs=[pl.BlockSpec(memory_space=pltpu.VMEM)] * len(shapes),
        out_shape=[jax.ShapeDtypeStruct(shape, BF) for shape in shapes],
        compiler_params=pltpu.CompilerParams(vmem_limit_bytes=24 * 1024 * 1024),
    )(two_scale)


def pick_kernel(slot_ref, blocks_ref, out_ref, *, parents):
    first = (1 - lax.axis_index("oct")) * parents
    for i in range(parents):
        for j in range(out_ref.shape[1]):
            out_ref[i, j] = blocks_ref[slot_ref[j, first + i]]


def pick_blocks(child_slot, blocks, parents):
    shape = (parents, child_slot.shape[0]) + blocks.shape[1:]
    return pl.pallas_call(
        functools.partial(pick_kernel, parents=parents),
        in_specs=[
            pl.BlockSpec(memory_space=pltpu.SMEM),
            pl.BlockSpec(memory_space=pltpu.VMEM),
        ],
        out_specs=pl.BlockSpec(memory_space=pltpu.VMEM),
        out_shape=jax.ShapeDtypeStruct(shape, BF),
    )(child_slot, blocks)


def by_output(table, edge, terms):
    low = edge // 4
    lanes = 4 * edge
    chunk = lax.broadcasted_iota(jnp.int32, (low, lanes), 1) // edge
    groups = []
    for start in range(0, terms, 4):
        tiles = [
            table[low * min(t, terms - 1) : low * (min(t, terms - 1) + 1)]
            for t in range(start, start + 4)
        ]
        for step in (1, 2):
            upper = (chunk // step) % 2 == 1
            mixed = list(tiles)
            for i in range(4):
                if i & step == 0:
                    mixed[i] = jnp.where(
                        upper, pltpu.roll(tiles[i + step], edge * step, 1), tiles[i]
                    )
                    mixed[i + step] = jnp.where(
                        upper, tiles[i + step], pltpu.roll(tiles[i], lanes - edge * step, 1)
                    )
            tiles = mixed
        groups.append(jnp.concatenate(tiles, axis=0))
    return jnp.concatenate(groups, axis=1)[:, : terms * edge]


def apply_kernel(
    kind_ref, *refs, half, terms, parent, picked,
):
    if picked:
        slot_ref, refs = refs[0], refs[1:]
    (
        blocks_ref, far_ref, table_ref, s1e_ref, s2e_ref, m1_ref, m2_ref, fw1_ref, fw2_ref,
        sa_ref, st_ref, keep_ref, send_ref, cube_ref, sec_ref,
    ) = refs[:15]
    sets = refs[15:18], refs[18:21]
    edge = 2 * half
    low = half // 2
    wide = edge * low
    quarter = wide // 4
    rows = terms * low
    step = pl.program_id(0)

    def expand(axis, kind, into):
        table = table_ref[kind, rows * axis : rows * (axis + 1), :].astype(F32)
        spread = by_output(table, edge, terms)
        if axis == 0:
            into[0][...] = dot(st_ref[...], spread.astype(BF)).astype(BF)
        elif axis == 1:
            into[1][...] = dot(spread.T.astype(BF), s1e_ref[...]).astype(BF)
        else:
            once = dot(spread.T.astype(BF), s2e_ref[...])
            for i in range(terms * 4):
                tile = once[low * i : low * (i + 1)]
                into[2][half * i : half * (i + 1), :] = jnp.concatenate(
                    [tile, tile], axis=0
                ).astype(BF)

    @pl.when(step == 0)
    def _():
        if picked:
            first = lax.axis_index("oct") * far_ref.shape[0] + parent
            near = [blocks_ref[slot_ref[i, first]] for i in range(4)]
        else:
            near = [blocks_ref[parent, i] for i in range(4)]
        total = None
        for bit in range(2):
            parts = []
            for mid in range(2):
                parts += [near[2 * mid + bit], far_ref[parent, 2 * mid + bit]]
            part = dot(jnp.concatenate(parts, axis=0), fw1_ref[bit])
            total = part if total is None else total + part
        total = total.astype(BF)
        lanes = wide // 2
        moved = jnp.concatenate(
            [
                jnp.concatenate(
                    [
                        total[:edge, lanes * i : lanes * (i + 1)],
                        total[edge:, lanes * i : lanes * (i + 1)],
                    ],
                    axis=1,
                )
                for i in range(4)
            ],
            axis=0,
        )
        second = dot(moved, fw2_ref[...]).astype(BF)
        for i in range(4):
            cube_ref[edge * i : edge * (i + 1), :] = dot(
                sa_ref[...], second[edge * i : edge * (i + 1)]
            ).astype(BF)
        for axis in range(3):
            expand(axis, kind_ref[parent, 0], sets[0])

    def entry(now, after):
        g0_ref, w1e_ref, w2e_ref = now
        next_kind = kind_ref[parent, jnp.minimum(step + 1, kind_ref.shape[1] - 1)]
        cube = cube_ref[...]
        none = jnp.zeros((half, wide // 2), BF)
        for t in range(terms):
            one = w1e_ref[edge * t : edge * (t + 1), :]
            w1 = jnp.concatenate(
                [
                    one[half * j : half * (j + 1)] * m1_ref[half * i : half * (i + 1), :]
                    for i in range(low)
                    for j in range(2)
                ],
                axis=0,
            )
            first = dot(cube, w1).astype(BF)
            moved = jnp.concatenate(
                [
                    jnp.concatenate(
                        [
                            first[edge * i : edge * (i + 1), quarter * j : quarter * (j + 1)]
                            for i in range(4)
                        ],
                        axis=1,
                    )
                    for j in range(4)
                ],
                axis=0,
            )
            w2 = []
            for i in range(4):
                tile = w2e_ref[half * (4 * t + i) : half * (4 * t + i + 1), :]
                pair = [tile * m2_ref[half * q : half * (q + 1), :] for q in range(2)]
                w2 += [jnp.concatenate([x, none], axis=1) for x in pair]
                w2 += [jnp.concatenate([none, x], axis=1) for x in pair]
            second = dot(moved, jnp.concatenate(w2, axis=0)).astype(BF)
            for i in range(4):
                sec_ref[i, edge * t : edge * (t + 1), :] = second[edge * i : edge * (i + 1)]
            if t % 3 == 0 and t // 3 < 3:
                expand(t // 3, next_kind, after)
        for i in range(4):
            out = dot(g0_ref[...], sec_ref[i]).astype(BF)
            keep_ref[step, :, wide * i : wide * (i + 1)] = out[:half]
            send_ref[step, :, wide * i : wide * (i + 1)] = out[half:]

    @pl.when(step % 2 == 0)
    def _():
        entry(sets[0], sets[1])

    @pl.when(step % 2 == 1)
    def _():
        entry(sets[1], sets[0])


def apply_parent(parent, kinds, child_slot, near, far, table, weights, half):
    edge = 2 * half
    wide = edge * half // 2
    terms = table.shape[1] // (3 * edge // 4)
    disps = kinds.shape[1]
    shape = jax.ShapeDtypeStruct((disps, half, 4 * wide), BF)
    scalars = (kinds,) if child_slot is None else (kinds, child_slot)
    arrays = (near, far, table) + tuple(weights)
    expanded = [
        pltpu.VMEM((edge, terms * edge), BF),
        pltpu.VMEM((terms * edge, wide), BF),
        pltpu.VMEM((terms * 2 * edge, wide // 2), BF),
    ]
    return pl.pallas_call(
        functools.partial(
            apply_kernel, half=half, terms=terms, parent=parent, picked=child_slot is not None
        ),
        grid=(disps,),
        in_specs=[pl.BlockSpec(memory_space=pltpu.SMEM)] * len(scalars)
        + [pl.BlockSpec(memory_space=pltpu.VMEM)] * len(arrays),
        out_specs=[pl.BlockSpec(memory_space=pltpu.VMEM)] * 2,
        out_shape=[shape, shape],
        scratch_shapes=[
            pltpu.VMEM((4 * edge, wide), BF),
            pltpu.VMEM((4, terms * edge, wide), BF),
        ]
        + expanded * 2,
        compiler_params=pltpu.CompilerParams(vmem_limit_bytes=24 * 1024 * 1024),
    )(*scalars, *arrays)


def sum_kernel(slot_ref, *refs, rows):
    row_refs, (even_ref, odd_ref, total_ref) = refs[:-3], refs[-3:]
    total_ref[...] = jnp.zeros_like(total_ref)
    for i in range(len(row_refs)):
        for j in range(rows):
            slot = slot_ref[i * rows + j]
            total_ref[slot] = total_ref[slot] + row_refs[i][j].astype(F32)
    count = even_ref.shape[0]
    even_ref[...] = total_ref[:count].astype(BF)
    odd_ref[...] = total_ref[count:].astype(BF)


def sum_rows(slots, arrays, slot_count):
    rows = arrays[0].shape[0]
    tail = arrays[0].shape[1:]
    shape = jax.ShapeDtypeStruct((slot_count // 2,) + tail, BF)
    return pl.pallas_call(
        functools.partial(sum_kernel, rows=rows),
        in_specs=[pl.BlockSpec(memory_space=pltpu.SMEM)]
        + [pl.BlockSpec(memory_space=pltpu.VMEM)] * len(arrays),
        out_specs=[pl.BlockSpec(memory_space=pltpu.VMEM)] * 2,
        out_shape=[shape, shape],
        scratch_shapes=[pltpu.VMEM((slot_count,) + tail, F32)],
        compiler_params=pltpu.CompilerParams(vmem_limit_bytes=24 * 1024 * 1024),
    )(slots, *arrays)


def combine_kernel(*refs, bits, lanes, inputs, last):
    kept, arrived, outs = refs[:inputs], refs[inputs : 2 * inputs], refs[2 * inputs :]
    for i, bit in enumerate(bits):
        source, start = (i, 0) if inputs == len(bits) else (0, lanes * i)
        for r in range(arrived[source].shape[0]):
            total = kept[source][r, :, :, start : start + lanes].astype(F32)
            total = total + arrived[source][r, :, :, start : start + lanes].astype(F32)
            total = total.astype(BF)
            if not last:
                place = (r >> (bit + 1) << bit) | (r & ((1 << bit) - 1))
                outs[2 * i + (r >> bit & 1)][place] = total
            elif outs[0].shape[1] == 4:
                wide = lanes // 2
                half = wide // 16
                order = one_hot(
                    (wide, wide),
                    lambda x: x % (2 * half) // half * (wide // 2) + x // (2 * half) * half + x % half,
                    lambda x: x,
                )
                for n in range(total.shape[0]):
                    for c in range(2):
                        moved = exact(total[n, :, wide * c : wide * (c + 1)], order)
                        to = wide // 2 * c
                        for bit in range(2):
                            outs[0][n, 2 * i + bit, :, to : to + wide // 2] = moved[
                                :, wide // 2 * bit : wide // 2 * (bit + 1)
                            ]
            else:
                outs[0][:, 0, :, lanes * i : lanes * (i + 1)] = total


def combine(kept, arrived, bits, out=None):
    lanes = arrived[0].shape[-1] * len(arrived) // len(bits)
    if out is None:
        shape = (arrived[0].shape[0] // 2,) + arrived[0].shape[1:3] + (lanes,)
        shapes = [shape] * (2 * len(bits))
    else:
        shapes = [out]
    return pl.pallas_call(
        functools.partial(
            combine_kernel, bits=bits, lanes=lanes, inputs=len(kept), last=out is not None
        ),
        in_specs=[pl.BlockSpec(memory_space=pltpu.VMEM)] * (2 * len(kept)),
        out_specs=[pl.BlockSpec(memory_space=pltpu.VMEM)] * len(shapes),
        out_shape=[jax.ShapeDtypeStruct(shape, BF) for shape in shapes],
        compiler_params=pltpu.CompilerParams(vmem_limit_bytes=24 * 1024 * 1024),
    )(*kept, *arrived)


def swap(x, axis, mask):
    count = lax.axis_size(axis)
    return lax.ppermute(x, axis, [(i, i ^ mask) for i in range(count)])


def local(children, child_slot, two_scale, factors, disp_kind, target_leaf, target_node):
    oct_count = lax.axis_size("oct")
    leaf_count = lax.axis_size("leaf")
    my_leaf = lax.axis_index("leaf")
    edge = two_scale.shape[0]
    half = edge // 2
    held = child_slot.shape[1]
    parents, disps = disp_kind.shape
    paired = oct_count == 2

    blocks = children.reshape(-1, half, half * half)
    if paired:
        near = blocks
        near_slot = child_slot.T
        far = swap(pick_blocks(near_slot, blocks, parents), "oct", 1)
    else:
        arrived = lax.all_to_all(
            blocks[child_slot], "oct", split_axis=0, concat_axis=1, tiled=True
        ).reshape(parents, 2, 4, half, half * half)
        near, far = arrived[:, 0], arrived[:, 1]
        near_slot = None

    nodes = 2 * oct_count
    goal = target_leaf.reshape(parents, disps) * nodes + target_node
    if paired:
        goals = jnp.stack([goal, swap(goal, "oct", 1)], axis=1)
    else:
        goals = lax.all_gather(goal, "oct").transpose(1, 0, 2)
    leaf_off = jnp.bitwise_xor(goals // nodes, my_leaf)
    slots = ((leaf_off % 2) * (leaf_count // 2) + leaf_off // 2) * nodes + goals % nodes

    table = factors.reshape(factors.shape[0], -1, 4 * edge)
    weights = make_weights(two_scale, paired)

    arrays = []
    for parent in range(parents):
        kept, sent = apply_parent(
            parent, disp_kind, near_slot, near, far, table, weights, half
        )
        if paired:
            arrays += [kept, swap(sent, "oct", 1)]
        else:
            rows = jnp.stack([kept, sent], axis=1).reshape(disps, 2, half, 2, half, 2, half)
            rows = rows.transpose(1, 3, 5, 0, 2, 4, 6)
            rows = rows.reshape(oct_count, held, disps, half, half * half)
            rows = rows.transpose(0, 2, 1, 3, 4)
            rows = lax.all_to_all(rows, "oct", split_axis=0, concat_axis=0, tiled=True)
            arrays += [rows.reshape(oct_count * disps, held * half, half * half)]

    even, odd = sum_rows(slots.reshape(-1), arrays, leaf_count * nodes)
    shape = (leaf_count // 2, nodes) + even.shape[1:]
    even = even.reshape(shape)
    odd = swap(odd, "leaf", 1).reshape(shape)
    masks = [1 << i for i in range(1, (leaf_count - 1).bit_length())]
    orders = [masks, masks[1::-1] + masks[2:]]
    left = [list(masks), list(masks)]
    kept, arrived = [even], [odd]
    for step in range(len(masks)):
        bits = [left[i].index(orders[i][step]) for i in range(2)]
        parts = combine(kept, arrived, bits)
        kept = [parts[0], parts[2]]
        arrived = [swap(parts[2 * i + 1], "leaf", orders[i][step]) for i in range(2)]
        for i in range(2):
            left[i].remove(orders[i][step])
    tail = (nodes, held, half, half * half) if paired else (nodes, 1) + shape[2:]
    (out,) = combine(kept, arrived, (0, 0), tail)
    return out.reshape(nodes, held, -1)


def solution(mesh):
    placed = (
        P(("leaf", "oct"), None),
        P("leaf", "oct"),
        P(),
        P(),
        P(("leaf", "oct"), None),
        P(("leaf", "oct"), None, None),
        P(("leaf", "oct"), None),
    )
    return jax.shard_map(
        local, mesh=mesh, in_specs=placed, out_specs=P("leaf", "oct", None), check_vma=False
    )
```

```python
import functools

import jax
import jax.numpy as jnp
from jax import lax
from jax.experimental import pallas as pl
from jax.experimental.pallas import tpu as pltpu
from jax.sharding import PartitionSpec as P

BF = jnp.bfloat16
F32 = jnp.float32


def dot(x, y):
    return jnp.dot(x, y, preferred_element_type=F32)


def one_hot(shape, row_of, lane_of):
    rows = lax.broadcasted_iota(jnp.int32, shape, 0)
    lanes = lax.broadcasted_iota(jnp.int32, shape, 1)
    return (row_of(rows) == lane_of(lanes)).astype(BF)


def exact(x, y):
    return dot(x, y).astype(BF)


def weights_kernel(
    scale_ref, s1e_ref, s2e_ref, m1_ref, m2_ref, fw1_ref, fw2_ref, sa_ref, st_ref, *, half, paired
):
    edge = 2 * half
    low = half // 2
    wide = edge * low
    scale = scale_ref[...]
    turn = lax.axis_index("oct") * half if paired else 0

    def same(x):
        return x

    def turned(x):
        return lax.rem(x + turn, edge)

    def chunked(x):
        return (x % low) * 4 + x // low

    by_chunk = exact(one_hot((edge, edge), chunked, same), scale)
    s1e_ref[...] = exact(by_chunk, one_hot((edge, wide), same, lambda x: x // low))
    s2e_ref[...] = exact(by_chunk, one_hot((edge, wide // 2), same, lambda x: x % edge))
    m1_ref[...] = one_hot((low * half, wide), lambda x: x // half, lambda x: x % low)
    m2_ref[...] = one_hot((edge, wide // 2), lambda x: x // low, lambda x: x // edge)
    sa_ref[...] = exact(scale, one_hot((edge, edge), same, turned))
    pick = one_hot((edge, edge), turned, same)
    st_ref[...] = lax.dot_general(
        pick, by_chunk, (((1,), (1,)), ((), ())), preferred_element_type=F32
    ).astype(BF)

    def spread(row_of, lane_of, lane_count):
        rows = lax.dot_general(
            one_hot((wide, edge), row_of, same),
            scale,
            (((1,), (1,)), ((), ())),
            preferred_element_type=F32,
        ).astype(BF)
        return exact(rows, one_hot((edge, lane_count), same, lane_of))

    for bit in range(2):
        fw1_ref[bit] = spread(
            lambda x: x % half + bit * half, lambda x: x // half, 2 * wide
        ) * one_hot((wide, 2 * wide), lambda x: x // half, lambda x: x % half)
    fw2_ref[...] = spread(
        lambda x: x // (wide // 2) * half + x % half, lambda x: x % edge, wide
    ) * one_hot((wide, wide), lambda x: x // half % low, lambda x: x // edge)


def make_weights(two_scale, paired):
    edge = two_scale.shape[0]
    half = edge // 2
    low = half // 2
    wide = edge * low
    shapes = [
        (edge, wide), (edge, wide // 2), (low * half, wide), (edge, wide // 2),
        (2, wide, 2 * wide), (wide, wide), (edge, edge), (edge, edge),
    ]
    return pl.pallas_call(
        functools.partial(weights_kernel, half=half, paired=paired),
        in_specs=[pl.BlockSpec(memory_space=pltpu.VMEM)],
        out_specs=[pl.BlockSpec(memory_space=pltpu.VMEM)] * len(shapes),
        out_shape=[jax.ShapeDtypeStruct(shape, BF) for shape in shapes],
        compiler_params=pltpu.CompilerParams(vmem_limit_bytes=24 * 1024 * 1024),
    )(two_scale)


def pick_kernel(slot_ref, blocks_ref, out_ref, *, parents):
    first = (1 - lax.axis_index("oct")) * parents
    for i in range(parents):
        for j in range(out_ref.shape[1]):
            out_ref[i, j] = blocks_ref[slot_ref[j, first + i]]


def pick_blocks(child_slot, blocks, parents):
    shape = (parents, child_slot.shape[0]) + blocks.shape[1:]
    return pl.pallas_call(
        functools.partial(pick_kernel, parents=parents),
        in_specs=[
            pl.BlockSpec(memory_space=pltpu.SMEM),
            pl.BlockSpec(memory_space=pltpu.VMEM),
        ],
        out_specs=pl.BlockSpec(memory_space=pltpu.VMEM),
        out_shape=jax.ShapeDtypeStruct(shape, BF),
    )(child_slot, blocks)


def by_output(table, edge, terms):
    low = edge // 4
    lanes = 4 * edge
    chunk = lax.broadcasted_iota(jnp.int32, (low, lanes), 1) // edge
    groups = []
    for start in range(0, terms, 4):
        tiles = [
            table[low * min(t, terms - 1) : low * (min(t, terms - 1) + 1)]
            for t in range(start, start + 4)
        ]
        for step in (1, 2):
            upper = (chunk // step) % 2 == 1
            mixed = list(tiles)
            for i in range(4):
                if i & step == 0:
                    mixed[i] = jnp.where(
                        upper, pltpu.roll(tiles[i + step], edge * step, 1), tiles[i]
                    )
                    mixed[i + step] = jnp.where(
                        upper, tiles[i + step], pltpu.roll(tiles[i], lanes - edge * step, 1)
                    )
            tiles = mixed
        groups.append(jnp.concatenate(tiles, axis=0))
    return jnp.concatenate(groups, axis=1)[:, : terms * edge]


def apply_kernel(
    kind_ref, *refs, half, terms, parent, picked,
):
    if picked:
        slot_ref, refs = refs[0], refs[1:]
    (
        blocks_ref, far_ref, table_ref, s1e_ref, s2e_ref, m1_ref, m2_ref, fw1_ref, fw2_ref,
        sa_ref, st_ref, keep_ref, send_ref, cube_ref, sec_ref,
    ) = refs[:15]
    expanded = refs[15:]
    edge = 2 * half
    low = half // 2
    wide = edge * low
    quarter = wide // 4
    rows = terms * low
    step = pl.program_id(0)

    def expand(kinds):
        g0_ref, w1e_ref, w2e_ref = expanded
        spread = [
            [
                by_output(
                    table_ref[kind, rows * axis : rows * (axis + 1), :].astype(F32), edge, terms
                ).astype(BF)
                for kind in kinds
            ]
            for axis in range(3)
        ]
        turned = [[x.T for x in spread[axis]] for axis in (1, 2)]
        for k in range(len(kinds)):
            g0_ref[k] = dot(st_ref[...], spread[0][k]).astype(BF)
        for k in range(len(kinds)):
            w1e_ref[k] = dot(turned[0][k], s1e_ref[...]).astype(BF)
        for k in range(len(kinds)):
            once = dot(turned[1][k], s2e_ref[...])
            for i in range(terms * 4):
                tile = once[low * i : low * (i + 1)]
                w2e_ref[k, half * i : half * (i + 1), :] = jnp.concatenate(
                    [tile, tile], axis=0
                ).astype(BF)

    @pl.when(step == 0)
    def _():
        if picked:
            first = lax.axis_index("oct") * far_ref.shape[0] + parent
            near = [blocks_ref[slot_ref[i, first]] for i in range(4)]
        else:
            near = [blocks_ref[parent, i] for i in range(4)]
        total = None
        for bit in range(2):
            parts = []
            for mid in range(2):
                parts += [near[2 * mid + bit], far_ref[parent, 2 * mid + bit]]
            part = dot(jnp.concatenate(parts, axis=0), fw1_ref[bit])
            total = part if total is None else total + part
        total = total.astype(BF)
        lanes = wide // 2
        moved = jnp.concatenate(
            [
                jnp.concatenate(
                    [
                        total[:edge, lanes * i : lanes * (i + 1)],
                        total[edge:, lanes * i : lanes * (i + 1)],
                    ],
                    axis=1,
                )
                for i in range(4)
            ],
            axis=0,
        )
        second = dot(moved, fw2_ref[...]).astype(BF)
        for i in range(4):
            cube_ref[edge * i : edge * (i + 1), :] = dot(
                sa_ref[...], second[edge * i : edge * (i + 1)]
            ).astype(BF)
        expand([kind_ref[parent, k] for k in range(kind_ref.shape[1])])

    g0_ref, w1e_ref, w2e_ref = expanded
    cube = cube_ref[...]
    none = jnp.zeros((half, wide // 2), BF)
    for t in range(terms):
        one = w1e_ref[step, edge * t : edge * (t + 1), :]
        w1 = jnp.concatenate(
            [
                one[half * j : half * (j + 1)] * m1_ref[half * i : half * (i + 1), :]
                for i in range(low)
                for j in range(2)
            ],
            axis=0,
        )
        first = dot(cube, w1).astype(BF)
        moved = jnp.concatenate(
            [
                jnp.concatenate(
                    [
                        first[edge * i : edge * (i + 1), quarter * j : quarter * (j + 1)]
                        for i in range(4)
                    ],
                    axis=1,
                )
                for j in range(4)
            ],
            axis=0,
        )
        w2 = []
        for i in range(4):
            tile = w2e_ref[step, half * (4 * t + i) : half * (4 * t + i + 1), :]
            pair = [tile * m2_ref[half * q : half * (q + 1), :] for q in range(2)]
            w2 += [jnp.concatenate([x, none], axis=1) for x in pair]
            w2 += [jnp.concatenate([none, x], axis=1) for x in pair]
        second = dot(moved, jnp.concatenate(w2, axis=0)).astype(BF)
        for i in range(4):
            sec_ref[i, edge * t : edge * (t + 1), :] = second[edge * i : edge * (i + 1)]
    for i in range(4):
        out = dot(g0_ref[step], sec_ref[i]).astype(BF)
        keep_ref[step, :, wide * i : wide * (i + 1)] = out[:half]
        send_ref[step, :, wide * i : wide * (i + 1)] = out[half:]


def apply_parent(parent, kinds, child_slot, near, far, table, weights, half):
    edge = 2 * half
    wide = edge * half // 2
    terms = table.shape[1] // (3 * edge // 4)
    disps = kinds.shape[1]
    shape = jax.ShapeDtypeStruct((disps, half, 4 * wide), BF)
    scalars = (kinds,) if child_slot is None else (kinds, child_slot)
    arrays = (near, far, table) + tuple(weights)
    expanded = [
        pltpu.VMEM((disps, edge, terms * edge), BF),
        pltpu.VMEM((disps, terms * edge, wide), BF),
        pltpu.VMEM((disps, terms * 2 * edge, wide // 2), BF),
    ]
    return pl.pallas_call(
        functools.partial(
            apply_kernel, half=half, terms=terms, parent=parent, picked=child_slot is not None
        ),
        grid=(disps,),
        in_specs=[pl.BlockSpec(memory_space=pltpu.SMEM)] * len(scalars)
        + [pl.BlockSpec(memory_space=pltpu.VMEM)] * len(arrays),
        out_specs=[pl.BlockSpec(memory_space=pltpu.VMEM)] * 2,
        out_shape=[shape, shape],
        scratch_shapes=[
            pltpu.VMEM((4 * edge, wide), BF),
            pltpu.VMEM((4, terms * edge, wide), BF),
        ]
        + expanded,
        compiler_params=pltpu.CompilerParams(vmem_limit_bytes=24 * 1024 * 1024),
    )(*scalars, *arrays)


def sum_kernel(slot_ref, *refs, rows):
    row_refs, (even_ref, odd_ref, total_ref) = refs[:-3], refs[-3:]
    total_ref[...] = jnp.zeros_like(total_ref)
    for i in range(len(row_refs)):
        for j in range(rows):
            slot = slot_ref[i * rows + j]
            total_ref[slot] = total_ref[slot] + row_refs[i][j].astype(F32)
    count = even_ref.shape[0]
    even_ref[...] = total_ref[:count].astype(BF)
    odd_ref[...] = total_ref[count:].astype(BF)


def sum_rows(slots, arrays, slot_count):
    rows = arrays[0].shape[0]
    tail = arrays[0].shape[1:]
    shape = jax.ShapeDtypeStruct((slot_count // 2,) + tail, BF)
    return pl.pallas_call(
        functools.partial(sum_kernel, rows=rows),
        in_specs=[pl.BlockSpec(memory_space=pltpu.SMEM)]
        + [pl.BlockSpec(memory_space=pltpu.VMEM)] * len(arrays),
        out_specs=[pl.BlockSpec(memory_space=pltpu.VMEM)] * 2,
        out_shape=[shape, shape],
        scratch_shapes=[pltpu.VMEM((slot_count,) + tail, F32)],
        compiler_params=pltpu.CompilerParams(vmem_limit_bytes=24 * 1024 * 1024),
    )(slots, *arrays)


def combine_kernel(*refs, bits, lanes, inputs, last):
    kept, arrived, outs = refs[:inputs], refs[inputs : 2 * inputs], refs[2 * inputs :]
    for i, bit in enumerate(bits):
        source, start = (i, 0) if inputs == len(bits) else (0, lanes * i)
        for r in range(arrived[source].shape[0]):
            total = kept[source][r, :, :, start : start + lanes].astype(F32)
            total = total + arrived[source][r, :, :, start : start + lanes].astype(F32)
            total = total.astype(BF)
            if not last:
                place = (r >> (bit + 1) << bit) | (r & ((1 << bit) - 1))
                outs[2 * i + (r >> bit & 1)][place] = total
            elif outs[0].shape[1] == 4:
                wide = lanes // 2
                half = wide // 16
                order = one_hot(
                    (wide, wide),
                    lambda x: x % (2 * half) // half * (wide // 2) + x // (2 * half) * half + x % half,
                    lambda x: x,
                )
                for n in range(total.shape[0]):
                    for c in range(2):
                        moved = exact(total[n, :, wide * c : wide * (c + 1)], order)
                        to = wide // 2 * c
                        for bit in range(2):
                            outs[0][n, 2 * i + bit, :, to : to + wide // 2] = moved[
                                :, wide // 2 * bit : wide // 2 * (bit + 1)
                            ]
            else:
                outs[0][:, 0, :, lanes * i : lanes * (i + 1)] = total


def combine(kept, arrived, bits, out=None):
    lanes = arrived[0].shape[-1] * len(arrived) // len(bits)
    if out is None:
        shape = (arrived[0].shape[0] // 2,) + arrived[0].shape[1:3] + (lanes,)
        shapes = [shape] * (2 * len(bits))
    else:
        shapes = [out]
    return pl.pallas_call(
        functools.partial(
            combine_kernel, bits=bits, lanes=lanes, inputs=len(kept), last=out is not None
        ),
        in_specs=[pl.BlockSpec(memory_space=pltpu.VMEM)] * (2 * len(kept)),
        out_specs=[pl.BlockSpec(memory_space=pltpu.VMEM)] * len(shapes),
        out_shape=[jax.ShapeDtypeStruct(shape, BF) for shape in shapes],
        compiler_params=pltpu.CompilerParams(vmem_limit_bytes=24 * 1024 * 1024),
    )(*kept, *arrived)


def swap(x, axis, mask):
    count = lax.axis_size(axis)
    return lax.ppermute(x, axis, [(i, i ^ mask) for i in range(count)])


def local(children, child_slot, two_scale, factors, disp_kind, target_leaf, target_node):
    oct_count = lax.axis_size("oct")
    leaf_count = lax.axis_size("leaf")
    my_leaf = lax.axis_index("leaf")
    edge = two_scale.shape[0]
    half = edge // 2
    held = child_slot.shape[1]
    parents, disps = disp_kind.shape
    paired = oct_count == 2

    blocks = children.reshape(-1, half, half * half)
    if paired:
        near = blocks
        near_slot = child_slot.T
        far = swap(pick_blocks(near_slot, blocks, parents), "oct", 1)
    else:
        arrived = lax.all_to_all(
            blocks[child_slot], "oct", split_axis=0, concat_axis=1, tiled=True
        ).reshape(parents, 2, 4, half, half * half)
        near, far = arrived[:, 0], arrived[:, 1]
        near_slot = None

    nodes = 2 * oct_count
    goal = target_leaf.reshape(parents, disps) * nodes + target_node
    if paired:
        goals = jnp.stack([goal, swap(goal, "oct", 1)], axis=1)
    else:
        goals = lax.all_gather(goal, "oct").transpose(1, 0, 2)
    leaf_off = jnp.bitwise_xor(goals // nodes, my_leaf)
    slots = ((leaf_off % 2) * (leaf_count // 2) + leaf_off // 2) * nodes + goals % nodes

    table = factors.reshape(factors.shape[0], -1, 4 * edge)
    weights = make_weights(two_scale, paired)

    arrays = []
    for parent in range(parents):
        kept, sent = apply_parent(
            parent, disp_kind, near_slot, near, far, table, weights, half
        )
        if paired:
            arrays += [kept, swap(sent, "oct", 1)]
        else:
            rows = jnp.stack([kept, sent], axis=1).reshape(disps, 2, half, 2, half, 2, half)
            rows = rows.transpose(1, 3, 5, 0, 2, 4, 6)
            rows = rows.reshape(oct_count, held, disps, half, half * half)
            rows = rows.transpose(0, 2, 1, 3, 4)
            rows = lax.all_to_all(rows, "oct", split_axis=0, concat_axis=0, tiled=True)
            arrays += [rows.reshape(oct_count * disps, held * half, half * half)]

    even, odd = sum_rows(slots.reshape(-1), arrays, leaf_count * nodes)
    shape = (leaf_count // 2, nodes) + even.shape[1:]
    even = even.reshape(shape)
    odd = swap(odd, "leaf", 1).reshape(shape)
    masks = [1 << i for i in range(1, (leaf_count - 1).bit_length())]
    orders = [masks, masks[1::-1] + masks[2:]]
    left = [list(masks), list(masks)]
    kept, arrived = [even], [odd]
    for step in range(len(masks)):
        bits = [left[i].index(orders[i][step]) for i in range(2)]
        parts = combine(kept, arrived, bits)
        kept = [parts[0], parts[2]]
        arrived = [swap(parts[2 * i + 1], "leaf", orders[i][step]) for i in range(2)]
        for i in range(2):
            left[i].remove(orders[i][step])
    tail = (nodes, held, half, half * half) if paired else (nodes, 1) + shape[2:]
    (out,) = combine(kept, arrived, (0, 0), tail)
    return out.reshape(nodes, held, -1)


def solution(mesh):
    placed = (
        P(("leaf", "oct"), None),
        P("leaf", "oct"),
        P(),
        P(),
        P(("leaf", "oct"), None),
        P(("leaf", "oct"), None, None),
        P(("leaf", "oct"), None),
    )
    return jax.shard_map(
        local, mesh=mesh, in_specs=placed, out_specs=P("leaf", "oct", None), check_vma=False
    )
```

```python
import functools

import jax
import jax.numpy as jnp
from jax import lax
from jax.experimental import pallas as pl
from jax.experimental.pallas import tpu as pltpu
from jax.sharding import PartitionSpec as P

BF = jnp.bfloat16
F32 = jnp.float32


def dot(x, y):
    return jnp.dot(x, y, preferred_element_type=F32)


def one_hot(shape, row_of, lane_of):
    rows = lax.broadcasted_iota(jnp.int32, shape, 0)
    lanes = lax.broadcasted_iota(jnp.int32, shape, 1)
    return (row_of(rows) == lane_of(lanes)).astype(BF)


def exact(x, y):
    return dot(x, y).astype(BF)


def weights_kernel(
    scale_ref, s1e_ref, s2e_ref, m1_ref, m2_ref, fw1_ref, fw2_ref, sa_ref, st_ref, *, half, paired
):
    edge = 2 * half
    low = half // 2
    wide = edge * low
    scale = scale_ref[...]
    turn = lax.axis_index("oct") * half if paired else 0

    def same(x):
        return x

    def turned(x):
        return lax.rem(x + turn, edge)

    def chunked(x):
        return (x % low) * 4 + x // low

    by_chunk = exact(one_hot((edge, edge), chunked, same), scale)
    s1e_ref[...] = exact(by_chunk, one_hot((edge, wide), same, lambda x: x // low))
    s2e_ref[...] = exact(by_chunk, one_hot((edge, wide // 2), same, lambda x: x % edge))
    m1_ref[...] = one_hot((low * half, wide), lambda x: x // half, lambda x: x % low)
    m2_ref[...] = one_hot((edge, wide // 2), lambda x: x // low, lambda x: x // edge)
    sa_ref[...] = exact(scale, one_hot((edge, edge), same, turned))
    pick = one_hot((edge, edge), turned, same)
    st_ref[...] = lax.dot_general(
        pick, by_chunk, (((1,), (1,)), ((), ())), preferred_element_type=F32
    ).astype(BF)

    def spread(row_of, lane_of, lane_count):
        rows = lax.dot_general(
            one_hot((wide, edge), row_of, same),
            scale,
            (((1,), (1,)), ((), ())),
            preferred_element_type=F32,
        ).astype(BF)
        return exact(rows, one_hot((edge, lane_count), same, lane_of))

    for bit in range(2):
        fw1_ref[bit] = spread(
            lambda x: x % half + bit * half, lambda x: x // half, 2 * wide
        ) * one_hot((wide, 2 * wide), lambda x: x // half, lambda x: x % half)
    fw2_ref[...] = spread(
        lambda x: x // (wide // 2) * half + x % half, lambda x: x % edge, wide
    ) * one_hot((wide, wide), lambda x: x // half % low, lambda x: x // edge)


def make_weights(two_scale, paired):
    edge = two_scale.shape[0]
    half = edge // 2
    low = half // 2
    wide = edge * low
    shapes = [
        (edge, wide), (edge, wide // 2), (low * half, wide), (edge, wide // 2),
        (2, wide, 2 * wide), (wide, wide), (edge, edge), (edge, edge),
    ]
    return pl.pallas_call(
        functools.partial(weights_kernel, half=half, paired=paired),
        in_specs=[pl.BlockSpec(memory_space=pltpu.VMEM)],
        out_specs=[pl.BlockSpec(memory_space=pltpu.VMEM)] * len(shapes),
        out_shape=[jax.ShapeDtypeStruct(shape, BF) for shape in shapes],
        compiler_params=pltpu.CompilerParams(vmem_limit_bytes=24 * 1024 * 1024),
    )(two_scale)


def pick_kernel(slot_ref, blocks_ref, out_ref, *, parents):
    first = (1 - lax.axis_index("oct")) * parents
    for i in range(parents):
        for j in range(out_ref.shape[1]):
            out_ref[i, j] = blocks_ref[slot_ref[j, first + i]]


def pick_blocks(child_slot, blocks, parents):
    shape = (parents, child_slot.shape[0]) + blocks.shape[1:]
    return pl.pallas_call(
        functools.partial(pick_kernel, parents=parents),
        in_specs=[
            pl.BlockSpec(memory_space=pltpu.SMEM),
            pl.BlockSpec(memory_space=pltpu.VMEM),
        ],
        out_specs=pl.BlockSpec(memory_space=pltpu.VMEM),
        out_shape=jax.ShapeDtypeStruct(shape, BF),
    )(child_slot, blocks)


def by_output(table, edge, terms):
    low = edge // 4
    lanes = 4 * edge
    chunk = lax.broadcasted_iota(jnp.int32, (low, lanes), 1) // edge
    groups = []
    for start in range(0, terms, 4):
        tiles = [
            table[low * min(t, terms - 1) : low * (min(t, terms - 1) + 1)]
            for t in range(start, start + 4)
        ]
        for step in (1, 2):
            upper = (chunk // step) % 2 == 1
            mixed = list(tiles)
            for i in range(4):
                if i & step == 0:
                    mixed[i] = jnp.where(
                        upper, pltpu.roll(tiles[i + step], edge * step, 1), tiles[i]
                    )
                    mixed[i + step] = jnp.where(
                        upper, tiles[i + step], pltpu.roll(tiles[i], lanes - edge * step, 1)
                    )
            tiles = mixed
        groups.append(jnp.concatenate(tiles, axis=0))
    return jnp.concatenate(groups, axis=1)[:, : terms * edge]


def apply_kernel(
    kind_ref, *refs, half, terms, first_parent, picked,
):
    if picked:
        slot_ref, refs = refs[0], refs[1:]
    (
        blocks_ref, far_ref, table_ref, s1e_ref, s2e_ref, m1_ref, m2_ref, fw1_ref, fw2_ref,
        sa_ref, st_ref, keep_ref, send_ref, cube_ref, sec_ref,
    ) = refs[:15]
    expanded = refs[15:]
    edge = 2 * half
    low = half // 2
    wide = edge * low
    quarter = wide // 4
    rows = terms * low
    step = pl.program_id(1)
    parent = first_parent + pl.program_id(0)
    item = pl.program_id(0) * pl.num_programs(1) + step

    def expand(kinds):
        g0_ref, w1e_ref, w2e_ref = expanded
        spread = [
            [
                by_output(
                    table_ref[kind, rows * axis : rows * (axis + 1), :].astype(F32), edge, terms
                ).astype(BF)
                for kind in kinds
            ]
            for axis in range(3)
        ]
        turned = [[x.T for x in spread[axis]] for axis in (1, 2)]
        for k in range(len(kinds)):
            g0_ref[k] = dot(st_ref[...], spread[0][k]).astype(BF)
        for k in range(len(kinds)):
            w1e_ref[k] = dot(turned[0][k], s1e_ref[...]).astype(BF)
        for k in range(len(kinds)):
            once = dot(turned[1][k], s2e_ref[...])
            for i in range(terms * 4):
                tile = once[low * i : low * (i + 1)]
                w2e_ref[k, half * i : half * (i + 1), :] = jnp.concatenate(
                    [tile, tile], axis=0
                ).astype(BF)

    @pl.when(step == 0)
    def _():
        if picked:
            first = lax.axis_index("oct") * far_ref.shape[0] + parent
            near = [blocks_ref[slot_ref[i, first]] for i in range(4)]
        else:
            near = [blocks_ref[parent, i] for i in range(4)]
        total = None
        for bit in range(2):
            parts = []
            for mid in range(2):
                parts += [near[2 * mid + bit], far_ref[parent, 2 * mid + bit]]
            part = dot(jnp.concatenate(parts, axis=0), fw1_ref[bit])
            total = part if total is None else total + part
        total = total.astype(BF)
        lanes = wide // 2
        moved = jnp.concatenate(
            [
                jnp.concatenate(
                    [
                        total[:edge, lanes * i : lanes * (i + 1)],
                        total[edge:, lanes * i : lanes * (i + 1)],
                    ],
                    axis=1,
                )
                for i in range(4)
            ],
            axis=0,
        )
        second = dot(moved, fw2_ref[...]).astype(BF)
        for i in range(4):
            cube_ref[edge * i : edge * (i + 1), :] = dot(
                sa_ref[...], second[edge * i : edge * (i + 1)]
            ).astype(BF)
        expand([kind_ref[parent, k] for k in range(kind_ref.shape[1])])

    g0_ref, w1e_ref, w2e_ref = expanded
    cube = cube_ref[...]
    none = jnp.zeros((half, wide // 2), BF)
    for t in range(terms):
        one = w1e_ref[step, edge * t : edge * (t + 1), :]
        w1 = jnp.concatenate(
            [
                one[half * j : half * (j + 1)] * m1_ref[half * i : half * (i + 1), :]
                for i in range(low)
                for j in range(2)
            ],
            axis=0,
        )
        first = dot(cube, w1).astype(BF)
        moved = jnp.concatenate(
            [
                jnp.concatenate(
                    [
                        first[edge * i : edge * (i + 1), quarter * j : quarter * (j + 1)]
                        for i in range(4)
                    ],
                    axis=1,
                )
                for j in range(4)
            ],
            axis=0,
        )
        w2 = []
        for i in range(4):
            tile = w2e_ref[step, half * (4 * t + i) : half * (4 * t + i + 1), :]
            pair = [tile * m2_ref[half * q : half * (q + 1), :] for q in range(2)]
            w2 += [jnp.concatenate([x, none], axis=1) for x in pair]
            w2 += [jnp.concatenate([none, x], axis=1) for x in pair]
        second = dot(moved, jnp.concatenate(w2, axis=0)).astype(BF)
        for i in range(4):
            sec_ref[i, edge * t : edge * (t + 1), :] = second[edge * i : edge * (i + 1)]
    for i in range(4):
        out = dot(g0_ref[step], sec_ref[i]).astype(BF)
        keep_ref[item, :, wide * i : wide * (i + 1)] = out[:half]
        send_ref[item, :, wide * i : wide * (i + 1)] = out[half:]


def apply_parents(first_parent, count, kinds, child_slot, near, far, table, weights, half):
    edge = 2 * half
    wide = edge * half // 2
    terms = table.shape[1] // (3 * edge // 4)
    disps = kinds.shape[1]
    shape = jax.ShapeDtypeStruct((count * disps, half, 4 * wide), BF)
    scalars = (kinds,) if child_slot is None else (kinds, child_slot)
    arrays = (near, far, table) + tuple(weights)
    expanded = [
        pltpu.VMEM((disps, edge, terms * edge), BF),
        pltpu.VMEM((disps, terms * edge, wide), BF),
        pltpu.VMEM((disps, terms * 2 * edge, wide // 2), BF),
    ]
    return pl.pallas_call(
        functools.partial(
            apply_kernel,
            half=half,
            terms=terms,
            first_parent=first_parent,
            picked=child_slot is not None,
        ),
        grid=(count, disps),
        in_specs=[pl.BlockSpec(memory_space=pltpu.SMEM)] * len(scalars)
        + [pl.BlockSpec(memory_space=pltpu.VMEM)] * len(arrays),
        out_specs=[pl.BlockSpec(memory_space=pltpu.VMEM)] * 2,
        out_shape=[shape, shape],
        scratch_shapes=[
            pltpu.VMEM((4 * edge, wide), BF),
            pltpu.VMEM((4, terms * edge, wide), BF),
        ]
        + expanded,
        compiler_params=pltpu.CompilerParams(vmem_limit_bytes=24 * 1024 * 1024),
    )(*scalars, *arrays)


def target(goal_ref, item, nodes):
    goal = goal_ref[item]
    offset = jnp.bitwise_xor(goal // nodes, lax.axis_index("leaf"))
    return offset % 2, offset // 2 * nodes + goal % nodes


def sum_kernel(goal_ref, *refs, sources, nodes):
    row_refs, (even_ref, odd_ref, total_ref) = refs[:-3], refs[-3:]
    total_ref[...] = jnp.zeros_like(total_ref)
    count = even_ref.shape[0]
    for row_ref, items in zip(row_refs, sources):
        for i, item in enumerate(items):
            parity, slot = target(goal_ref, item, nodes)
            slot = parity * count + slot
            total_ref[slot] = total_ref[slot] + row_ref[i].astype(F32)
    even_ref[...] = total_ref[:count].astype(BF)
    odd_ref[...] = total_ref[count:].astype(BF)


def sum_rows(goals, arrays, sources, nodes, leaf_count):
    tail = arrays[0].shape[1:]
    slot_count = leaf_count * nodes
    shape = jax.ShapeDtypeStruct((slot_count // 2,) + tail, BF)
    return pl.pallas_call(
        functools.partial(sum_kernel, sources=sources, nodes=nodes),
        in_specs=[pl.BlockSpec(memory_space=pltpu.SMEM)]
        + [pl.BlockSpec(memory_space=pltpu.VMEM)] * len(arrays),
        out_specs=[pl.BlockSpec(memory_space=pltpu.VMEM)] * 2,
        out_shape=[shape, shape],
        scratch_shapes=[pltpu.VMEM((slot_count,) + tail, F32)],
        compiler_params=pltpu.CompilerParams(vmem_limit_bytes=24 * 1024 * 1024),
    )(goals, *arrays)


def place(offset, bit):
    return (offset >> (bit + 1) << bit) | (offset & ((1 << bit) - 1))


def first_kernel(even_ref, odd_ref, *outs, bits):
    lanes = outs[0].shape[-1]
    for i, bit in enumerate(bits):
        for r in range(even_ref.shape[0]):
            here = (slice(None), slice(None), slice(lanes * i, lanes * (i + 1)))
            total = even_ref[(r,) + here].astype(F32) + odd_ref[(r,) + here].astype(F32)
            outs[2 * i + (r >> bit & 1)][place(r, bit)] = total.astype(BF)


def first_combine(even, odd, bits):
    offsets, nodes, rows, lanes = even.shape
    shape = jax.ShapeDtypeStruct((offsets // 2, nodes, rows, lanes // 2), BF)
    return pl.pallas_call(
        functools.partial(first_kernel, bits=bits),
        in_specs=[pl.BlockSpec(memory_space=pltpu.VMEM)] * 2,
        out_specs=[pl.BlockSpec(memory_space=pltpu.VMEM)] * 4,
        out_shape=[shape] * 4,
        compiler_params=pltpu.CompilerParams(vmem_limit_bytes=24 * 1024 * 1024),
    )(even, odd)


def combine_kernel(kept_ref, arrived_ref, keep_ref, send_ref, *, bit):
    for r in range(kept_ref.shape[0]):
        total = (kept_ref[r].astype(F32) + arrived_ref[r].astype(F32)).astype(BF)
        out_ref = send_ref if r >> bit & 1 else keep_ref
        out_ref[place(r, bit)] = total


def combine(kept, arrived, bit):
    shape = jax.ShapeDtypeStruct((kept.shape[0] // 2,) + kept.shape[1:], BF)
    return pl.pallas_call(
        functools.partial(combine_kernel, bit=bit),
        in_specs=[pl.BlockSpec(memory_space=pltpu.VMEM)] * 2,
        out_specs=[pl.BlockSpec(memory_space=pltpu.VMEM)] * 2,
        out_shape=[shape, shape],
        compiler_params=pltpu.CompilerParams(vmem_limit_bytes=24 * 1024 * 1024),
    )(kept, arrived)


def last_kernel(kept0_ref, kept1_ref, arrived0_ref, arrived1_ref, out_ref):
    for i, (kept_ref, arrived_ref) in enumerate(
        ((kept0_ref, arrived0_ref), (kept1_ref, arrived1_ref))
    ):
        lanes = kept_ref.shape[-1]
        total = (kept_ref[0].astype(F32) + arrived_ref[0].astype(F32)).astype(BF)
        if out_ref.shape[1] != 4:
            out_ref[:, 0, :, lanes * i : lanes * (i + 1)] = total
            continue
        wide = lanes // 2
        half = wide // 16
        order = one_hot(
            (wide, wide),
            lambda x: x % (2 * half) // half * (wide // 2) + x // (2 * half) * half + x % half,
            lambda x: x,
        )
        for n in range(total.shape[0]):
            for c in range(2):
                moved = exact(total[n, :, wide * c : wide * (c + 1)], order)
                to = wide // 2 * c
                for bit in range(2):
                    out_ref[n, 2 * i + bit, :, to : to + wide // 2] = moved[
                        :, wide // 2 * bit : wide // 2 * (bit + 1)
                    ]


def last_combine(kept, arrived, shape):
    return pl.pallas_call(
        last_kernel,
        in_specs=[pl.BlockSpec(memory_space=pltpu.VMEM)] * 4,
        out_specs=pl.BlockSpec(memory_space=pltpu.VMEM),
        out_shape=jax.ShapeDtypeStruct(shape, BF),
        compiler_params=pltpu.CompilerParams(vmem_limit_bytes=24 * 1024 * 1024),
    )(*kept, *arrived)


def swap(x, axis, mask):
    count = lax.axis_size(axis)
    return lax.ppermute(x, axis, [(i, i ^ mask) for i in range(count)])


def local(children, child_slot, two_scale, factors, disp_kind, target_leaf, target_node):
    oct_count = lax.axis_size("oct")
    leaf_count = lax.axis_size("leaf")
    edge = two_scale.shape[0]
    half = edge // 2
    held = child_slot.shape[1]
    parents, disps = disp_kind.shape
    paired = oct_count == 2

    blocks = children.reshape(-1, half, half * half)
    if paired:
        near = blocks
        near_slot = child_slot.T
        far = swap(pick_blocks(near_slot, blocks, parents), "oct", 1)
    else:
        arrived = lax.all_to_all(
            blocks[child_slot], "oct", split_axis=0, concat_axis=1, tiled=True
        ).reshape(parents, 2, 4, half, half * half)
        near, far = arrived[:, 0], arrived[:, 1]
        near_slot = None

    table = factors.reshape(factors.shape[0], -1, 4 * edge)
    weights = make_weights(two_scale, paired)

    arrays, sources = [], []
    done, counts = 0, [max(1, parents - 2)] + [1] * min(2, parents - 1)
    for count in counts:
        kept, sent = apply_parents(
            done, count, disp_kind, near_slot, near, far, table, weights, half
        )
        if done == 0:
            target_leaf, target_node, kept = lax.optimization_barrier(
                (target_leaf, target_node, kept)
            )
            nodes = 2 * oct_count
            goal = (target_leaf.reshape(parents, disps) * nodes + target_node).reshape(-1)
            if paired:
                goals = jnp.concatenate([goal, swap(goal, "oct", 1)])
            else:
                goals = lax.all_gather(goal, "oct", tiled=True)
        items = [done * disps + i for i in range(count * disps)]
        if paired:
            arrays += [kept, swap(sent, "oct", 1)]
            sources += [items, [goal.size + item for item in items]]
        else:
            rows = jnp.stack([kept, sent], axis=1).reshape(-1, 2, half, 2, half, 2, half)
            rows = rows.transpose(1, 3, 5, 0, 2, 4, 6)
            rows = rows.reshape(oct_count, held, -1, half, half * half)
            rows = rows.transpose(0, 2, 1, 3, 4)
            rows = lax.all_to_all(rows, "oct", split_axis=0, concat_axis=0, tiled=True)
            arrays += [rows.reshape(-1, held * half, half * half)]
            sources += [[goal.size * o + item for o in range(oct_count) for item in items]]
        done += count

    even, odd = sum_rows(goals, arrays, sources, nodes, leaf_count)
    shape = (leaf_count // 2, nodes) + even.shape[1:]
    even = even.reshape(shape)
    odd = swap(odd, "leaf", 1).reshape(shape)
    masks = [1 << i for i in range(1, (leaf_count - 1).bit_length())]
    orders = [masks[1::-1] + masks[2:], masks]
    parts = first_combine(even, odd, [masks.index(order[0]) for order in orders])
    kept, arrived = [], []
    for i in range(2):
        left = list(masks)
        left.remove(orders[i][0])
        keep, come = parts[2 * i], swap(parts[2 * i + 1], "leaf", orders[i][0])
        for mask in orders[i][1:]:
            keep, send = combine(keep, come, left.index(mask))
            left.remove(mask)
            come = swap(send, "leaf", mask)
        kept.append(keep)
        arrived.append(come)
    if paired:
        shape = (nodes, held, half, half * half)
    else:
        shape = (nodes, 1) + shape[2:]
    return last_combine(kept, arrived, shape).reshape(nodes, held, -1)


def solution(mesh):
    placed = (
        P(("leaf", "oct"), None),
        P("leaf", "oct"),
        P(),
        P(),
        P(("leaf", "oct"), None),
        P(("leaf", "oct"), None, None),
        P(("leaf", "oct"), None),
    )
    return jax.shard_map(
        local, mesh=mesh, in_specs=placed, out_specs=P("leaf", "oct", None), check_vma=False
    )
```

```python
import functools
import math

import jax
import jax.numpy as jnp
from jax import lax
from jax.experimental import pallas as pl
from jax.experimental.pallas import tpu as pltpu
from jax.sharding import PartitionSpec as P

BF = jnp.bfloat16
F32 = jnp.float32


def dot(x, y):
    return jnp.dot(x, y, preferred_element_type=F32)


def one_hot(shape, row_of, lane_of):
    rows = lax.broadcasted_iota(jnp.int32, shape, 0)
    lanes = lax.broadcasted_iota(jnp.int32, shape, 1)
    return (row_of(rows) == lane_of(lanes)).astype(BF)


def exact(x, y):
    return dot(x, y).astype(BF)


def weights_kernel(
    scale_ref, s1e_ref, s2e_ref, m1_ref, m2_ref, fw1_ref, fw2_ref, sa_ref, st_ref, *, half, paired
):
    edge = 2 * half
    low = half // 2
    wide = edge * low
    scale = scale_ref[...]
    turn = lax.axis_index("oct") * half if paired else 0

    def same(x):
        return x

    def turned(x):
        return lax.rem(x + turn, edge)

    def chunked(x):
        return (x % low) * 4 + x // low

    by_chunk = exact(one_hot((edge, edge), chunked, same), scale)
    s1e_ref[...] = exact(by_chunk, one_hot((edge, wide), same, lambda x: x // low))
    s2e_ref[...] = exact(by_chunk, one_hot((edge, wide // 2), same, lambda x: x % edge))
    m1_ref[...] = one_hot((low * half, wide), lambda x: x // half, lambda x: x % low)
    m2_ref[...] = one_hot((edge, wide // 2), lambda x: x // low, lambda x: x // edge)
    sa_ref[...] = exact(scale, one_hot((edge, edge), same, turned))
    pick = one_hot((edge, edge), turned, same)
    st_ref[...] = lax.dot_general(
        pick, by_chunk, (((1,), (1,)), ((), ())), preferred_element_type=F32
    ).astype(BF)

    def spread(row_of, lane_of, lane_count):
        rows = lax.dot_general(
            one_hot((wide, edge), row_of, same),
            scale,
            (((1,), (1,)), ((), ())),
            preferred_element_type=F32,
        ).astype(BF)
        return exact(rows, one_hot((edge, lane_count), same, lane_of))

    for bit in range(2):
        fw1_ref[bit] = spread(
            lambda x: x % half + bit * half, lambda x: x // half, 2 * wide
        ) * one_hot((wide, 2 * wide), lambda x: x // half, lambda x: x % half)
    fw2_ref[...] = spread(
        lambda x: x // (wide // 2) * half + x % half, lambda x: x % edge, wide
    ) * one_hot((wide, wide), lambda x: x // half % low, lambda x: x // edge)


def make_weights(two_scale, paired):
    edge = two_scale.shape[0]
    half = edge // 2
    low = half // 2
    wide = edge * low
    shapes = [
        (edge, wide), (edge, wide // 2), (low * half, wide), (edge, wide // 2),
        (2, wide, 2 * wide), (wide, wide), (edge, edge), (edge, edge),
    ]
    return pl.pallas_call(
        functools.partial(weights_kernel, half=half, paired=paired),
        in_specs=[pl.BlockSpec(memory_space=pltpu.VMEM)],
        out_specs=[pl.BlockSpec(memory_space=pltpu.VMEM)] * len(shapes),
        out_shape=[jax.ShapeDtypeStruct(shape, BF) for shape in shapes],
        compiler_params=pltpu.CompilerParams(vmem_limit_bytes=24 * 1024 * 1024),
    )(two_scale)


def pick_kernel(slot_ref, children_ref, near_ref, send_ref, wide_ref):
    blocks, size = children_ref.shape
    groups = size // 128
    for v in range(groups):
        wide_ref[blocks * v : blocks * (v + 1), :] = children_ref[
            :, 128 * v : 128 * (v + 1)
        ].astype(F32)
    parents, held, rows, lanes = near_ref.shape
    across = lanes // 128
    mine = lax.axis_index("oct")
    for out_ref, owner in ((send_ref, 1 - mine), (near_ref, mine)):
        for i in range(parents):
            for j in range(held):
                slot = slot_ref[j, owner * parents + i]
                for h in range(across):
                    out_ref[i, j, :, 128 * h : 128 * (h + 1)] = wide_ref[
                        pl.ds(blocks * h + slot, rows, stride=blocks * across), :
                    ].astype(BF)


def pick_blocks(child_slot, children, parents, half):
    shape = jax.ShapeDtypeStruct((parents, child_slot.shape[0], half, half * half), BF)
    return pl.pallas_call(
        pick_kernel,
        in_specs=[
            pl.BlockSpec(memory_space=pltpu.SMEM),
            pl.BlockSpec(memory_space=pltpu.VMEM),
        ],
        out_specs=[pl.BlockSpec(memory_space=pltpu.VMEM)] * 2,
        out_shape=[shape, shape],
        scratch_shapes=[pltpu.VMEM((children.size // 128, 128), F32)],
        compiler_params=pltpu.CompilerParams(vmem_limit_bytes=16 * 1024 * 1024),
    )(child_slot, children)


def by_output(table, edge, terms):
    low = edge // 4
    lanes = 4 * edge
    chunk = lax.broadcasted_iota(jnp.int32, (low, lanes), 1) // edge
    groups = []
    for start in range(0, terms, 4):
        tiles = [
            table[low * min(t, terms - 1) : low * (min(t, terms - 1) + 1)]
            for t in range(start, start + 4)
        ]
        for step in (1, 2):
            upper = (chunk // step) % 2 == 1
            mixed = list(tiles)
            for i in range(4):
                if i & step == 0:
                    mixed[i] = jnp.where(
                        upper, pltpu.roll(tiles[i + step], edge * step, 1), tiles[i]
                    )
                    mixed[i + step] = jnp.where(
                        upper, tiles[i + step], pltpu.roll(tiles[i], lanes - edge * step, 1)
                    )
            tiles = mixed
        groups.append(jnp.concatenate(tiles, axis=0))
    return jnp.concatenate(groups, axis=1)[:, : terms * edge]


def apply_kernel(
    kind_ref, *refs, half, terms, first_parent,
):
    (
        near_ref, far_ref, table_ref, s1e_ref, s2e_ref, m1_ref, m2_ref, fw1_ref, fw2_ref,
        sa_ref, st_ref, keep_ref, send_ref, cube_ref, sec_ref,
    ) = refs[:15]
    g0_ref, w1e_ref, w2e_ref = refs[15:]
    edge = 2 * half
    low = half // 2
    wide = edge * low
    quarter = wide // 4
    rows = terms * low
    parent = first_parent + pl.program_id(0)
    disps = kind_ref.shape[1]

    def expand(entries):
        kinds = [kind_ref[parent, k] for k in entries]
        spread = [
            [
                by_output(
                    table_ref[kind, rows * axis : rows * (axis + 1), :].astype(F32), edge, terms
                ).astype(BF)
                for kind in kinds
            ]
            for axis in range(3)
        ]
        turned = [[x.T for x in spread[axis]] for axis in (1, 2)]
        for k, x in zip(entries, spread[0]):
            g0_ref[k] = dot(st_ref[...], x).astype(BF)
        for k, x in zip(entries, turned[0]):
            w1e_ref[k] = dot(x, s1e_ref[...]).astype(BF)
        for k, x in zip(entries, turned[1]):
            once = dot(x, s2e_ref[...])
            for i in range(terms * 4):
                tile = once[low * i : low * (i + 1)]
                w2e_ref[k, half * i : half * (i + 1), :] = jnp.concatenate(
                    [tile, tile], axis=0
                ).astype(BF)

    def filtered():
        total = None
        for bit in range(2):
            parts = []
            for mid in range(2):
                parts += [near_ref[parent, 2 * mid + bit], far_ref[parent, 2 * mid + bit]]
            part = dot(jnp.concatenate(parts, axis=0), fw1_ref[bit])
            total = part if total is None else total + part
        total = total.astype(BF)
        lanes = wide // 2
        moved = jnp.concatenate(
            [
                jnp.concatenate(
                    [
                        total[:edge, lanes * i : lanes * (i + 1)],
                        total[edge:, lanes * i : lanes * (i + 1)],
                    ],
                    axis=1,
                )
                for i in range(4)
            ],
            axis=0,
        )
        second = dot(moved, fw2_ref[...]).astype(BF)
        return jnp.concatenate(
            [
                dot(sa_ref[...], second[edge * i : edge * (i + 1)]).astype(BF)
                for i in range(4)
            ],
            axis=0,
        )

    def products(k):
        cube = cube_ref[...]
        none = jnp.zeros((half, wide // 2), BF)
        for t in range(terms):
            one = w1e_ref[k, edge * t : edge * (t + 1), :]
            w1 = jnp.concatenate(
                [
                    one[half * j : half * (j + 1)] * m1_ref[half * i : half * (i + 1), :]
                    for i in range(low)
                    for j in range(2)
                ],
                axis=0,
            )
            first = dot(cube, w1).astype(BF)
            moved = jnp.concatenate(
                [
                    jnp.concatenate(
                        [
                            first[edge * i : edge * (i + 1), quarter * j : quarter * (j + 1)]
                            for i in range(4)
                        ],
                        axis=1,
                    )
                    for j in range(4)
                ],
                axis=0,
            )
            w2 = []
            for i in range(4):
                tile = w2e_ref[k, half * (4 * t + i) : half * (4 * t + i + 1), :]
                pair = [tile * m2_ref[half * q : half * (q + 1), :] for q in range(2)]
                w2 += [jnp.concatenate([x, none], axis=1) for x in pair]
                w2 += [jnp.concatenate([none, x], axis=1) for x in pair]
            second = dot(moved, jnp.concatenate(w2, axis=0)).astype(BF)
            for i in range(4):
                sec_ref[k, i, edge * t : edge * (t + 1), :] = second[edge * i : edge * (i + 1)]

    def finish(k):
        item = pl.program_id(0) * disps + k
        for i in range(4):
            out = dot(g0_ref[k], sec_ref[k, i]).astype(BF)
            keep_ref[item, :, wide * i : wide * (i + 1)] = out[:half]
            send_ref[item, :, wide * i : wide * (i + 1)] = out[half:]

    cube_ref[...] = filtered()
    expand(range(disps))
    for k in range(disps):
        products(k)
    for k in range(disps):
        finish(k)


def apply_parents(first_parent, count, kinds, near, far, table, weights, half):
    edge = 2 * half
    wide = edge * half // 2
    terms = table.shape[1] // (3 * edge // 4)
    disps = kinds.shape[1]
    shape = jax.ShapeDtypeStruct((count * disps, half, 4 * wide), BF)
    arrays = (near, far, table) + tuple(weights)
    expanded = [
        pltpu.VMEM((disps, edge, terms * edge), BF),
        pltpu.VMEM((disps, terms * edge, wide), BF),
        pltpu.VMEM((disps, terms * 2 * edge, wide // 2), BF),
    ]
    return pl.pallas_call(
        functools.partial(
            apply_kernel,
            half=half,
            terms=terms,
            first_parent=first_parent,
        ),
        grid=(count,),
        in_specs=[pl.BlockSpec(memory_space=pltpu.SMEM)]
        + [pl.BlockSpec(memory_space=pltpu.VMEM)] * len(arrays),
        out_specs=[pl.BlockSpec(memory_space=pltpu.VMEM)] * 2,
        out_shape=[shape, shape],
        scratch_shapes=[
            pltpu.VMEM((4 * edge, wide), BF),
            pltpu.VMEM((disps, 4, terms * edge, wide), BF),
        ]
        + expanded,
        compiler_params=pltpu.CompilerParams(vmem_limit_bytes=24 * 1024 * 1024),
    )(kinds, *arrays)


def target(goal_ref, item, nodes):
    goal = goal_ref[item]
    offset = jnp.bitwise_xor(goal // nodes, lax.axis_index("leaf"))
    return offset % 2, offset // 2 * nodes + goal % nodes


def sum_kernel(goal_ref, *refs, sources, nodes):
    row_refs, (even_ref, odd_ref, total_ref) = refs[:-3], refs[-3:]
    total_ref[...] = jnp.zeros_like(total_ref)
    count = even_ref.shape[0]
    for row_ref, items in zip(row_refs, sources):
        for i, item in enumerate(items):
            parity, slot = target(goal_ref, item, nodes)
            slot = parity * count + slot
            total_ref[slot] = total_ref[slot] + row_ref[i].astype(F32)
    even_ref[...] = total_ref[:count].astype(BF)
    odd_ref[...] = total_ref[count:].astype(BF)


def sum_rows(goals, arrays, sources, nodes, leaf_count):
    tail = arrays[0].shape[1:]
    slot_count = leaf_count * nodes
    shape = jax.ShapeDtypeStruct((slot_count // 2,) + tail, BF)
    return pl.pallas_call(
        functools.partial(sum_kernel, sources=sources, nodes=nodes),
        in_specs=[pl.BlockSpec(memory_space=pltpu.SMEM)]
        + [pl.BlockSpec(memory_space=pltpu.VMEM)] * len(arrays),
        out_specs=[pl.BlockSpec(memory_space=pltpu.VMEM)] * 2,
        out_shape=[shape, shape],
        scratch_shapes=[pltpu.VMEM((slot_count,) + tail, F32)],
        compiler_params=pltpu.CompilerParams(vmem_limit_bytes=24 * 1024 * 1024),
    )(goals, *arrays)


def place(offset, bit):
    return (offset >> (bit + 1) << bit) | (offset & ((1 << bit) - 1))


def first_kernel(even_ref, odd_ref, *outs, bits):
    lanes = outs[0].shape[-1]
    for i, bit in enumerate(bits):
        for r in range(even_ref.shape[0]):
            here = (slice(None), slice(None), slice(lanes * i, lanes * (i + 1)))
            total = even_ref[(r,) + here].astype(F32) + odd_ref[(r,) + here].astype(F32)
            outs[2 * i + (r >> bit & 1)][place(r, bit)] = total.astype(BF)


def first_combine(even, odd, bits):
    offsets, nodes, rows, lanes = even.shape
    shape = jax.ShapeDtypeStruct((offsets // 2, nodes, rows, lanes // 2), BF)
    return pl.pallas_call(
        functools.partial(first_kernel, bits=bits),
        in_specs=[pl.BlockSpec(memory_space=pltpu.VMEM)] * 2,
        out_specs=[pl.BlockSpec(memory_space=pltpu.VMEM)] * 4,
        out_shape=[shape] * 4,
        compiler_params=pltpu.CompilerParams(vmem_limit_bytes=24 * 1024 * 1024),
    )(even, odd)


def combine_kernel(kept_ref, arrived_ref, keep_ref, send_ref, *, bit):
    for r in range(kept_ref.shape[0]):
        total = (kept_ref[r].astype(F32) + arrived_ref[r].astype(F32)).astype(BF)
        out_ref = send_ref if r >> bit & 1 else keep_ref
        out_ref[place(r, bit)] = total


def combine(kept, arrived, bit):
    shape = jax.ShapeDtypeStruct((kept.shape[0] // 2,) + kept.shape[1:], BF)
    return pl.pallas_call(
        functools.partial(combine_kernel, bit=bit),
        in_specs=[pl.BlockSpec(memory_space=pltpu.VMEM)] * 2,
        out_specs=[pl.BlockSpec(memory_space=pltpu.VMEM)] * 2,
        out_shape=[shape, shape],
        compiler_params=pltpu.CompilerParams(vmem_limit_bytes=24 * 1024 * 1024),
    )(kept, arrived)


def last_kernel(kept0_ref, kept1_ref, arrived0_ref, arrived1_ref, out_ref, wide_ref):
    nodes, octants, size = out_ref.shape
    groups = size // 128
    rows, lanes = kept0_ref.shape[2:]

    def store(total, n, first, step):
        wide_ref[pl.ds(n * octants * groups + first, rows, stride=step), :] = total[
            rows * n : rows * (n + 1)
        ]

    for i, (kept_ref, arrived_ref) in enumerate(
        ((kept0_ref, arrived0_ref), (kept1_ref, arrived1_ref))
    ):
        total = kept_ref[0].astype(F32) + arrived_ref[0].astype(F32)
        total = total.reshape(nodes * rows, lanes)
        if octants == 4:
            wide = lanes // 2
            half = wide // 16
            order = one_hot(
                (wide, wide),
                lambda x: x % (2 * half) // half * (wide // 2) + x // (2 * half) * half + x % half,
                lambda x: x,
            )
            for c in range(2):
                moved = dot(total[:, wide * c : wide * (c + 1)].astype(BF), order)
                for bit in range(2):
                    part = moved[:, wide // 2 * bit : wide // 2 * (bit + 1)]
                    for n in range(nodes):
                        store(part, n, (2 * i + bit) * groups + c, 2)
        else:
            for h in range(lanes // 128):
                part = total[:, 128 * h : 128 * (h + 1)]
                for n in range(nodes):
                    store(part, n, i * (lanes // 128) + h, lanes // 64)
    for n in range(nodes):
        for v in range(groups):
            out_ref[n, :, 128 * v : 128 * (v + 1)] = wide_ref[
                pl.ds(n * octants * groups + v, octants, stride=groups), :
            ].astype(BF)


def last_combine(kept, arrived, shape):
    return pl.pallas_call(
        last_kernel,
        in_specs=[pl.BlockSpec(memory_space=pltpu.VMEM)] * 4,
        out_specs=pl.BlockSpec(memory_space=pltpu.VMEM),
        out_shape=jax.ShapeDtypeStruct(shape, BF),
        scratch_shapes=[pltpu.VMEM((math.prod(shape) // 128, 128), F32)],
        compiler_params=pltpu.CompilerParams(vmem_limit_bytes=24 * 1024 * 1024),
    )(*kept, *arrived)


def swap(x, axis, mask):
    count = lax.axis_size(axis)
    return lax.ppermute(x, axis, [(i, i ^ mask) for i in range(count)])


def local(children, child_slot, two_scale, factors, disp_kind, target_leaf, target_node):
    oct_count = lax.axis_size("oct")
    leaf_count = lax.axis_size("leaf")
    edge = two_scale.shape[0]
    half = edge // 2
    held = child_slot.shape[1]
    parents, disps = disp_kind.shape
    paired = oct_count == 2

    if paired:
        near, sent = pick_blocks(child_slot.T, children, parents, half)
        far = swap(sent, "oct", 1)
    else:
        blocks = children.reshape(-1, half, half * half)
        arrived = lax.all_to_all(
            blocks[child_slot], "oct", split_axis=0, concat_axis=1, tiled=True
        ).reshape(parents, 2, 4, half, half * half)
        near, far = arrived[:, 0], arrived[:, 1]

    table = factors.reshape(factors.shape[0], -1, 4 * edge)
    weights = make_weights(two_scale, paired)

    arrays, sources = [], []
    done, counts = 0, [max(1, parents - 2)] + [1] * min(2, parents - 1)
    for count in counts:
        kept, sent = apply_parents(
            done, count, disp_kind, near, far, table, weights, half
        )
        if done == 0:
            target_leaf, target_node, kept = lax.optimization_barrier(
                (target_leaf, target_node, kept)
            )
            nodes = 2 * oct_count
            goal = (target_leaf.reshape(parents, disps) * nodes + target_node).reshape(-1)
            if paired:
                goals = jnp.concatenate([goal, swap(goal, "oct", 1)])
            else:
                goals = lax.all_gather(goal, "oct", tiled=True)
        items = [done * disps + i for i in range(count * disps)]
        if paired:
            arrays += [kept, swap(sent, "oct", 1)]
            sources += [items, [goal.size + item for item in items]]
        else:
            rows = jnp.stack([kept, sent], axis=1).reshape(-1, 2, half, 2, half, 2, half)
            rows = rows.transpose(1, 3, 5, 0, 2, 4, 6)
            rows = rows.reshape(oct_count, held, -1, half, half * half)
            rows = rows.transpose(0, 2, 1, 3, 4)
            rows = lax.all_to_all(rows, "oct", split_axis=0, concat_axis=0, tiled=True)
            arrays += [rows.reshape(-1, held * half, half * half)]
            sources += [[goal.size * o + item for o in range(oct_count) for item in items]]
        done += count

    even, odd = sum_rows(goals, arrays, sources, nodes, leaf_count)
    shape = (leaf_count // 2, nodes) + even.shape[1:]
    even = even.reshape(shape)
    odd = swap(odd, "leaf", 1).reshape(shape)
    masks = [1 << i for i in range(1, (leaf_count - 1).bit_length())]
    orders = [masks[1::-1] + masks[2:], masks]
    parts = first_combine(even, odd, [masks.index(order[0]) for order in orders])
    kept, arrived = [], []
    for i in range(2):
        left = list(masks)
        left.remove(orders[i][0])
        keep, come = parts[2 * i], swap(parts[2 * i + 1], "leaf", orders[i][0])
        for mask in orders[i][1:]:
            keep, send = combine(keep, come, left.index(mask))
            left.remove(mask)
            come = swap(send, "leaf", mask)
        kept.append(keep)
        arrived.append(come)
    return last_combine(kept, arrived, (nodes, held, half * half * half))


def solution(mesh):
    placed = (
        P(("leaf", "oct"), None),
        P("leaf", "oct"),
        P(),
        P(),
        P(("leaf", "oct"), None),
        P(("leaf", "oct"), None, None),
        P(("leaf", "oct"), None),
    )
    return jax.shard_map(
        local, mesh=mesh, in_specs=placed, out_specs=P("leaf", "oct", None), check_vma=False
    )
```

```python
import functools
import math

import jax
import jax.numpy as jnp
from jax import lax
from jax.experimental import pallas as pl
from jax.experimental.pallas import tpu as pltpu
from jax.sharding import PartitionSpec as P

BF = jnp.bfloat16
F32 = jnp.float32


def dot(x, y):
    return jnp.dot(x, y, preferred_element_type=F32)


def one_hot(shape, row_of, lane_of):
    rows = lax.broadcasted_iota(jnp.int32, shape, 0)
    lanes = lax.broadcasted_iota(jnp.int32, shape, 1)
    return (row_of(rows) == lane_of(lanes)).astype(BF)


def exact(x, y):
    return dot(x, y).astype(BF)


def weights_kernel(
    scale_ref, s1e_ref, s2e_ref, m1_ref, m2_ref, fw1_ref, fw2_ref, sa_ref, st_ref, *, half, paired
):
    edge = 2 * half
    low = half // 2
    wide = edge * low
    scale = scale_ref[...]
    turn = lax.axis_index("oct") * half if paired else 0

    def same(x):
        return x

    def turned(x):
        return lax.rem(x + turn, edge)

    def chunked(x):
        return (x % low) * 4 + x // low

    by_chunk = exact(one_hot((edge, edge), chunked, same), scale)
    s1e_ref[...] = exact(by_chunk, one_hot((edge, wide), same, lambda x: x // low))
    s2e_ref[...] = exact(by_chunk, one_hot((edge, wide // 2), same, lambda x: x % edge))
    m1_ref[...] = one_hot((low * half, wide), lambda x: x // half, lambda x: x % low)
    m2_ref[...] = one_hot((edge, wide // 2), lambda x: x // low, lambda x: x // edge)
    sa_ref[...] = exact(scale, one_hot((edge, edge), same, turned))
    pick = one_hot((edge, edge), turned, same)
    st_ref[...] = lax.dot_general(
        pick, by_chunk, (((1,), (1,)), ((), ())), preferred_element_type=F32
    ).astype(BF)

    def spread(row_of, lane_of, lane_count):
        rows = lax.dot_general(
            one_hot((wide, edge), row_of, same),
            scale,
            (((1,), (1,)), ((), ())),
            preferred_element_type=F32,
        ).astype(BF)
        return exact(rows, one_hot((edge, lane_count), same, lane_of))

    for bit in range(2):
        fw1_ref[bit] = spread(
            lambda x: x % half + bit * half, lambda x: x // half, 2 * wide
        ) * one_hot((wide, 2 * wide), lambda x: x // half, lambda x: x % half)
    fw2_ref[...] = spread(
        lambda x: x // (wide // 2) * half + x % half, lambda x: x % edge, wide
    ) * one_hot((wide, wide), lambda x: x // half % low, lambda x: x // edge)


def make_weights(two_scale, paired):
    edge = two_scale.shape[0]
    half = edge // 2
    low = half // 2
    wide = edge * low
    shapes = [
        (edge, wide), (edge, wide // 2), (low * half, wide), (edge, wide // 2),
        (2, wide, 2 * wide), (wide, wide), (edge, edge), (edge, edge),
    ]
    return pl.pallas_call(
        functools.partial(weights_kernel, half=half, paired=paired),
        in_specs=[pl.BlockSpec(memory_space=pltpu.VMEM)],
        out_specs=[pl.BlockSpec(memory_space=pltpu.VMEM)] * len(shapes),
        out_shape=[jax.ShapeDtypeStruct(shape, BF) for shape in shapes],
        compiler_params=pltpu.CompilerParams(vmem_limit_bytes=24 * 1024 * 1024),
    )(two_scale)


def pick_kernel(slot_ref, children_ref, near_ref, send_ref, wide_ref):
    blocks, size = children_ref.shape
    groups = size // 128
    for v in range(groups):
        wide_ref[blocks * v : blocks * (v + 1), :] = children_ref[
            :, 128 * v : 128 * (v + 1)
        ].astype(F32)
    parents, held, rows, lanes = near_ref.shape
    across = lanes // 128
    mine = lax.axis_index("oct")
    for out_ref, owner in ((send_ref, 1 - mine), (near_ref, mine)):
        for i in range(parents):
            for j in range(held):
                slot = slot_ref[j, owner * parents + i]
                for h in range(across):
                    out_ref[i, j, :, 128 * h : 128 * (h + 1)] = wide_ref[
                        pl.ds(blocks * h + slot, rows, stride=blocks * across), :
                    ].astype(BF)


def pick_blocks(child_slot, children, parents, half):
    shape = jax.ShapeDtypeStruct((parents, child_slot.shape[0], half, half * half), BF)
    return pl.pallas_call(
        pick_kernel,
        in_specs=[
            pl.BlockSpec(memory_space=pltpu.SMEM),
            pl.BlockSpec(memory_space=pltpu.VMEM),
        ],
        out_specs=[pl.BlockSpec(memory_space=pltpu.VMEM)] * 2,
        out_shape=[shape, shape],
        scratch_shapes=[pltpu.VMEM((children.size // 128 + 2 * children.shape[0], 128), F32)],
        compiler_params=pltpu.CompilerParams(vmem_limit_bytes=60 * 1024 * 1024),
    )(child_slot, children)


def by_output(table, edge, terms):
    low = edge // 4
    lanes = 4 * edge
    chunk = lax.broadcasted_iota(jnp.int32, (low, lanes), 1) // edge
    groups = []
    for start in range(0, terms, 4):
        tiles = [
            table[low * min(t, terms - 1) : low * (min(t, terms - 1) + 1)]
            for t in range(start, start + 4)
        ]
        for step in (1, 2):
            upper = (chunk // step) % 2 == 1
            mixed = list(tiles)
            for i in range(4):
                if i & step == 0:
                    mixed[i] = jnp.where(
                        upper, pltpu.roll(tiles[i + step], edge * step, 1), tiles[i]
                    )
                    mixed[i + step] = jnp.where(
                        upper, tiles[i + step], pltpu.roll(tiles[i], lanes - edge * step, 1)
                    )
            tiles = mixed
        groups.append(jnp.concatenate(tiles, axis=0))
    return jnp.concatenate(groups, axis=1)[:, : terms * edge]


def apply_kernel(
    kind_ref, *refs, half, terms, first_parent,
):
    (
        near_ref, far_ref, table_ref, s1e_ref, s2e_ref, m1_ref, m2_ref, fw1_ref, fw2_ref,
        sa_ref, st_ref, keep_ref, send_ref, cube_ref, sec_ref,
    ) = refs[:15]
    g0_ref, w1e_ref, w2e_ref = refs[15:]
    edge = 2 * half
    low = half // 2
    wide = edge * low
    quarter = wide // 4
    rows = terms * low
    disps = kind_ref.shape[1]
    count = keep_ref.shape[0] // disps

    def expand(entries):
        kinds = [kind_ref[first_parent + k // disps, k % disps] for k in entries]
        spread = [
            [
                by_output(
                    table_ref[kind, rows * axis : rows * (axis + 1), :].astype(F32), edge, terms
                ).astype(BF)
                for kind in kinds
            ]
            for axis in range(3)
        ]
        turned = [[x.T for x in spread[axis]] for axis in (1, 2)]
        for k, x in zip(entries, spread[0]):
            g0_ref[k] = dot(st_ref[...], x).astype(BF)
        for k, x in zip(entries, turned[0]):
            w1e_ref[k] = dot(x, s1e_ref[...]).astype(BF)
        for k, x in zip(entries, turned[1]):
            once = dot(x, s2e_ref[...])
            for i in range(terms * 4):
                tile = once[low * i : low * (i + 1)]
                w2e_ref[k, half * i : half * (i + 1), :] = jnp.concatenate(
                    [tile, tile], axis=0
                ).astype(BF)

    def filtered(parent):
        total = None
        for bit in range(2):
            parts = []
            for mid in range(2):
                parts += [near_ref[parent, 2 * mid + bit], far_ref[parent, 2 * mid + bit]]
            part = dot(jnp.concatenate(parts, axis=0), fw1_ref[bit])
            total = part if total is None else total + part
        total = total.astype(BF)
        lanes = wide // 2
        moved = jnp.concatenate(
            [
                jnp.concatenate(
                    [
                        total[:edge, lanes * i : lanes * (i + 1)],
                        total[edge:, lanes * i : lanes * (i + 1)],
                    ],
                    axis=1,
                )
                for i in range(4)
            ],
            axis=0,
        )
        second = dot(moved, fw2_ref[...]).astype(BF)
        return jnp.concatenate(
            [
                dot(sa_ref[...], second[edge * i : edge * (i + 1)]).astype(BF)
                for i in range(4)
            ],
            axis=0,
        )

    def products(k):
        cube = cube_ref[k // disps]
        none = jnp.zeros((half, wide // 2), BF)
        for t in range(terms):
            one = w1e_ref[k, edge * t : edge * (t + 1), :]
            w1 = jnp.concatenate(
                [
                    one[half * j : half * (j + 1)] * m1_ref[half * i : half * (i + 1), :]
                    for i in range(low)
                    for j in range(2)
                ],
                axis=0,
            )
            first = dot(cube, w1).astype(BF)
            moved = jnp.concatenate(
                [
                    jnp.concatenate(
                        [
                            first[edge * i : edge * (i + 1), quarter * j : quarter * (j + 1)]
                            for i in range(4)
                        ],
                        axis=1,
                    )
                    for j in range(4)
                ],
                axis=0,
            )
            w2 = []
            for i in range(4):
                tile = w2e_ref[k, half * (4 * t + i) : half * (4 * t + i + 1), :]
                pair = [tile * m2_ref[half * q : half * (q + 1), :] for q in range(2)]
                w2 += [jnp.concatenate([x, none], axis=1) for x in pair]
                w2 += [jnp.concatenate([none, x], axis=1) for x in pair]
            second = dot(moved, jnp.concatenate(w2, axis=0)).astype(BF)
            for i in range(4):
                sec_ref[k, i, edge * t : edge * (t + 1), :] = second[edge * i : edge * (i + 1)]

    def finish(k):
        for i in range(4):
            out = dot(g0_ref[k], sec_ref[k, i]).astype(BF)
            keep_ref[k, :, wide * i : wide * (i + 1)] = out[:half]
            send_ref[k, :, wide * i : wide * (i + 1)] = out[half:]

    for i in range(count):
        cube_ref[i] = filtered(first_parent + i)
    expand(range(count * disps))
    for k in range(count * disps):
        products(k)
    for k in range(count * disps):
        finish(k)


def apply_parents(first_parent, count, kinds, near, far, table, weights, half):
    edge = 2 * half
    wide = edge * half // 2
    terms = table.shape[1] // (3 * edge // 4)
    disps = kinds.shape[1]
    shape = jax.ShapeDtypeStruct((count * disps, half, 4 * wide), BF)
    arrays = (near, far, table) + tuple(weights)
    expanded = [
        pltpu.VMEM((count * disps, edge, terms * edge), BF),
        pltpu.VMEM((count * disps, terms * edge, wide), BF),
        pltpu.VMEM((count * disps, terms * 2 * edge, wide // 2), BF),
    ]
    return pl.pallas_call(
        functools.partial(
            apply_kernel,
            half=half,
            terms=terms,
            first_parent=first_parent,
        ),
        in_specs=[pl.BlockSpec(memory_space=pltpu.SMEM)]
        + [pl.BlockSpec(memory_space=pltpu.VMEM)] * len(arrays),
        out_specs=[pl.BlockSpec(memory_space=pltpu.VMEM)] * 2,
        out_shape=[shape, shape],
        scratch_shapes=[
            pltpu.VMEM((count, 4 * edge, wide), BF),
            pltpu.VMEM((count * disps, 4, terms * edge, wide), BF),
        ]
        + expanded,
        compiler_params=pltpu.CompilerParams(vmem_limit_bytes=24 * 1024 * 1024),
    )(kinds, *arrays)


def target(goal_ref, item, nodes):
    goal = goal_ref[item]
    offset = jnp.bitwise_xor(lax.div(goal, nodes), lax.axis_index("leaf"))
    return offset & 1, (offset >> 1) * nodes + lax.rem(goal, nodes)


LANE_PARTS = 2


def sum_kernel(goal_ref, *refs, sources, nodes):
    count = len(refs) - 2 - LANE_PARTS
    row_refs, even_ref, odd_ref, totals = refs[:count], refs[count], refs[count + 1], refs[-LANE_PARTS:]
    slots = even_ref.shape[0]
    lanes = totals[0].shape[-1]
    for total_ref in totals:
        total_ref[...] = jnp.zeros_like(total_ref)
    for row_ref, items in zip(row_refs, sources):
        for i, item in enumerate(items):
            parity, slot = target(goal_ref, item, nodes)
            slot = parity * slots + slot
            for j, total_ref in enumerate(totals):
                part = row_ref[i, :, lanes * j : lanes * (j + 1)].astype(F32)
                total_ref[slot] = (total_ref[slot].astype(F32) + part).astype(BF)
    for j, total_ref in enumerate(totals):
        even_ref[:, :, lanes * j : lanes * (j + 1)] = total_ref[:slots].astype(BF)
        odd_ref[:, :, lanes * j : lanes * (j + 1)] = total_ref[slots:].astype(BF)


def sum_rows(goals, arrays, sources, nodes, leaf_count):
    rows, lanes = arrays[0].shape[1:]
    slots = leaf_count // 2 * nodes
    shape = jax.ShapeDtypeStruct((slots, rows, lanes), BF)
    return pl.pallas_call(
        functools.partial(sum_kernel, sources=sources, nodes=nodes),
        in_specs=[pl.BlockSpec(memory_space=pltpu.SMEM)]
        + [pl.BlockSpec(memory_space=pltpu.VMEM)] * len(arrays),
        out_specs=[pl.BlockSpec(memory_space=pltpu.VMEM)] * 2,
        out_shape=[shape, shape],
        scratch_shapes=[pltpu.VMEM((2 * slots, rows, lanes // LANE_PARTS), BF)] * LANE_PARTS,
        compiler_params=pltpu.CompilerParams(vmem_limit_bytes=24 * 1024 * 1024),
    )(goals, *arrays)


def place(offset, bit):
    return (offset >> (bit + 1) << bit) | (offset & ((1 << bit) - 1))


def first_kernel(even_ref, odd_ref, *outs, bits):
    lanes = outs[0].shape[-1]
    for i, bit in enumerate(bits):
        for r in range(even_ref.shape[0]):
            here = (slice(None), slice(None), slice(lanes * i, lanes * (i + 1)))
            total = even_ref[(r,) + here].astype(F32) + odd_ref[(r,) + here].astype(F32)
            outs[2 * i + (r >> bit & 1)][place(r, bit)] = total.astype(BF)


def first_combine(even, odd, bits):
    offsets, nodes, rows, lanes = even.shape
    shape = jax.ShapeDtypeStruct((offsets // 2, nodes, rows, lanes // 2), BF)
    return pl.pallas_call(
        functools.partial(first_kernel, bits=bits),
        in_specs=[pl.BlockSpec(memory_space=pltpu.VMEM)] * 2,
        out_specs=[pl.BlockSpec(memory_space=pltpu.VMEM)] * 4,
        out_shape=[shape] * 4,
        compiler_params=pltpu.CompilerParams(vmem_limit_bytes=24 * 1024 * 1024),
    )(even, odd)


def combine_kernel(kept_ref, arrived_ref, keep_ref, send_ref, *, bit):
    for r in range(kept_ref.shape[0]):
        total = (kept_ref[r].astype(F32) + arrived_ref[r].astype(F32)).astype(BF)
        out_ref = send_ref if r >> bit & 1 else keep_ref
        out_ref[place(r, bit)] = total


def combine(kept, arrived, bit):
    shape = jax.ShapeDtypeStruct((kept.shape[0] // 2,) + kept.shape[1:], BF)
    return pl.pallas_call(
        functools.partial(combine_kernel, bit=bit),
        in_specs=[pl.BlockSpec(memory_space=pltpu.VMEM)] * 2,
        out_specs=[pl.BlockSpec(memory_space=pltpu.VMEM)] * 2,
        out_shape=[shape, shape],
        compiler_params=pltpu.CompilerParams(vmem_limit_bytes=24 * 1024 * 1024),
    )(kept, arrived)


def last_kernel(kept0_ref, kept1_ref, arrived0_ref, arrived1_ref, out_ref, wide_ref):
    nodes, octants, size = out_ref.shape
    groups = size // 128
    rows, lanes = kept0_ref.shape[2:]

    def store(total, n, first, step):
        wide_ref[pl.ds(n * octants * groups + first, rows, stride=step), :] = total[
            rows * n : rows * (n + 1)
        ]

    for i, (kept_ref, arrived_ref) in enumerate(
        ((kept0_ref, arrived0_ref), (kept1_ref, arrived1_ref))
    ):
        total = kept_ref[0].astype(F32) + arrived_ref[0].astype(F32)
        total = total.reshape(nodes * rows, lanes)
        if octants == 4:
            wide = lanes // 2
            half = wide // 16
            order = one_hot(
                (wide, wide),
                lambda x: x % (2 * half) // half * (wide // 2) + x // (2 * half) * half + x % half,
                lambda x: x,
            )
            for c in range(2):
                moved = dot(total[:, wide * c : wide * (c + 1)].astype(BF), order)
                for bit in range(2):
                    part = moved[:, wide // 2 * bit : wide // 2 * (bit + 1)]
                    for n in range(nodes):
                        store(part, n, (2 * i + bit) * groups + c, 2)
        else:
            for h in range(lanes // 128):
                part = total[:, 128 * h : 128 * (h + 1)]
                for n in range(nodes):
                    store(part, n, i * (lanes // 128) + h, lanes // 64)
    for n in range(nodes):
        for v in range(groups):
            out_ref[n, :, 128 * v : 128 * (v + 1)] = wide_ref[
                pl.ds(n * octants * groups + v, octants, stride=groups), :
            ].astype(BF)


def last_combine(kept, arrived, shape):
    return pl.pallas_call(
        last_kernel,
        in_specs=[pl.BlockSpec(memory_space=pltpu.VMEM)] * 4,
        out_specs=pl.BlockSpec(memory_space=pltpu.VMEM),
        out_shape=jax.ShapeDtypeStruct(shape, BF),
        scratch_shapes=[pltpu.VMEM((math.prod(shape) // 128, 128), F32)],
        compiler_params=pltpu.CompilerParams(vmem_limit_bytes=24 * 1024 * 1024),
    )(*kept, *arrived)


def swap(x, axis, mask):
    count = lax.axis_size(axis)
    return lax.ppermute(x, axis, [(i, i ^ mask) for i in range(count)])


def local(children, child_slot, two_scale, factors, disp_kind, target_leaf, target_node):
    oct_count = lax.axis_size("oct")
    leaf_count = lax.axis_size("leaf")
    edge = two_scale.shape[0]
    half = edge // 2
    held = child_slot.shape[1]
    parents, disps = disp_kind.shape
    paired = oct_count == 2

    if paired:
        near, sent = pick_blocks(child_slot.T, children, parents, half)
        far = swap(sent, "oct", 1)
    else:
        blocks = children.reshape(-1, half, half * half)
        arrived = lax.all_to_all(
            blocks[child_slot], "oct", split_axis=0, concat_axis=1, tiled=True
        ).reshape(parents, 2, 4, half, half * half)
        near, far = arrived[:, 0], arrived[:, 1]

    table = factors.reshape(factors.shape[0], -1, 4 * edge)
    weights = make_weights(two_scale, paired)

    arrays, sources = [], []
    done, counts = 0, [max(1, parents - 2)] + [1] * min(2, parents - 1)
    for count in counts:
        kept, sent = apply_parents(
            done, count, disp_kind, near, far, table, weights, half
        )
        if done == 0:
            target_leaf, target_node, kept = lax.optimization_barrier(
                (target_leaf, target_node, kept)
            )
            nodes = 2 * oct_count
            goal = (target_leaf.reshape(parents, disps) * nodes + target_node).reshape(-1)
            if paired:
                goals = jnp.concatenate([goal, swap(goal, "oct", 1)])
            else:
                goals = lax.all_gather(goal, "oct", tiled=True)
        items = [done * disps + i for i in range(count * disps)]
        if paired:
            arrays += [kept, swap(sent, "oct", 1)]
            sources += [items, [goal.size + item for item in items]]
        else:
            rows = jnp.stack([kept, sent], axis=1).reshape(-1, 2, half, 2, half, 2, half)
            rows = rows.transpose(1, 3, 5, 0, 2, 4, 6)
            rows = rows.reshape(oct_count, held, -1, half, half * half)
            rows = rows.transpose(0, 2, 1, 3, 4)
            rows = lax.all_to_all(rows, "oct", split_axis=0, concat_axis=0, tiled=True)
            arrays += [rows.reshape(-1, held * half, half * half)]
            sources += [[goal.size * o + item for o in range(oct_count) for item in items]]
        done += count

    even, odd = sum_rows(goals, arrays, sources, nodes, leaf_count)
    shape = (leaf_count // 2, nodes) + even.shape[1:]
    even = even.reshape(shape)
    odd = swap(odd, "leaf", 1).reshape(shape)
    masks = [1 << i for i in range(1, (leaf_count - 1).bit_length())]
    orders = [masks[1::-1] + masks[2:], masks]
    parts = first_combine(even, odd, [masks.index(order[0]) for order in orders])
    kept, arrived = [], []
    for i in range(2):
        left = list(masks)
        left.remove(orders[i][0])
        keep, come = parts[2 * i], swap(parts[2 * i + 1], "leaf", orders[i][0])
        for mask in orders[i][1:]:
            keep, send = combine(keep, come, left.index(mask))
            left.remove(mask)
            come = swap(send, "leaf", mask)
        kept.append(keep)
        arrived.append(come)
    return last_combine(kept, arrived, (nodes, held, half * half * half))


def solution(mesh):
    placed = (
        P(("leaf", "oct"), None),
        P("leaf", "oct"),
        P(),
        P(),
        P(("leaf", "oct"), None),
        P(("leaf", "oct"), None, None),
        P(("leaf", "oct"), None),
    )
    return jax.shard_map(
        local, mesh=mesh, in_specs=placed, out_specs=P("leaf", "oct", None), check_vma=False
    )
```

```python
import functools
import math

import jax
import jax.numpy as jnp
from jax import lax
from jax.experimental import pallas as pl
from jax.experimental.pallas import tpu as pltpu
from jax.sharding import PartitionSpec as P

BF = jnp.bfloat16
F32 = jnp.float32


def dot(x, y):
    return jnp.dot(x, y, preferred_element_type=F32)


def one_hot(shape, row_of, lane_of):
    rows = lax.broadcasted_iota(jnp.int32, shape, 0)
    lanes = lax.broadcasted_iota(jnp.int32, shape, 1)
    return (row_of(rows) == lane_of(lanes)).astype(BF)


def exact(x, y):
    return dot(x, y).astype(BF)


def weights_kernel(
    scale_ref, s1e_ref, s2e_ref, m1_ref, m2_ref, fw1_ref, fw2_ref, sa_ref, st_ref, *, half, paired
):
    edge = 2 * half
    low = half // 2
    wide = edge * low
    scale = scale_ref[...]
    turn = lax.axis_index("oct") * half if paired else 0

    def same(x):
        return x

    def turned(x):
        return lax.rem(x + turn, edge)

    def chunked(x):
        return (x % low) * 4 + x // low

    by_chunk = exact(one_hot((edge, edge), chunked, same), scale)
    s1e_ref[...] = exact(by_chunk, one_hot((edge, wide), same, lambda x: x // low))
    s2e_ref[...] = exact(by_chunk, one_hot((edge, wide // 2), same, lambda x: x % edge))
    m1_ref[...] = one_hot((low * half, wide), lambda x: x // half, lambda x: x % low)
    m2_ref[...] = one_hot((edge, wide // 2), lambda x: x // low, lambda x: x // edge)
    sa_ref[...] = exact(scale, one_hot((edge, edge), same, turned))
    pick = one_hot((edge, edge), turned, same)
    st_ref[...] = lax.dot_general(
        pick, by_chunk, (((1,), (1,)), ((), ())), preferred_element_type=F32
    ).astype(BF)

    def spread(row_of, lane_of, lane_count):
        rows = lax.dot_general(
            one_hot((wide, edge), row_of, same),
            scale,
            (((1,), (1,)), ((), ())),
            preferred_element_type=F32,
        ).astype(BF)
        return exact(rows, one_hot((edge, lane_count), same, lane_of))

    for bit in range(2):
        fw1_ref[bit] = spread(
            lambda x: x % half + bit * half, lambda x: x // half, 2 * wide
        ) * one_hot((wide, 2 * wide), lambda x: x // half, lambda x: x % half)
    fw2_ref[...] = spread(
        lambda x: x // (wide // 2) * half + x % half, lambda x: x % edge, wide
    ) * one_hot((wide, wide), lambda x: x // half % low, lambda x: x // edge)


def make_weights(two_scale, paired):
    edge = two_scale.shape[0]
    half = edge // 2
    low = half // 2
    wide = edge * low
    shapes = [
        (edge, wide), (edge, wide // 2), (low * half, wide), (edge, wide // 2),
        (2, wide, 2 * wide), (wide, wide), (edge, edge), (edge, edge),
    ]
    return pl.pallas_call(
        functools.partial(weights_kernel, half=half, paired=paired),
        in_specs=[pl.BlockSpec(memory_space=pltpu.VMEM)],
        out_specs=[pl.BlockSpec(memory_space=pltpu.VMEM)] * len(shapes),
        out_shape=[jax.ShapeDtypeStruct(shape, BF) for shape in shapes],
        compiler_params=pltpu.CompilerParams(vmem_limit_bytes=24 * 1024 * 1024),
    )(two_scale)


def pick_kernel(slot_ref, children_ref, near_ref, send_ref, wide_ref):
    blocks, size = children_ref.shape
    groups = size // 128
    for v in range(groups):
        wide_ref[blocks * v : blocks * (v + 1), :] = children_ref[
            :, 128 * v : 128 * (v + 1)
        ].astype(F32)
    parents, held, rows, lanes = near_ref.shape
    across = lanes // 128
    mine = lax.axis_index("oct")
    for out_ref, owner in ((send_ref, 1 - mine), (near_ref, mine)):
        for i in range(parents):
            for j in range(held):
                slot = slot_ref[j, owner * parents + i]
                for h in range(across):
                    out_ref[i, j, :, 128 * h : 128 * (h + 1)] = wide_ref[
                        pl.ds(blocks * h + slot, rows, stride=blocks * across), :
                    ].astype(BF)


def pick_blocks(child_slot, children, parents, half):
    shape = jax.ShapeDtypeStruct((parents, child_slot.shape[0], half, half * half), BF)
    return pl.pallas_call(
        pick_kernel,
        in_specs=[
            pl.BlockSpec(memory_space=pltpu.SMEM),
            pl.BlockSpec(memory_space=pltpu.VMEM),
        ],
        out_specs=[pl.BlockSpec(memory_space=pltpu.VMEM)] * 2,
        out_shape=[shape, shape],
        scratch_shapes=[pltpu.VMEM((children.size // 128 + 2 * children.shape[0], 128), F32)],
        compiler_params=pltpu.CompilerParams(vmem_limit_bytes=60 * 1024 * 1024),
    )(child_slot, children)


def by_output(table, edge, terms):
    low = edge // 4
    lanes = 4 * edge
    chunk = lax.broadcasted_iota(jnp.int32, (low, lanes), 1) // edge
    groups = []
    for start in range(0, terms, 4):
        tiles = [
            table[low * min(t, terms - 1) : low * (min(t, terms - 1) + 1)]
            for t in range(start, start + 4)
        ]
        for step in (1, 2):
            upper = (chunk // step) % 2 == 1
            mixed = list(tiles)
            for i in range(4):
                if i & step == 0:
                    mixed[i] = jnp.where(
                        upper, pltpu.roll(tiles[i + step], edge * step, 1), tiles[i]
                    )
                    mixed[i + step] = jnp.where(
                        upper, tiles[i + step], pltpu.roll(tiles[i], lanes - edge * step, 1)
                    )
            tiles = mixed
        groups.append(jnp.concatenate(tiles, axis=0))
    return jnp.concatenate(groups, axis=1)[:, : terms * edge]


def apply_kernel(
    kind_ref, *refs, half, terms, first_parent,
):
    (
        near_ref, far_ref, table_ref, s1e_ref, s2e_ref, m1_ref, m2_ref, fw1_ref, fw2_ref,
        sa_ref, st_ref, keep_ref, send_ref, cube_ref, sec_ref,
    ) = refs[:15]
    g0_ref, w1e_ref, w2e_ref = refs[15:]
    edge = 2 * half
    low = half // 2
    wide = edge * low
    quarter = wide // 4
    rows = terms * low
    disps = kind_ref.shape[1]
    count = keep_ref.shape[0] // disps

    def expand(entries):
        kinds = [kind_ref[first_parent + k // disps, k % disps] for k in entries]
        spread = [
            [
                by_output(
                    table_ref[kind, rows * axis : rows * (axis + 1), :].astype(F32), edge, terms
                ).astype(BF)
                for kind in kinds
            ]
            for axis in range(3)
        ]
        turned = [[x.T for x in spread[axis]] for axis in (1, 2)]
        for k, x in zip(entries, spread[0]):
            g0_ref[k] = dot(st_ref[...], x).astype(BF)
        for k, x in zip(entries, turned[0]):
            w1e_ref[k] = dot(x, s1e_ref[...]).astype(BF)
        for k, x in zip(entries, turned[1]):
            once = dot(x, s2e_ref[...])
            for i in range(terms * 4):
                tile = once[low * i : low * (i + 1)]
                w2e_ref[k, half * i : half * (i + 1), :] = jnp.concatenate(
                    [tile, tile], axis=0
                ).astype(BF)

    def filtered(parent):
        total = None
        for bit in range(2):
            parts = []
            for mid in range(2):
                parts += [near_ref[parent, 2 * mid + bit], far_ref[parent, 2 * mid + bit]]
            part = dot(jnp.concatenate(parts, axis=0), fw1_ref[bit])
            total = part if total is None else total + part
        total = total.astype(BF)
        lanes = wide // 2
        moved = jnp.concatenate(
            [
                jnp.concatenate(
                    [
                        total[:edge, lanes * i : lanes * (i + 1)],
                        total[edge:, lanes * i : lanes * (i + 1)],
                    ],
                    axis=1,
                )
                for i in range(4)
            ],
            axis=0,
        )
        second = dot(moved, fw2_ref[...]).astype(BF)
        return jnp.concatenate(
            [
                dot(sa_ref[...], second[edge * i : edge * (i + 1)]).astype(BF)
                for i in range(4)
            ],
            axis=0,
        )

    def products(k):
        cube = cube_ref[k // disps]
        none = jnp.zeros((half, wide // 2), BF)
        for t in range(terms):
            one = w1e_ref[k, edge * t : edge * (t + 1), :]
            w1 = jnp.concatenate(
                [
                    one[half * j : half * (j + 1)] * m1_ref[half * i : half * (i + 1), :]
                    for i in range(low)
                    for j in range(2)
                ],
                axis=0,
            )
            first = dot(cube, w1).astype(BF)
            moved = jnp.concatenate(
                [
                    jnp.concatenate(
                        [
                            first[edge * i : edge * (i + 1), quarter * j : quarter * (j + 1)]
                            for i in range(4)
                        ],
                        axis=1,
                    )
                    for j in range(4)
                ],
                axis=0,
            )
            w2 = []
            for i in range(4):
                tile = w2e_ref[k, half * (4 * t + i) : half * (4 * t + i + 1), :]
                pair = [tile * m2_ref[half * q : half * (q + 1), :] for q in range(2)]
                w2 += [jnp.concatenate([x, none], axis=1) for x in pair]
                w2 += [jnp.concatenate([none, x], axis=1) for x in pair]
            second = dot(moved, jnp.concatenate(w2, axis=0)).astype(BF)
            for i in range(4):
                sec_ref[k, i, edge * t : edge * (t + 1), :] = second[edge * i : edge * (i + 1)]

    def finish(k):
        for i in range(4):
            out = dot(g0_ref[k], sec_ref[k, i]).astype(BF)
            keep_ref[k, :, wide * i : wide * (i + 1)] = out[:half]
            send_ref[k, :, wide * i : wide * (i + 1)] = out[half:]

    for i in range(count):
        cube_ref[i] = filtered(first_parent + i)
    expand(range(count * disps))
    for k in range(count * disps):
        products(k)
    for k in range(count * disps):
        finish(k)


def apply_parents(first_parent, count, kinds, near, far, table, weights, half):
    edge = 2 * half
    wide = edge * half // 2
    terms = table.shape[1] // (3 * edge // 4)
    disps = kinds.shape[1]
    shape = jax.ShapeDtypeStruct((count * disps, half, 4 * wide), BF)
    arrays = (near, far, table) + tuple(weights)
    expanded = [
        pltpu.VMEM((count * disps, edge, terms * edge), BF),
        pltpu.VMEM((count * disps, terms * edge, wide), BF),
        pltpu.VMEM((count * disps, terms * 2 * edge, wide // 2), BF),
    ]
    return pl.pallas_call(
        functools.partial(
            apply_kernel,
            half=half,
            terms=terms,
            first_parent=first_parent,
        ),
        in_specs=[pl.BlockSpec(memory_space=pltpu.SMEM)]
        + [pl.BlockSpec(memory_space=pltpu.VMEM)] * len(arrays),
        out_specs=[pl.BlockSpec(memory_space=pltpu.VMEM)] * 2,
        out_shape=[shape, shape],
        scratch_shapes=[
            pltpu.VMEM((count, 4 * edge, wide), BF),
            pltpu.VMEM((count * disps, 4, terms * edge, wide), BF),
        ]
        + expanded,
        compiler_params=pltpu.CompilerParams(vmem_limit_bytes=24 * 1024 * 1024),
    )(kinds, *arrays)


def target(goal_ref, item, nodes):
    goal = goal_ref[item]
    offset = jnp.bitwise_xor(lax.div(goal, nodes), lax.axis_index("leaf"))
    return offset & 1, (offset >> 1) * nodes + lax.rem(goal, nodes)


def sum_kernel(goal_ref, *refs, sources, nodes, start):
    row_refs, (even_ref, odd_ref, total_ref) = refs[:-3], refs[-3:]
    slots, _, lanes = even_ref.shape
    total_ref[...] = jnp.zeros_like(total_ref)
    for row_ref, items in zip(row_refs, sources):
        for i, item in enumerate(items):
            parity, slot = target(goal_ref, item, nodes)
            slot = parity * slots + slot
            part = row_ref[i, :, start : start + lanes].astype(F32)
            total_ref[slot] = (total_ref[slot].astype(F32) + part).astype(BF)
    even_ref[...] = total_ref[:slots]
    odd_ref[...] = total_ref[slots:]


def sum_rows(goals, arrays, sources, nodes, leaf_count, start, lanes):
    rows = arrays[0].shape[1]
    slots = leaf_count // 2 * nodes
    shape = jax.ShapeDtypeStruct((slots, rows, lanes), BF)
    return pl.pallas_call(
        functools.partial(sum_kernel, sources=sources, nodes=nodes, start=start),
        in_specs=[pl.BlockSpec(memory_space=pltpu.SMEM)]
        + [pl.BlockSpec(memory_space=pltpu.VMEM)] * len(arrays),
        out_specs=[pl.BlockSpec(memory_space=pltpu.VMEM)] * 2,
        out_shape=[shape, shape],
        scratch_shapes=[pltpu.VMEM((2 * slots, rows, lanes), BF)],
        compiler_params=pltpu.CompilerParams(vmem_limit_bytes=24 * 1024 * 1024),
    )(goals, *arrays)


def place(offset, bit):
    return (offset >> (bit + 1) << bit) | (offset & ((1 << bit) - 1))


def combine_kernel(kept_ref, arrived_ref, keep_ref, send_ref, *, bit):
    for r in range(kept_ref.shape[0]):
        total = (kept_ref[r].astype(F32) + arrived_ref[r].astype(F32)).astype(BF)
        out_ref = send_ref if r >> bit & 1 else keep_ref
        out_ref[place(r, bit)] = total


def combine(kept, arrived, bit):
    shape = jax.ShapeDtypeStruct((kept.shape[0] // 2,) + kept.shape[1:], BF)
    return pl.pallas_call(
        functools.partial(combine_kernel, bit=bit),
        in_specs=[pl.BlockSpec(memory_space=pltpu.VMEM)] * 2,
        out_specs=[pl.BlockSpec(memory_space=pltpu.VMEM)] * 2,
        out_shape=[shape, shape],
        compiler_params=pltpu.CompilerParams(vmem_limit_bytes=24 * 1024 * 1024),
    )(kept, arrived)


def last_kernel(kept0_ref, kept1_ref, arrived0_ref, arrived1_ref, out_ref, wide_ref):
    nodes, octants, size = out_ref.shape
    groups = size // 128
    rows, lanes = kept0_ref.shape[2:]

    def store(total, n, first, step):
        wide_ref[pl.ds(n * octants * groups + first, rows, stride=step), :] = total[
            rows * n : rows * (n + 1)
        ]

    for i, (kept_ref, arrived_ref) in enumerate(
        ((kept0_ref, arrived0_ref), (kept1_ref, arrived1_ref))
    ):
        total = kept_ref[0].astype(F32) + arrived_ref[0].astype(F32)
        total = total.reshape(nodes * rows, lanes)
        if octants == 4:
            wide = lanes // 2
            half = wide // 16
            order = one_hot(
                (wide, wide),
                lambda x: x % (2 * half) // half * (wide // 2) + x // (2 * half) * half + x % half,
                lambda x: x,
            )
            for c in range(2):
                moved = dot(total[:, wide * c : wide * (c + 1)].astype(BF), order)
                for bit in range(2):
                    part = moved[:, wide // 2 * bit : wide // 2 * (bit + 1)]
                    for n in range(nodes):
                        store(part, n, (2 * i + bit) * groups + c, 2)
        else:
            for h in range(lanes // 128):
                part = total[:, 128 * h : 128 * (h + 1)]
                for n in range(nodes):
                    store(part, n, i * (lanes // 128) + h, lanes // 64)
    for n in range(nodes):
        for v in range(groups):
            out_ref[n, :, 128 * v : 128 * (v + 1)] = wide_ref[
                pl.ds(n * octants * groups + v, octants, stride=groups), :
            ].astype(BF)


def last_combine(kept, arrived, shape):
    return pl.pallas_call(
        last_kernel,
        in_specs=[pl.BlockSpec(memory_space=pltpu.VMEM)] * 4,
        out_specs=pl.BlockSpec(memory_space=pltpu.VMEM),
        out_shape=jax.ShapeDtypeStruct(shape, BF),
        scratch_shapes=[pltpu.VMEM((math.prod(shape) // 128, 128), F32)],
        compiler_params=pltpu.CompilerParams(vmem_limit_bytes=24 * 1024 * 1024),
    )(*kept, *arrived)


def swap(x, axis, mask):
    count = lax.axis_size(axis)
    return lax.ppermute(x, axis, [(i, i ^ mask) for i in range(count)])


def local(children, child_slot, two_scale, factors, disp_kind, target_leaf, target_node):
    oct_count = lax.axis_size("oct")
    leaf_count = lax.axis_size("leaf")
    edge = two_scale.shape[0]
    half = edge // 2
    held = child_slot.shape[1]
    parents, disps = disp_kind.shape
    paired = oct_count == 2

    if paired:
        near, sent = pick_blocks(child_slot.T, children, parents, half)
        far = swap(sent, "oct", 1)
    else:
        blocks = children.reshape(-1, half, half * half)
        arrived = lax.all_to_all(
            blocks[child_slot], "oct", split_axis=0, concat_axis=1, tiled=True
        ).reshape(parents, 2, 4, half, half * half)
        near, far = arrived[:, 0], arrived[:, 1]

    table = factors.reshape(factors.shape[0], -1, 4 * edge)
    weights = make_weights(two_scale, paired)

    arrays, sources = [], []
    done, counts = 0, [max(1, parents - 2)] + [1] * min(2, parents - 1)
    for count in counts:
        kept, sent = apply_parents(
            done, count, disp_kind, near, far, table, weights, half
        )
        if done == 0:
            target_leaf, target_node, kept = lax.optimization_barrier(
                (target_leaf, target_node, kept)
            )
            nodes = 2 * oct_count
            goal = (target_leaf.reshape(parents, disps) * nodes + target_node).reshape(-1)
            if paired:
                goals = jnp.concatenate([goal, swap(goal, "oct", 1)])
            else:
                goals = lax.all_gather(goal, "oct", tiled=True)
        items = [done * disps + i for i in range(count * disps)]
        if paired:
            arrays += [kept, swap(sent, "oct", 1)]
            sources += [items, [goal.size + item for item in items]]
        else:
            rows = jnp.stack([kept, sent], axis=1).reshape(-1, 2, half, 2, half, 2, half)
            rows = rows.transpose(1, 3, 5, 0, 2, 4, 6)
            rows = rows.reshape(oct_count, held, -1, half, half * half)
            rows = rows.transpose(0, 2, 1, 3, 4)
            rows = lax.all_to_all(rows, "oct", split_axis=0, concat_axis=0, tiled=True)
            arrays += [rows.reshape(-1, held * half, half * half)]
            sources += [[goal.size * o + item for o in range(oct_count) for item in items]]
        done += count

    lanes = arrays[0].shape[-1] // 2
    masks = [1 << i for i in range(1, (leaf_count - 1).bit_length())]
    kept, arrived = [], []
    for i, order in enumerate((masks[1::-1] + masks[2:], masks)):
        keep, send = sum_rows(goals, arrays, sources, nodes, leaf_count, lanes * i, lanes)
        shape = (leaf_count // 2, nodes, -1, lanes)
        keep, come = keep.reshape(shape), swap(send, "leaf", 1).reshape(shape)
        left = list(masks)
        for mask in order:
            keep, send = combine(keep, come, left.index(mask))
            left.remove(mask)
            come = swap(send, "leaf", mask)
        kept.append(keep)
        arrived.append(come)
    return last_combine(kept, arrived, (nodes, held, half * half * half))


def solution(mesh):
    placed = (
        P(("leaf", "oct"), None),
        P("leaf", "oct"),
        P(),
        P(),
        P(("leaf", "oct"), None),
        P(("leaf", "oct"), None, None),
        P(("leaf", "oct"), None),
    )
    return jax.shard_map(
        local, mesh=mesh, in_specs=placed, out_specs=P("leaf", "oct", None), check_vma=False
    )
```

```python
import functools
import math

import jax
import jax.numpy as jnp
from jax import lax
from jax.experimental import pallas as pl
from jax.experimental.pallas import tpu as pltpu
from jax.sharding import PartitionSpec as P

BF = jnp.bfloat16
F32 = jnp.float32


def dot(x, y):
    return jnp.dot(x, y, preferred_element_type=F32)


def one_hot(shape, row_of, lane_of):
    rows = lax.broadcasted_iota(jnp.int32, shape, 0)
    lanes = lax.broadcasted_iota(jnp.int32, shape, 1)
    return (row_of(rows) == lane_of(lanes)).astype(BF)


def exact(x, y):
    return dot(x, y).astype(BF)


def weights_kernel(
    scale_ref, s1e_ref, s2e_ref, m1_ref, m2_ref, fw1_ref, fw2_ref, sa_ref, st_ref, *, half, paired
):
    edge = 2 * half
    low = half // 2
    wide = edge * low
    scale = scale_ref[...]
    turn = lax.axis_index("oct") * half if paired else 0

    def same(x):
        return x

    def turned(x):
        return lax.rem(x + turn, edge)

    def chunked(x):
        return (x % low) * 4 + x // low

    by_chunk = exact(one_hot((edge, edge), chunked, same), scale)
    s1e_ref[...] = exact(by_chunk, one_hot((edge, wide), same, lambda x: x // low))
    s2e_ref[...] = exact(by_chunk, one_hot((edge, wide // 2), same, lambda x: x % edge))
    m1_ref[...] = one_hot((low * half, wide), lambda x: x // half, lambda x: x % low)
    m2_ref[...] = one_hot((edge, wide // 2), lambda x: x // low, lambda x: x // edge)
    sa_ref[...] = exact(scale, one_hot((edge, edge), same, turned))
    pick = one_hot((edge, edge), turned, same)
    st_ref[...] = lax.dot_general(
        pick, by_chunk, (((1,), (1,)), ((), ())), preferred_element_type=F32
    ).astype(BF)

    def spread(row_of, lane_of, lane_count):
        rows = lax.dot_general(
            one_hot((wide, edge), row_of, same),
            scale,
            (((1,), (1,)), ((), ())),
            preferred_element_type=F32,
        ).astype(BF)
        return exact(rows, one_hot((edge, lane_count), same, lane_of))

    for bit in range(2):
        fw1_ref[bit] = spread(
            lambda x: x % half + bit * half, lambda x: x // half, 2 * wide
        ) * one_hot((wide, 2 * wide), lambda x: x // half, lambda x: x % half)
    fw2_ref[...] = spread(
        lambda x: x // (wide // 2) * half + x % half, lambda x: x % edge, wide
    ) * one_hot((wide, wide), lambda x: x // half % low, lambda x: x // edge)


def make_weights(two_scale, paired):
    edge = two_scale.shape[0]
    half = edge // 2
    low = half // 2
    wide = edge * low
    shapes = [
        (edge, wide), (edge, wide // 2), (low * half, wide), (edge, wide // 2),
        (2, wide, 2 * wide), (wide, wide), (edge, edge), (edge, edge),
    ]
    return pl.pallas_call(
        functools.partial(weights_kernel, half=half, paired=paired),
        in_specs=[pl.BlockSpec(memory_space=pltpu.VMEM)],
        out_specs=[pl.BlockSpec(memory_space=pltpu.VMEM)] * len(shapes),
        out_shape=[jax.ShapeDtypeStruct(shape, BF) for shape in shapes],
        compiler_params=pltpu.CompilerParams(vmem_limit_bytes=24 * 1024 * 1024),
    )(two_scale)


def pick_kernel(slot_ref, children_ref, near_ref, send_ref):
    blocks, _ = children_ref.shape
    parents, held, rows, lanes = near_ref.shape
    stacked = jnp.concatenate(
        [children_ref[:, lanes * p : lanes * (p + 1)] for p in range(rows)], axis=0
    )
    row = lax.broadcasted_iota(jnp.int32, (rows, rows * blocks), 0)
    place = lax.broadcasted_iota(jnp.int32, (rows, rows * blocks), 1) - row * blocks
    mine = lax.axis_index("oct")
    for out_ref, owner in ((send_ref, 1 - mine), (near_ref, mine)):
        wanted = [
            (place == slot_ref[j, owner * parents + i]).astype(F32).astype(BF)
            for i in range(parents)
            for j in range(held)
        ]
        picked = exact(jnp.concatenate(wanted, axis=0), stacked)
        for i in range(parents):
            for j in range(held):
                first = rows * (held * i + j)
                out_ref[i, j] = picked[first : first + rows]


def pick_blocks(child_slot, children, parents, half):
    shape = jax.ShapeDtypeStruct((parents, child_slot.shape[0], half, half * half), BF)
    return pl.pallas_call(
        pick_kernel,
        in_specs=[
            pl.BlockSpec(memory_space=pltpu.SMEM),
            pl.BlockSpec(memory_space=pltpu.VMEM),
        ],
        out_specs=[pl.BlockSpec(memory_space=pltpu.VMEM)] * 2,
        out_shape=[shape, shape],
        compiler_params=pltpu.CompilerParams(vmem_limit_bytes=60 * 1024 * 1024),
    )(child_slot, children)


def by_output(table, edge, terms):
    low = edge // 4
    lanes = 4 * edge
    chunk = lax.broadcasted_iota(jnp.int32, (low, lanes), 1) // edge
    groups = []
    for start in range(0, terms, 4):
        tiles = [
            table[low * min(t, terms - 1) : low * (min(t, terms - 1) + 1)]
            for t in range(start, start + 4)
        ]
        for step in (1, 2):
            upper = (chunk // step) % 2 == 1
            mixed = list(tiles)
            for i in range(4):
                if i & step == 0:
                    mixed[i] = jnp.where(
                        upper, pltpu.roll(tiles[i + step], edge * step, 1), tiles[i]
                    )
                    mixed[i + step] = jnp.where(
                        upper, tiles[i + step], pltpu.roll(tiles[i], lanes - edge * step, 1)
                    )
            tiles = mixed
        groups.append(jnp.concatenate(tiles, axis=0))
    return jnp.concatenate(groups, axis=1)[:, : terms * edge]


def apply_kernel(
    kind_ref, *refs, half, terms, first_parent,
):
    (
        near_ref, far_ref, table_ref, s1e_ref, s2e_ref, m1_ref, m2_ref, fw1_ref, fw2_ref,
        sa_ref, st_ref, keep_ref, send_ref, cube_ref, sec_ref,
    ) = refs[:15]
    g0_ref, w1e_ref, w2e_ref = refs[15:]
    edge = 2 * half
    low = half // 2
    wide = edge * low
    quarter = wide // 4
    rows = terms * low
    disps = kind_ref.shape[1]
    count = keep_ref.shape[0] // disps

    def expand(entries):
        kinds = [kind_ref[first_parent + k // disps, k % disps] for k in entries]
        spread = [
            [
                by_output(
                    table_ref[kind, rows * axis : rows * (axis + 1), :].astype(F32), edge, terms
                ).astype(BF)
                for kind in kinds
            ]
            for axis in range(3)
        ]
        turned = [[x.T for x in spread[axis]] for axis in (1, 2)]
        for k, x in zip(entries, spread[0]):
            g0_ref[k] = dot(st_ref[...], x).astype(BF)
        for k, x in zip(entries, turned[0]):
            w1e_ref[k] = dot(x, s1e_ref[...]).astype(BF)
        for k, x in zip(entries, turned[1]):
            once = dot(x, s2e_ref[...])
            for i in range(terms * 4):
                tile = once[low * i : low * (i + 1)]
                w2e_ref[k, half * i : half * (i + 1), :] = jnp.concatenate(
                    [tile, tile], axis=0
                ).astype(BF)

    def filtered(parent):
        total = None
        for bit in range(2):
            parts = []
            for mid in range(2):
                parts += [near_ref[parent, 2 * mid + bit], far_ref[parent, 2 * mid + bit]]
            part = dot(jnp.concatenate(parts, axis=0), fw1_ref[bit])
            total = part if total is None else total + part
        total = total.astype(BF)
        lanes = wide // 2
        moved = jnp.concatenate(
            [
                jnp.concatenate(
                    [
                        total[:edge, lanes * i : lanes * (i + 1)],
                        total[edge:, lanes * i : lanes * (i + 1)],
                    ],
                    axis=1,
                )
                for i in range(4)
            ],
            axis=0,
        )
        second = dot(moved, fw2_ref[...]).astype(BF)
        return jnp.concatenate(
            [
                dot(sa_ref[...], second[edge * i : edge * (i + 1)]).astype(BF)
                for i in range(4)
            ],
            axis=0,
        )

    def products(k):
        cube = cube_ref[k // disps]
        none = jnp.zeros((half, wide // 2), BF)
        for t in range(terms):
            one = w1e_ref[k, edge * t : edge * (t + 1), :]
            w1 = jnp.concatenate(
                [
                    one[half * j : half * (j + 1)] * m1_ref[half * i : half * (i + 1), :]
                    for i in range(low)
                    for j in range(2)
                ],
                axis=0,
            )
            first = dot(cube, w1).astype(BF)
            moved = jnp.concatenate(
                [
                    jnp.concatenate(
                        [
                            first[edge * i : edge * (i + 1), quarter * j : quarter * (j + 1)]
                            for i in range(4)
                        ],
                        axis=1,
                    )
                    for j in range(4)
                ],
                axis=0,
            )
            w2 = []
            for i in range(4):
                tile = w2e_ref[k, half * (4 * t + i) : half * (4 * t + i + 1), :]
                pair = [tile * m2_ref[half * q : half * (q + 1), :] for q in range(2)]
                w2 += [jnp.concatenate([x, none], axis=1) for x in pair]
                w2 += [jnp.concatenate([none, x], axis=1) for x in pair]
            second = dot(moved, jnp.concatenate(w2, axis=0)).astype(BF)
            for i in range(4):
                sec_ref[k, i, edge * t : edge * (t + 1), :] = second[edge * i : edge * (i + 1)]

    def finish(k):
        for i in range(4):
            out = dot(g0_ref[k], sec_ref[k, i]).astype(BF)
            keep_ref[k, :, wide * i : wide * (i + 1)] = out[:half]
            send_ref[k, :, wide * i : wide * (i + 1)] = out[half:]

    for i in range(count):
        cube_ref[i] = filtered(first_parent + i)
    expand(range(count * disps))
    for k in range(count * disps):
        products(k)
    for k in range(count * disps):
        finish(k)


def apply_parents(first_parent, count, kinds, near, far, table, weights, half):
    edge = 2 * half
    wide = edge * half // 2
    terms = table.shape[1] // (3 * edge // 4)
    disps = kinds.shape[1]
    shape = jax.ShapeDtypeStruct((count * disps, half, 4 * wide), BF)
    arrays = (near, far, table) + tuple(weights)
    expanded = [
        pltpu.VMEM((count * disps, edge, terms * edge), BF),
        pltpu.VMEM((count * disps, terms * edge, wide), BF),
        pltpu.VMEM((count * disps, terms * 2 * edge, wide // 2), BF),
    ]
    return pl.pallas_call(
        functools.partial(
            apply_kernel,
            half=half,
            terms=terms,
            first_parent=first_parent,
        ),
        in_specs=[pl.BlockSpec(memory_space=pltpu.SMEM)]
        + [pl.BlockSpec(memory_space=pltpu.VMEM)] * len(arrays),
        out_specs=[pl.BlockSpec(memory_space=pltpu.VMEM)] * 2,
        out_shape=[shape, shape],
        scratch_shapes=[
            pltpu.VMEM((count, 4 * edge, wide), BF),
            pltpu.VMEM((count * disps, 4, terms * edge, wide), BF),
        ]
        + expanded,
        compiler_params=pltpu.CompilerParams(vmem_limit_bytes=24 * 1024 * 1024),
    )(kinds, *arrays)


def target(goal_ref, item, nodes):
    goal = goal_ref[item]
    offset = jnp.bitwise_xor(lax.div(goal, nodes), lax.axis_index("leaf"))
    return offset & 1, (offset >> 1) * nodes + lax.rem(goal, nodes)


def sum_kernel(goal_ref, *refs, sources, nodes, start):
    row_refs, (even_ref, odd_ref, total_ref) = refs[:-3], refs[-3:]
    slots, _, lanes = even_ref.shape
    total_ref[...] = jnp.zeros_like(total_ref)
    for row_ref, items in zip(row_refs, sources):
        for i, item in enumerate(items):
            parity, slot = target(goal_ref, item, nodes)
            slot = parity * slots + slot
            part = row_ref[i, :, start : start + lanes].astype(F32)
            total_ref[slot] = (total_ref[slot].astype(F32) + part).astype(BF)
    even_ref[...] = total_ref[:slots]
    odd_ref[...] = total_ref[slots:]


def sum_rows(goals, arrays, sources, nodes, leaf_count, start, lanes):
    rows = arrays[0].shape[1]
    slots = leaf_count // 2 * nodes
    shape = jax.ShapeDtypeStruct((slots, rows, lanes), BF)
    return pl.pallas_call(
        functools.partial(sum_kernel, sources=sources, nodes=nodes, start=start),
        in_specs=[pl.BlockSpec(memory_space=pltpu.SMEM)]
        + [pl.BlockSpec(memory_space=pltpu.VMEM)] * len(arrays),
        out_specs=[pl.BlockSpec(memory_space=pltpu.VMEM)] * 2,
        out_shape=[shape, shape],
        scratch_shapes=[pltpu.VMEM((2 * slots, rows, lanes), BF)],
        compiler_params=pltpu.CompilerParams(vmem_limit_bytes=24 * 1024 * 1024),
    )(goals, *arrays)


def place(offset, bit):
    return (offset >> (bit + 1) << bit) | (offset & ((1 << bit) - 1))


def combine_kernel(kept_ref, arrived_ref, keep_ref, send_ref, *, bit):
    for r in range(kept_ref.shape[0]):
        total = (kept_ref[r].astype(F32) + arrived_ref[r].astype(F32)).astype(BF)
        out_ref = send_ref if r >> bit & 1 else keep_ref
        out_ref[place(r, bit)] = total


def combine(kept, arrived, bit):
    shape = jax.ShapeDtypeStruct((kept.shape[0] // 2,) + kept.shape[1:], BF)
    return pl.pallas_call(
        functools.partial(combine_kernel, bit=bit),
        in_specs=[pl.BlockSpec(memory_space=pltpu.VMEM)] * 2,
        out_specs=[pl.BlockSpec(memory_space=pltpu.VMEM)] * 2,
        out_shape=[shape, shape],
        compiler_params=pltpu.CompilerParams(vmem_limit_bytes=24 * 1024 * 1024),
    )(kept, arrived)


def last_kernel(kept0_ref, kept1_ref, arrived0_ref, arrived1_ref, out_ref, wide_ref):
    nodes, octants, size = out_ref.shape
    groups = size // 128
    rows, lanes = kept0_ref.shape[2:]

    def store(total, n, first, step):
        wide_ref[pl.ds(n * octants * groups + first, rows, stride=step), :] = total[
            rows * n : rows * (n + 1)
        ]

    for i, (kept_ref, arrived_ref) in enumerate(
        ((kept0_ref, arrived0_ref), (kept1_ref, arrived1_ref))
    ):
        total = kept_ref[0].astype(F32) + arrived_ref[0].astype(F32)
        total = total.reshape(nodes * rows, lanes)
        if octants == 4:
            wide = lanes // 2
            half = wide // 16
            order = one_hot(
                (wide, wide),
                lambda x: x % (2 * half) // half * (wide // 2) + x // (2 * half) * half + x % half,
                lambda x: x,
            )
            for c in range(2):
                moved = dot(total[:, wide * c : wide * (c + 1)].astype(BF), order)
                for bit in range(2):
                    part = moved[:, wide // 2 * bit : wide // 2 * (bit + 1)]
                    for n in range(nodes):
                        store(part, n, (2 * i + bit) * groups + c, 2)
        else:
            for h in range(lanes // 128):
                part = total[:, 128 * h : 128 * (h + 1)]
                for n in range(nodes):
                    store(part, n, i * (lanes // 128) + h, lanes // 64)
    for n in range(nodes):
        for v in range(groups):
            out_ref[n, :, 128 * v : 128 * (v + 1)] = wide_ref[
                pl.ds(n * octants * groups + v, octants, stride=groups), :
            ].astype(BF)


def last_combine(kept, arrived, shape):
    return pl.pallas_call(
        last_kernel,
        in_specs=[pl.BlockSpec(memory_space=pltpu.VMEM)] * 4,
        out_specs=pl.BlockSpec(memory_space=pltpu.VMEM),
        out_shape=jax.ShapeDtypeStruct(shape, BF),
        scratch_shapes=[pltpu.VMEM((math.prod(shape) // 128, 128), F32)],
        compiler_params=pltpu.CompilerParams(vmem_limit_bytes=24 * 1024 * 1024),
    )(*kept, *arrived)


def swap(x, axis, mask):
    count = lax.axis_size(axis)
    return lax.ppermute(x, axis, [(i, i ^ mask) for i in range(count)])


def local(children, child_slot, two_scale, factors, disp_kind, target_leaf, target_node):
    oct_count = lax.axis_size("oct")
    leaf_count = lax.axis_size("leaf")
    edge = two_scale.shape[0]
    half = edge // 2
    held = child_slot.shape[1]
    parents, disps = disp_kind.shape
    paired = oct_count == 2

    if paired:
        near, sent = pick_blocks(child_slot.T, children, parents, half)
        far = swap(sent, "oct", 1)
    else:
        blocks = children.reshape(-1, half, half * half)
        arrived = lax.all_to_all(
            blocks[child_slot], "oct", split_axis=0, concat_axis=1, tiled=True
        ).reshape(parents, 2, 4, half, half * half)
        near, far = arrived[:, 0], arrived[:, 1]

    table = factors.reshape(factors.shape[0], -1, 4 * edge)
    weights = make_weights(two_scale, paired)

    arrays, sources = [], []
    done, counts = 0, [max(1, parents - 2)] + [1] * min(2, parents - 1)
    for count in counts:
        kept, sent = apply_parents(
            done, count, disp_kind, near, far, table, weights, half
        )
        if done == 0:
            target_leaf, target_node, kept = lax.optimization_barrier(
                (target_leaf, target_node, kept)
            )
            nodes = 2 * oct_count
            goal = (target_leaf.reshape(parents, disps) * nodes + target_node).reshape(-1)
            if paired:
                goals = jnp.concatenate([goal, swap(goal, "oct", 1)])
            else:
                goals = lax.all_gather(goal, "oct", tiled=True)
        items = [done * disps + i for i in range(count * disps)]
        if paired:
            arrays += [kept, swap(sent, "oct", 1)]
            sources += [items, [goal.size + item for item in items]]
        else:
            rows = jnp.stack([kept, sent], axis=1).reshape(-1, 2, half, 2, half, 2, half)
            rows = rows.transpose(1, 3, 5, 0, 2, 4, 6)
            rows = rows.reshape(oct_count, held, -1, half, half * half)
            rows = rows.transpose(0, 2, 1, 3, 4)
            rows = lax.all_to_all(rows, "oct", split_axis=0, concat_axis=0, tiled=True)
            arrays += [rows.reshape(-1, held * half, half * half)]
            sources += [[goal.size * o + item for o in range(oct_count) for item in items]]
        done += count

    lanes = arrays[0].shape[-1] // 2
    masks = [1 << i for i in range(1, (leaf_count - 1).bit_length())]
    kept, arrived = [], []
    for i, order in enumerate((masks[1::-1] + masks[2:], masks)):
        keep, send = sum_rows(goals, arrays, sources, nodes, leaf_count, lanes * i, lanes)
        shape = (leaf_count // 2, nodes, -1, lanes)
        keep, come = keep.reshape(shape), swap(send, "leaf", 1).reshape(shape)
        left = list(masks)
        for mask in order:
            keep, send = combine(keep, come, left.index(mask))
            left.remove(mask)
            come = swap(send, "leaf", mask)
        kept.append(keep)
        arrived.append(come)
    return last_combine(kept, arrived, (nodes, held, half * half * half))


def solution(mesh):
    placed = (
        P(("leaf", "oct"), None),
        P("leaf", "oct"),
        P(),
        P(),
        P(("leaf", "oct"), None),
        P(("leaf", "oct"), None, None),
        P(("leaf", "oct"), None),
    )
    return jax.shard_map(
        local, mesh=mesh, in_specs=placed, out_specs=P("leaf", "oct", None), check_vma=False
    )
```

```python
import functools
import math

import jax
import jax.numpy as jnp
from jax import lax
from jax.experimental import pallas as pl
from jax.experimental.pallas import tpu as pltpu
from jax.sharding import PartitionSpec as P

BF = jnp.bfloat16
F32 = jnp.float32


def dot(x, y):
    return jnp.dot(x, y, preferred_element_type=F32)


def one_hot(shape, row_of, lane_of):
    rows = lax.broadcasted_iota(jnp.int32, shape, 0)
    lanes = lax.broadcasted_iota(jnp.int32, shape, 1)
    return (row_of(rows) == lane_of(lanes)).astype(BF)


def exact(x, y):
    return dot(x, y).astype(BF)


def weights_kernel(
    scale_ref, s1e_ref, s2e_ref, m1_ref, m2_ref, fw1_ref, fw2_ref, sa_ref, st_ref, *, half, paired
):
    edge = 2 * half
    low = half // 2
    wide = edge * low
    scale = scale_ref[...]
    turn = lax.axis_index("oct") * half if paired else 0

    def same(x):
        return x

    def turned(x):
        return lax.rem(x + turn, edge)

    def chunked(x):
        return (x % low) * 4 + x // low

    by_chunk = exact(one_hot((edge, edge), chunked, same), scale)
    s1e_ref[...] = exact(by_chunk, one_hot((edge, wide), same, lambda x: x // low))
    s2e_ref[...] = exact(by_chunk, one_hot((edge, wide // 2), same, lambda x: x % edge))
    m1_ref[...] = one_hot((low * half, wide), lambda x: x // half, lambda x: x % low)
    m2_ref[...] = one_hot((edge, wide // 2), lambda x: x // low, lambda x: x // edge)
    sa_ref[...] = exact(scale, one_hot((edge, edge), same, turned))
    pick = one_hot((edge, edge), turned, same)
    st_ref[...] = lax.dot_general(
        pick, by_chunk, (((1,), (1,)), ((), ())), preferred_element_type=F32
    ).astype(BF)

    def spread(row_of, lane_of, lane_count):
        rows = lax.dot_general(
            one_hot((wide, edge), row_of, same),
            scale,
            (((1,), (1,)), ((), ())),
            preferred_element_type=F32,
        ).astype(BF)
        return exact(rows, one_hot((edge, lane_count), same, lane_of))

    for bit in range(2):
        fw1_ref[bit] = spread(
            lambda x: x % half + bit * half, lambda x: x // half, 2 * wide
        ) * one_hot((wide, 2 * wide), lambda x: x // half, lambda x: x % half)
    fw2_ref[...] = spread(
        lambda x: x // (wide // 2) * half + x % half, lambda x: x % edge, wide
    ) * one_hot((wide, wide), lambda x: x // half % low, lambda x: x // edge)


def make_weights(two_scale, paired):
    edge = two_scale.shape[0]
    half = edge // 2
    low = half // 2
    wide = edge * low
    shapes = [
        (edge, wide), (edge, wide // 2), (low * half, wide), (edge, wide // 2),
        (2, wide, 2 * wide), (wide, wide), (edge, edge), (edge, edge),
    ]
    return pl.pallas_call(
        functools.partial(weights_kernel, half=half, paired=paired),
        in_specs=[pl.BlockSpec(memory_space=pltpu.VMEM)],
        out_specs=[pl.BlockSpec(memory_space=pltpu.VMEM)] * len(shapes),
        out_shape=[jax.ShapeDtypeStruct(shape, BF) for shape in shapes],
        compiler_params=pltpu.CompilerParams(vmem_limit_bytes=24 * 1024 * 1024),
    )(two_scale)


def pick_kernel(slot_ref, children_ref, near_ref, send_ref):
    blocks, _ = children_ref.shape
    parents, held, rows, lanes = near_ref.shape
    stacked = jnp.concatenate(
        [children_ref[:, lanes * p : lanes * (p + 1)] for p in range(rows)], axis=0
    )
    row = lax.broadcasted_iota(jnp.int32, (rows, rows * blocks), 0)
    place = lax.broadcasted_iota(jnp.int32, (rows, rows * blocks), 1) - row * blocks
    mine = lax.axis_index("oct")
    for out_ref, owner in ((send_ref, 1 - mine), (near_ref, mine)):
        wanted = [
            (place == slot_ref[j, owner * parents + i]).astype(F32).astype(BF)
            for i in range(parents)
            for j in range(held)
        ]
        picked = exact(jnp.concatenate(wanted, axis=0), stacked)
        for i in range(parents):
            for j in range(held):
                first = rows * (held * i + j)
                out_ref[i, j] = picked[first : first + rows]


def pick_blocks(child_slot, children, parents, half):
    shape = jax.ShapeDtypeStruct((parents, child_slot.shape[0], half, half * half), BF)
    return pl.pallas_call(
        pick_kernel,
        in_specs=[
            pl.BlockSpec(memory_space=pltpu.SMEM),
            pl.BlockSpec(memory_space=pltpu.VMEM),
        ],
        out_specs=[pl.BlockSpec(memory_space=pltpu.VMEM)] * 2,
        out_shape=[shape, shape],
        compiler_params=pltpu.CompilerParams(vmem_limit_bytes=60 * 1024 * 1024),
    )(child_slot, children)


def by_output(table, edge, terms):
    low = edge // 4
    lanes = 4 * edge
    chunk = lax.broadcasted_iota(jnp.int32, (low, lanes), 1) // edge
    groups = []
    for start in range(0, terms, 4):
        tiles = [
            table[low * min(t, terms - 1) : low * (min(t, terms - 1) + 1)]
            for t in range(start, start + 4)
        ]
        for step in (1, 2):
            upper = (chunk // step) % 2 == 1
            mixed = list(tiles)
            for i in range(4):
                if i & step == 0:
                    mixed[i] = jnp.where(
                        upper, pltpu.roll(tiles[i + step], edge * step, 1), tiles[i]
                    )
                    mixed[i + step] = jnp.where(
                        upper, tiles[i + step], pltpu.roll(tiles[i], lanes - edge * step, 1)
                    )
            tiles = mixed
        groups.append(jnp.concatenate(tiles, axis=0))
    return jnp.concatenate(groups, axis=1)[:, : terms * edge]


def apply_kernel(
    kind_ref, *refs, half, terms, first_parent,
):
    (
        near_ref, far_ref, table_ref, s1e_ref, s2e_ref, m1_ref, m2_ref, fw1_ref, fw2_ref,
        sa_ref, st_ref, keep_ref, send_ref, cube_ref, sec_ref,
    ) = refs[:15]
    g0_ref, w1e_ref, w2e_ref = refs[15:]
    edge = 2 * half
    low = half // 2
    wide = edge * low
    quarter = wide // 4
    rows = terms * low
    disps = kind_ref.shape[1]
    count = keep_ref.shape[0] // disps

    def expand(entries):
        kinds = [kind_ref[first_parent + k // disps, k % disps] for k in entries]
        spread = [
            [
                by_output(
                    table_ref[kind, rows * axis : rows * (axis + 1), :].astype(F32), edge, terms
                ).astype(BF)
                for kind in kinds
            ]
            for axis in range(3)
        ]
        turned = [[x.T for x in spread[axis]] for axis in (1, 2)]
        for k, x in zip(entries, spread[0]):
            g0_ref[k] = dot(st_ref[...], x).astype(BF)
        for k, x in zip(entries, turned[0]):
            w1e_ref[k] = dot(x, s1e_ref[...]).astype(BF)
        for k, x in zip(entries, turned[1]):
            once = dot(x, s2e_ref[...])
            for i in range(terms * 4):
                tile = once[low * i : low * (i + 1)]
                w2e_ref[k, half * i : half * (i + 1), :] = jnp.concatenate(
                    [tile, tile], axis=0
                ).astype(BF)

    def filtered(parent):
        total = None
        for bit in range(2):
            parts = []
            for mid in range(2):
                parts += [near_ref[parent, 2 * mid + bit], far_ref[parent, 2 * mid + bit]]
            part = dot(jnp.concatenate(parts, axis=0), fw1_ref[bit])
            total = part if total is None else total + part
        total = total.astype(BF)
        lanes = wide // 2
        moved = jnp.concatenate(
            [
                jnp.concatenate(
                    [
                        total[:edge, lanes * i : lanes * (i + 1)],
                        total[edge:, lanes * i : lanes * (i + 1)],
                    ],
                    axis=1,
                )
                for i in range(4)
            ],
            axis=0,
        )
        second = dot(moved, fw2_ref[...]).astype(BF)
        return jnp.concatenate(
            [
                dot(sa_ref[...], second[edge * i : edge * (i + 1)]).astype(BF)
                for i in range(4)
            ],
            axis=0,
        )

    def products(k):
        cube = cube_ref[k // disps]
        none = jnp.zeros((half, wide // 2), BF)
        for t in range(terms):
            one = w1e_ref[k, edge * t : edge * (t + 1), :]
            w1 = jnp.concatenate(
                [
                    one[half * j : half * (j + 1)] * m1_ref[half * i : half * (i + 1), :]
                    for i in range(low)
                    for j in range(2)
                ],
                axis=0,
            )
            first = dot(cube, w1).astype(BF)
            moved = jnp.concatenate(
                [
                    jnp.concatenate(
                        [
                            first[edge * i : edge * (i + 1), quarter * j : quarter * (j + 1)]
                            for i in range(4)
                        ],
                        axis=1,
                    )
                    for j in range(4)
                ],
                axis=0,
            )
            w2 = []
            for i in range(4):
                tile = w2e_ref[k, half * (4 * t + i) : half * (4 * t + i + 1), :]
                pair = [tile * m2_ref[half * q : half * (q + 1), :] for q in range(2)]
                w2 += [jnp.concatenate([x, none], axis=1) for x in pair]
                w2 += [jnp.concatenate([none, x], axis=1) for x in pair]
            second = dot(moved, jnp.concatenate(w2, axis=0)).astype(BF)
            for i in range(4):
                sec_ref[k, i, edge * t : edge * (t + 1), :] = second[edge * i : edge * (i + 1)]

    def finish(k):
        for i in range(4):
            out = dot(g0_ref[k], sec_ref[k, i]).astype(BF)
            keep_ref[k, :, wide * i : wide * (i + 1)] = out[:half]
            send_ref[k, :, wide * i : wide * (i + 1)] = out[half:]

    for i in range(count):
        cube_ref[i] = filtered(first_parent + i)
    expand(range(count * disps))
    for k in range(count * disps):
        products(k)
    for k in range(count * disps):
        finish(k)


def apply_parents(first_parent, count, kinds, near, far, table, weights, half):
    edge = 2 * half
    wide = edge * half // 2
    terms = table.shape[1] // (3 * edge // 4)
    disps = kinds.shape[1]
    shape = jax.ShapeDtypeStruct((count * disps, half, 4 * wide), BF)
    arrays = (near, far, table) + tuple(weights)
    expanded = [
        pltpu.VMEM((count * disps, edge, terms * edge), BF),
        pltpu.VMEM((count * disps, terms * edge, wide), BF),
        pltpu.VMEM((count * disps, terms * 2 * edge, wide // 2), BF),
    ]
    return pl.pallas_call(
        functools.partial(
            apply_kernel,
            half=half,
            terms=terms,
            first_parent=first_parent,
        ),
        in_specs=[pl.BlockSpec(memory_space=pltpu.SMEM)]
        + [pl.BlockSpec(memory_space=pltpu.VMEM)] * len(arrays),
        out_specs=[pl.BlockSpec(memory_space=pltpu.VMEM)] * 2,
        out_shape=[shape, shape],
        scratch_shapes=[
            pltpu.VMEM((count, 4 * edge, wide), BF),
            pltpu.VMEM((count * disps, 4, terms * edge, wide), BF),
        ]
        + expanded,
        compiler_params=pltpu.CompilerParams(vmem_limit_bytes=24 * 1024 * 1024),
    )(kinds, *arrays)


def target(goal_ref, item, nodes):
    goal = goal_ref[item]
    offset = jnp.bitwise_xor(lax.div(goal, nodes), lax.axis_index("leaf"))
    return offset & 1, (offset >> 1) * nodes + lax.rem(goal, nodes)


def sum_kernel(goal_ref, *refs, sources, nodes, start):
    row_refs, (even_ref, odd_ref, total_ref) = refs[:-3], refs[-3:]
    slots, _, lanes = even_ref.shape
    total_ref[...] = jnp.zeros_like(total_ref)
    for row_ref, items in zip(row_refs, sources):
        for i, item in enumerate(items):
            parity, slot = target(goal_ref, item, nodes)
            slot = parity * slots + slot
            part = row_ref[i, :, start : start + lanes].astype(F32)
            total_ref[slot] = (total_ref[slot].astype(F32) + part).astype(BF)
    even_ref[...] = total_ref[:slots]
    odd_ref[...] = total_ref[slots:]


def sum_rows(goals, arrays, sources, nodes, leaf_count, start, lanes):
    rows = arrays[0].shape[1]
    slots = leaf_count // 2 * nodes
    shape = jax.ShapeDtypeStruct((slots, rows, lanes), BF)
    return pl.pallas_call(
        functools.partial(sum_kernel, sources=sources, nodes=nodes, start=start),
        in_specs=[pl.BlockSpec(memory_space=pltpu.SMEM)]
        + [pl.BlockSpec(memory_space=pltpu.VMEM)] * len(arrays),
        out_specs=[pl.BlockSpec(memory_space=pltpu.VMEM)] * 2,
        out_shape=[shape, shape],
        scratch_shapes=[pltpu.VMEM((2 * slots, rows, lanes), BF)],
        compiler_params=pltpu.CompilerParams(vmem_limit_bytes=24 * 1024 * 1024),
    )(goals, *arrays)


def place(offset, bit):
    return (offset >> (bit + 1) << bit) | (offset & ((1 << bit) - 1))


def combine_kernel(kept_ref, arrived_ref, keep_ref, send_ref, *, bit):
    for r in range(kept_ref.shape[0]):
        total = (kept_ref[r].astype(F32) + arrived_ref[r].astype(F32)).astype(BF)
        out_ref = send_ref if r >> bit & 1 else keep_ref
        out_ref[place(r, bit)] = total


def combine(kept, arrived, bit):
    shape = jax.ShapeDtypeStruct((kept.shape[0] // 2,) + kept.shape[1:], BF)
    return pl.pallas_call(
        functools.partial(combine_kernel, bit=bit),
        in_specs=[pl.BlockSpec(memory_space=pltpu.VMEM)] * 2,
        out_specs=[pl.BlockSpec(memory_space=pltpu.VMEM)] * 2,
        out_shape=[shape, shape],
        compiler_params=pltpu.CompilerParams(vmem_limit_bytes=24 * 1024 * 1024),
    )(kept, arrived)


def last_kernel(
    kept0_ref, kept1_ref, arrived0_ref, arrived1_ref, result_ref, out_ref, wide_ref, sem
):
    nodes, octants, size = out_ref.shape
    groups = size // 128
    rows, lanes = kept0_ref.shape[2:]

    def store(total, n, first, step):
        wide_ref[pl.ds(n * octants * groups + first, rows, stride=step), :] = total[
            rows * n : rows * (n + 1)
        ]

    for i, (kept_ref, arrived_ref) in enumerate(
        ((kept0_ref, arrived0_ref), (kept1_ref, arrived1_ref))
    ):
        total = kept_ref[0].astype(F32) + arrived_ref[0].astype(F32)
        total = total.reshape(nodes * rows, lanes)
        if octants == 4:
            wide = lanes // 2
            half = wide // 16
            order = one_hot(
                (wide, wide),
                lambda x: x % (2 * half) // half * (wide // 2) + x // (2 * half) * half + x % half,
                lambda x: x,
            )
            for c in range(2):
                moved = dot(total[:, wide * c : wide * (c + 1)].astype(BF), order)
                for bit in range(2):
                    part = moved[:, wide // 2 * bit : wide // 2 * (bit + 1)]
                    for n in range(nodes):
                        store(part, n, (2 * i + bit) * groups + c, 2)
        else:
            for h in range(lanes // 128):
                part = total[:, 128 * h : 128 * (h + 1)]
                for n in range(nodes):
                    store(part, n, i * (lanes // 128) + h, lanes // 64)
    copies = []
    for n in range(nodes):
        for v in range(groups):
            out_ref[n, :, 128 * v : 128 * (v + 1)] = wide_ref[
                pl.ds(n * octants * groups + v, octants, stride=groups), :
            ].astype(BF)
        copies.append(pltpu.make_async_copy(out_ref.at[n], result_ref.at[n], sem.at[n]))
        copies[-1].start()
    for copy in copies:
        copy.wait()


def last_combine(kept, arrived, shape):
    return pl.pallas_call(
        last_kernel,
        in_specs=[pl.BlockSpec(memory_space=pltpu.VMEM)] * 4,
        out_specs=pl.BlockSpec(memory_space=pl.ANY),
        out_shape=jax.ShapeDtypeStruct(shape, BF),
        scratch_shapes=[
            pltpu.VMEM(shape, BF),
            pltpu.VMEM((math.prod(shape) // 128, 128), F32),
            pltpu.SemaphoreType.DMA(shape[:1]),
        ],
        compiler_params=pltpu.CompilerParams(vmem_limit_bytes=24 * 1024 * 1024),
    )(*kept, *arrived)


def swap(x, axis, mask):
    count = lax.axis_size(axis)
    return lax.ppermute(x, axis, [(i, i ^ mask) for i in range(count)])


def local(children, child_slot, two_scale, factors, disp_kind, target_leaf, target_node):
    oct_count = lax.axis_size("oct")
    leaf_count = lax.axis_size("leaf")
    edge = two_scale.shape[0]
    half = edge // 2
    held = child_slot.shape[1]
    parents, disps = disp_kind.shape
    paired = oct_count == 2

    if paired:
        near, sent = pick_blocks(child_slot.T, children, parents, half)
        far = swap(sent, "oct", 1)
    else:
        blocks = children.reshape(-1, half, half * half)
        arrived = lax.all_to_all(
            blocks[child_slot], "oct", split_axis=0, concat_axis=1, tiled=True
        ).reshape(parents, 2, 4, half, half * half)
        near, far = arrived[:, 0], arrived[:, 1]

    table = factors.reshape(factors.shape[0], -1, 4 * edge)
    weights = make_weights(two_scale, paired)

    arrays, sources = [], []
    done, counts = 0, [max(1, parents - 2)] + [1] * min(2, parents - 1)
    for count in counts:
        kept, sent = apply_parents(
            done, count, disp_kind, near, far, table, weights, half
        )
        if done == 0:
            target_leaf, target_node, kept = lax.optimization_barrier(
                (target_leaf, target_node, kept)
            )
            nodes = 2 * oct_count
            goal = (target_leaf.reshape(parents, disps) * nodes + target_node).reshape(-1)
            if paired:
                goals = jnp.concatenate([goal, swap(goal, "oct", 1)])
            else:
                goals = lax.all_gather(goal, "oct", tiled=True)
        items = [done * disps + i for i in range(count * disps)]
        if paired:
            arrays += [kept, swap(sent, "oct", 1)]
            sources += [items, [goal.size + item for item in items]]
        else:
            rows = jnp.stack([kept, sent], axis=1).reshape(-1, 2, half, 2, half, 2, half)
            rows = rows.transpose(1, 3, 5, 0, 2, 4, 6)
            rows = rows.reshape(oct_count, held, -1, half, half * half)
            rows = rows.transpose(0, 2, 1, 3, 4)
            rows = lax.all_to_all(rows, "oct", split_axis=0, concat_axis=0, tiled=True)
            arrays += [rows.reshape(-1, held * half, half * half)]
            sources += [[goal.size * o + item for o in range(oct_count) for item in items]]
        done += count

    lanes = arrays[0].shape[-1] // 2
    masks = [1 << i for i in range(1, (leaf_count - 1).bit_length())]
    kept, arrived = [], []
    for i, order in enumerate((masks[1::-1] + masks[2:], masks)):
        keep, send = sum_rows(goals, arrays, sources, nodes, leaf_count, lanes * i, lanes)
        shape = (leaf_count // 2, nodes, -1, lanes)
        keep, come = keep.reshape(shape), swap(send, "leaf", 1).reshape(shape)
        left = list(masks)
        for mask in order:
            keep, send = combine(keep, come, left.index(mask))
            left.remove(mask)
            come = swap(send, "leaf", mask)
        kept.append(keep)
        arrived.append(come)
    return last_combine(kept, arrived, (nodes, held, half * half * half))


def solution(mesh):
    placed = (
        P(("leaf", "oct"), None),
        P("leaf", "oct"),
        P(),
        P(),
        P(("leaf", "oct"), None),
        P(("leaf", "oct"), None, None),
        P(("leaf", "oct"), None),
    )
    return jax.shard_map(
        local, mesh=mesh, in_specs=placed, out_specs=P("leaf", "oct", None), check_vma=False
    )
```
